256 devices in a mesh: row: 8 (over x, y_hi), col: 32 (over y_lo, z, core).
Axes of the slice: x: 4, y: 4 (y_hi: 2, y_lo: 2; y = y_hi * 2 + y_lo), z: 8, core: 2. Of those that a mesh axis runs over, the one named last changes fastest.
Arguments:
- pair_left: bfloat16 [1024, 256, 128], P('row', 'col'), may hold values from -6 to 6
- pair_right: bfloat16 [2048, 256, 128], P('col', 'row'), may hold values from -6 to 6
- pair_tile: bfloat16 [1024, 2048, 128], P('row', 'col'), may hold values from -6 to 6
- d_update: bfloat16 [1024, 2048, 128], P('row', 'col'), may hold values from -6 to 6
- mask_rows: int32 [1024], P('row'), may hold values 0 or 1
- mask_cols: int32 [2048], P('col'), may hold values 0 or 1
- mask_mid: int32 [256], replicated, may hold values 0 or 1
- ln_in_gain: float32 [128], replicated, may hold values from 0.1 to 1.9
- left_gate_w: bfloat16 [128, 128], replicated, may hold values from -0.5 to 0.5
- left_proj_w: bfloat16 [128, 128], replicated, may hold values from -0.5 to 0.5
- right_gate_w: bfloat16 [128, 128], replicated, may hold values from -0.5 to 0.5
- right_proj_w: bfloat16 [128, 128], replicated, may hold values from -0.5 to 0.5
- out_gate_w: bfloat16 [128, 128], replicated, may hold values from -0.5 to 0.5
- ln_mid_gain: float32 [128], replicated, may hold values from 0.1 to 1.9
- out_proj_w: bfloat16 [128, 128], replicated, may hold values from -0.5 to 0.5
Outputs:
- update: bfloat16 [1024, 2048, 128], P('row', 'col')
- d_pair_left: bfloat16 [1024, 256, 128], P('row', 'col')
- d_pair_right: bfloat16 [2048, 256, 128], P('col', 'row')
- d_pair_tile: bfloat16 [1024, 2048, 128], P('row', 'col')
The draws below stay inside these ranges and needn't reach their ends.
All inputs are finite; a program needn't handle non-finite values. No bound on the sum of `mask_rows` or of `mask_cols` on one device may be relied on, other than what follows from the above.
Results may differ from the reference program's by a relative error of at most 0.03.
Values may be sent and summed in bfloat16 or wider, within the bound.
A program may use at most 128 MiB of HBM per device.

```python
import jax
import jax.numpy as jnp
from jax import lax

PAIR_CH = 128
HID_CH = 128
ROWS_DEV = 128
COLS_DEV = 64
ROWS = 1024
COLS = 2048
MIDS = 256
N_ROW = 8
N_COL = 32


def touch_ends(values, key, least, largest):
    extent = values.shape
    index_at = [jax.random.randint(jax.random.fold_in(key, axis), (), 0, extent[axis]) for axis in range(len(extent))]
    values = values.at[tuple(index_at)].set(least)
    longest = extent.index(max(extent))
    index_at[longest] = (index_at[longest] + 1) % extent[longest]
    return values.at[tuple(index_at)].set(largest)


def shard_levels(key, extent, split, smallest, largest):
    loudness = 1.0
    for dim, blocks in split:
        steps = jax.random.uniform(jax.random.fold_in(jax.random.fold_in(key, 6), dim), (blocks,), jnp.float32, smallest / len(split), largest / len(split))
        loudness = loudness * jnp.repeat(jnp.exp(steps), extent[dim] // blocks).reshape((-1,) + (1,) * (len(extent) - 1 - dim))
    return loudness


def normal_values(key, shape, spread, most, cuts=(), dtype=jnp.bfloat16):
    level = shard_levels(key, shape, cuts, -0.22, 0.18) if cuts else 1.0
    entries = jax.random.normal(key, shape, jnp.float32) * spread * level
    return jnp.minimum(jnp.maximum(entries, -most), most).astype(dtype)


def setup_inputs(seed: int = 0) -> dict:
    splits = jax.random.split(jax.random.key(seed), 16)
    return {
        "pair_left": normal_values(splits[0], (ROWS, MIDS, PAIR_CH), 1.0, 6.0, ((0, 8), (1, 32))),
        "pair_right": normal_values(splits[1], (COLS, MIDS, PAIR_CH), 1.0, 6.0, ((0, 32), (1, 8))),
        "pair_tile": normal_values(splits[2], (ROWS, COLS, PAIR_CH), 1.0, 6.0, ((0, 8), (1, 32))),
        "d_update": normal_values(splits[3], (ROWS, COLS, PAIR_CH), 1.0, 6.0, ((0, 8), (1, 32))),
        "mask_rows": touch_ends((jax.random.randint(splits[4], (ROWS,), 0, 8) < 7).astype(jnp.int32), jax.random.fold_in(splits[4], 1), 0, 1),
        "mask_cols": touch_ends((jax.random.randint(splits[5], (COLS,), 0, 8) < 7).astype(jnp.int32), jax.random.fold_in(splits[5], 1), 0, 1),
        "mask_mid": touch_ends((jax.random.randint(splits[6], (MIDS,), 0, 8) < 7).astype(jnp.int32), jax.random.fold_in(splits[6], 1), 0, 1),
        "ln_in_gain": jnp.clip(1.0 + 0.18 * jax.random.normal(splits[7], (PAIR_CH,), jnp.float32), 0.1, 1.9),
        "left_gate_w": normal_values(splits[8], (PAIR_CH, HID_CH), PAIR_CH ** -0.5, 0.5),
        "left_proj_w": normal_values(splits[9], (PAIR_CH, HID_CH), PAIR_CH ** -0.5, 0.5),
        "right_gate_w": normal_values(splits[10], (PAIR_CH, HID_CH), PAIR_CH ** -0.5, 0.5),
        "right_proj_w": normal_values(splits[11], (PAIR_CH, HID_CH), PAIR_CH ** -0.5, 0.5),
        "out_gate_w": normal_values(splits[12], (PAIR_CH, PAIR_CH), PAIR_CH ** -0.5, 0.5),
        "ln_mid_gain": jnp.clip(1.0 + 0.18 * jax.random.normal(splits[13], (HID_CH,), jnp.float32), 0.1, 1.9),
        "out_proj_w": normal_values(splits[14], (HID_CH, PAIR_CH), HID_CH ** -0.5, 0.5),
    }


def layer_norm(values, gain):
    mean = lax.optimization_barrier(jnp.mean(values, axis=-1, keepdims=True))
    centred = values - mean
    rstd = lax.rsqrt(lax.optimization_barrier(jnp.mean(centred * centred, axis=-1, keepdims=True)) + 1e-05)
    normed = centred * rstd
    return (normed * gain, normed, rstd)

def norm_back(normed, rstd, gain, upstream):
    scaled = upstream * gain
    inner = lax.optimization_barrier(jnp.mean(scaled * normed, axis=-1, keepdims=True))
    return (scaled - lax.optimization_barrier(jnp.mean(scaled, axis=-1, keepdims=True)) - normed * inner) * rstd

def project_side(pair, mask_two, gain, gate_w, proj_w):
    normed_out, normed, rstd = layer_norm(pair.astype(jnp.float32), gain)
    rounded = normed_out.astype(jnp.bfloat16)
    gate = jax.nn.sigmoid(jnp.dot(rounded, gate_w, preferred_element_type=jnp.float32))
    value = jnp.dot(rounded, proj_w, preferred_element_type=jnp.float32)
    result = (mask_two[..., None] * gate * value).astype(jnp.bfloat16)
    return (result, gate, value, normed, rstd)

def side_back(grad, mask_two, gate, value, normed, rstd, gain, gate_w, proj_w):
    masked = grad * mask_two[..., None]
    d_value = (masked * gate).astype(jnp.bfloat16)
    d_gate = (masked * value * gate * (1.0 - gate)).astype(jnp.bfloat16)
    d_norm = jnp.dot(d_value, proj_w.T, preferred_element_type=jnp.float32)
    d_norm = d_norm + jnp.dot(d_gate, gate_w.T, preferred_element_type=jnp.float32)
    return norm_back(normed, rstd, gain, d_norm).astype(jnp.bfloat16)

def reference(pair_left, pair_right, pair_tile, d_update, mask_rows, mask_cols, mask_mid, ln_in_gain, left_gate_w, left_proj_w, right_gate_w, right_proj_w, out_gate_w, ln_mid_gain, out_proj_w):
    midf = mask_mid.astype(jnp.float32)
    mask_left = mask_rows.astype(jnp.float32)[:, None] * midf[None, :]
    mask_right = mask_cols.astype(jnp.float32)[:, None] * midf[None, :]
    left, left_gate, left_value, left_normed, left_rstd = project_side(pair_left, mask_left, ln_in_gain, left_gate_w, left_proj_w)
    right, right_gate, right_value, right_normed, right_rstd = project_side(pair_right, mask_right, ln_in_gain, right_gate_w, right_proj_w)
    right_wide = right.astype(jnp.float32)
    right_blocks = right_wide.reshape(N_COL, COLS_DEV, MIDS, HID_CH)
    left_blocks = left.reshape(N_ROW, ROWS_DEV, MIDS, HID_CH)
    tile_blocks = pair_tile.reshape(N_ROW, ROWS_DEV, COLS, PAIR_CH)
    grad_blocks = d_update.reshape(N_ROW, ROWS_DEV, COLS, PAIR_CH)

    def row_step(carry, items):
        left_block, tile_block, grad_block = items
        left_wide = left_block.astype(jnp.float32)
        triangle = jnp.einsum('ikc,jkc->ijc', left_wide, right_wide)
        tri_out, tri_normed, tri_rstd = layer_norm(triangle, ln_mid_gain)
        tri_norm = tri_out.astype(jnp.bfloat16)
        tile_out, tile_normed, tile_rstd = layer_norm(tile_block.astype(jnp.float32), ln_in_gain)
        tile_norm = tile_out.astype(jnp.bfloat16)
        out_gate = jax.nn.sigmoid(jnp.dot(tile_norm, out_gate_w, preferred_element_type=jnp.float32))
        out_value = jnp.dot(tri_norm, out_proj_w, preferred_element_type=jnp.float32)
        update_block = (out_gate * out_value).astype(jnp.bfloat16)
        upstream = grad_block.astype(jnp.float32)
        d_value = (upstream * out_gate).astype(jnp.bfloat16)
        d_gate = (upstream * out_value * out_gate * (1.0 - out_gate)).astype(jnp.bfloat16)
        d_tri_norm = jnp.dot(d_value, out_proj_w.T, preferred_element_type=jnp.float32)
        d_tile_norm = jnp.dot(d_gate, out_gate_w.T, preferred_element_type=jnp.float32)
        d_triangle = norm_back(tri_normed, tri_rstd, ln_mid_gain, d_tri_norm).astype(jnp.bfloat16)
        d_tile = norm_back(tile_normed, tile_rstd, ln_in_gain, d_tile_norm).astype(jnp.bfloat16)
        d_tri_wide = d_triangle.astype(jnp.float32)
        d_tri_cols = jnp.transpose(d_tri_wide.reshape(ROWS_DEV, N_COL, COLS_DEV, HID_CH), (1, 0, 2, 3))

        def col_step(total, pieces):
            piece_grad, piece_right = pieces
            term = jnp.einsum('ijc,jkc->ikc', piece_grad, piece_right)
            return (total + term.astype(jnp.bfloat16).astype(jnp.float32), None)
        start = jnp.zeros((ROWS_DEV, MIDS, HID_CH), jnp.float32)
        d_left_block, unused = lax.scan(col_step, start, (d_tri_cols, right_blocks))
        right_term = jnp.einsum('ijc,ikc->jkc', d_tri_wide, left_wide)
        carry = carry + right_term.astype(jnp.bfloat16).astype(jnp.float32)
        return (carry, (update_block, d_tile, d_left_block))
    start_right = jnp.zeros((COLS, MIDS, HID_CH), jnp.float32)
    d_right, outputs = lax.scan(row_step, start_right, (left_blocks, tile_blocks, grad_blocks))
    update = outputs[0].reshape(ROWS, COLS, PAIR_CH)
    d_pair_tile = outputs[1].reshape(ROWS, COLS, PAIR_CH)
    d_left = outputs[2].reshape(ROWS, MIDS, HID_CH)
    d_pair_left = side_back(d_left, mask_left, left_gate, left_value, left_normed, left_rstd, ln_in_gain, left_gate_w, left_proj_w)
    d_pair_right = side_back(d_right, mask_right, right_gate, right_value, right_normed, right_rstd, ln_in_gain, right_gate_w, right_proj_w)
    return (update, d_pair_left, d_pair_right, d_pair_tile)
```

```python
import functools

import jax
import jax.numpy as jnp
from jax import lax
from jax.experimental import pallas as pl
from jax.experimental.pallas import tpu as pltpu
from jax.sharding import PartitionSpec as P

MESH = pl.DeviceIdType.MESH
BF = jnp.bfloat16
F32 = jnp.float32
VMEM = pl.BlockSpec(memory_space=pltpu.VMEM)
SMEM = pl.BlockSpec(memory_space=pltpu.SMEM)
ANY = pl.BlockSpec(memory_space=pl.ANY)
LIMIT = 60 * 1024 * 1024


def nn(a, b):
    return lax.dot_general(a, b, (((1,), (0,)), ((), ())), preferred_element_type=F32)


def nt(a, b):
    return lax.dot_general(a, b, (((1,), (1,)), ((), ())), preferred_element_type=F32)


def tn(a, b):
    return lax.dot_general(a, b, (((0,), (0,)), ((), ())), preferred_element_type=F32)


def sigmoid(v):
    return 0.5 * jnp.tanh(0.5 * v) + 0.5


def norm(values, axis):
    centred = values - jnp.mean(values, axis=axis, keepdims=True)
    rstd = lax.rsqrt(jnp.mean(centred * centred, axis=axis, keepdims=True) + 1e-05)
    return centred * rstd, rstd


def norm_back(normed, rstd, gain, upstream, axis):
    scaled = upstream * gain
    inner = jnp.mean(scaled * normed, axis=axis, keepdims=True)
    return (scaled - jnp.mean(scaled, axis=axis, keepdims=True) - normed * inner) * rstd


def left_mask(mid_ref, rows_ref, k):
    keep = mid_ref[lax.axis_index("col") * 8 + k].astype(F32)
    return rows_ref[...].astype(F32) * keep


def right_mask(mid_ref, cols_ref, k):
    base = lax.axis_index("row") * 32 + k
    low = mid_ref[base].astype(F32)
    high = mid_ref[base + 16].astype(F32)
    lane = lax.broadcasted_iota(jnp.int32, (1, 128), 1)
    return cols_ref[...].astype(F32) * jnp.where(lane < 64, low, high)


def side_kernel(
    left_ref, right_ref, rows_ref, cols_ref, mid_ref, gain_ref, lg, lp, rg, rp,
    left_out, right_out, flat, wide,
):
    gain = gain_ref[...]

    def project(ref, count, weights):
        @pl.loop(0, count // 256)
        def _(t):
            rows = pl.ds(pl.multiple_of(t * 256, 256), 256)
            normed, _ = norm(ref[rows, :].astype(F32), -1)
            both = nn((normed * gain).astype(BF), weights)
            flat[rows, :] = sigmoid(both[:, :128]) * both[:, 128:]

    project(left_ref, 1024, jnp.concatenate([lg[...], lp[...]], axis=1))

    @pl.loop(0, 8)
    def _(k):
        turned = flat[pl.ds(k, 128, stride=8), :].T
        left_out[pl.ds(k, 128, stride=8), :] = turned * left_mask(mid_ref, rows_ref, k)

    project(right_ref, 2048, jnp.concatenate([rg[...], rp[...]], axis=1))

    @pl.loop(0, 16)
    def _(k):
        low = flat[pl.ds(k, 64, stride=32), :]
        high = flat[pl.ds(k + 16, 64, stride=32), :]
        turned = jnp.concatenate([low, high], axis=0).T
        wide[pl.ds(k, 128, stride=16), :] = turned * right_mask(mid_ref, cols_ref, k)

    @pl.loop(0, 8)
    def _(t):
        rows = pl.ds(pl.multiple_of(t * 256, 256), 256)
        right_out[rows, :] = wide[rows, :].astype(BF)


def side_back_kernel(
    left_ref, right_ref, dl_ref, dr_ref, rows_ref, cols_ref, mid_ref, gain_ref,
    lg, lp, rg, rp, left_out, right_out, flat,
):
    gain = gain_ref[...]

    def back(ref, count, gate_w, proj_w, out):
        weights = jnp.concatenate([gate_w[...], proj_w[...]], axis=1)

        @pl.loop(0, count // 256)
        def _(t):
            rows = pl.ds(pl.multiple_of(t * 256, 256), 256)
            normed, rstd = norm(ref[rows, :].astype(F32), -1)
            both = nn((normed * gain).astype(BF), weights)
            gate = sigmoid(both[:, :128])
            value = both[:, 128:]
            masked = flat[rows, :]
            d_value = (masked * gate).astype(BF)
            d_gate = (masked * value * gate * (1.0 - gate)).astype(BF)
            d_norm = nt(jnp.concatenate([d_gate, d_value], axis=1), weights)
            out[rows, :] = norm_back(normed, rstd, gain, d_norm, -1).astype(BF)

    @pl.loop(0, 8)
    def _(k):
        rows = dl_ref[pl.ds(k, 128, stride=8), :] * left_mask(mid_ref, rows_ref, k)
        flat[pl.ds(k, 128, stride=8), :] = rows.T

    back(left_ref, 1024, lg, lp, left_out)

    @pl.loop(0, 16)
    def _(k):
        rows = dr_ref[pl.ds(k, 128, stride=16), :] * right_mask(mid_ref, cols_ref, k)
        turned = rows.T
        flat[pl.ds(k, 64, stride=32), :] = turned[:64, :]
        flat[pl.ds(k + 16, 64, stride=32), :] = turned[64:, :]

    back(right_ref, 2048, rg, rp, right_out)


class Place:
    def __init__(self):
        row, col = lax.axis_index("row"), lax.axis_index("col")
        self.row, self.col = row, col
        self.x, self.yh = row // 2, lax.rem(row, 2)
        self.yl, self.z = col // 16, lax.rem(col // 2, 8)
        self.e = lax.rem(col, 2)

    def at(self, x=None, y=None, z=None, e=None):
        here = self.yh * 2 + self.yl
        y = here if y is None else lax.rem(here + y + 4, 4)
        x = self.x if x is None else lax.rem(self.x + x + 4, 4)
        z = self.z if z is None else lax.rem(self.z + z + 8, 8)
        e = self.e if e is None else 1 - self.e
        return (x * 2 + y // 2, lax.rem(y, 2) * 16 + z * 2 + e)

    def mate(self):
        return (self.row, (1 - self.yl) * 16 + self.z * 2 + self.e)

    def slot(self, same_y, dz):
        z = lax.rem(self.z + dz + 8, 8)
        yl = self.yl if same_y else 1 - self.yl
        return lax.rem(z, 2), yl * 4 + z // 2

    def across(self, same_y, dx):
        x = lax.rem(self.x + dx + 4, 4)
        yh = self.yh if same_y else 1 - self.yh
        return x * 2 + yh


def greet(place):
    barrier = pltpu.get_barrier_semaphore()
    partners = [
        place.at(e=1), place.at(z=1), place.at(z=-1), place.at(x=1), place.at(x=-1),
        place.at(y=1), place.at(y=-1),
    ]
    for partner in partners:
        pl.semaphore_signal(barrier, inc=1, device_id=partner, device_id_type=MESH)
    pl.semaphore_wait(barrier, len(partners))


class Wire:
    def __init__(self, send, recv):
        self.send, self.recv = send, recv
        self.number, self.open = {}, []

    def copy(self, name, src, dst, to):
        index = self.number.setdefault(name, len(self.number))
        return pltpu.make_async_remote_copy(
            src_ref=src, dst_ref=dst, send_sem=self.send.at[index],
            recv_sem=self.recv.at[index], device_id=to, device_id_type=MESH,
        )

    def start(self, name, src, dst, to):
        made = self.copy(name, src, dst, to)
        made.start()
        self.open.append(made)

    def arrived(self, name, dst, to):
        self.copy(name, dst, dst, to).wait_recv()

    def finish(self):
        for made in self.open:
            made.wait_send()


def gather_kernel(
    left_ref, right_ref, lp, rp, given, own, relay, send, recv, local
):
    me = Place()
    wire = Wire(send, recv)
    half = pl.ds(pl.multiple_of(me.e * 64, 64), 64)
    other = pl.ds(pl.multiple_of((1 - me.e) * 64, 64), 64)
    core, up, down = me.at(e=1), me.at(z=1), me.at(z=-1)
    east, west, north, south = me.at(x=1), me.at(x=-1), me.at(y=1), me.at(y=-1)
    low, high = pl.ds(0, 64), pl.ds(64, 64)
    greet(me)

    wire.start("core", left_ref.at[other], given, core)
    mine = rp.at[me.row]
    wire.start("ya", right_ref.at[low], relay.at[0], north)
    wire.start("yb", right_ref.at[high], relay.at[1], south)
    wire.start("x+a1", right_ref.at[low], mine.at[low], east)
    wire.start("x-b1", right_ref.at[high], mine.at[high], west)
    wire.start("x+b1", right_ref.at[high], mine.at[high], east)
    wire.start("x-a1", right_ref.at[low], mine.at[low], west)
    keep_right = pltpu.make_async_copy(right_ref, mine, local.at[0])
    keep_right.start()

    wire.arrived("core", given, core)

    @pl.loop(0, 8)
    def _(t):
        part = pl.ds(pl.multiple_of(t * 8, 8), 8)
        ours = left_ref[pl.ds(pl.multiple_of(me.e * 64 + t * 8, 8), 8)]
        theirs = given[part]
        first = jnp.where(me.e == 0, ours, theirs)
        second = jnp.where(me.e == 0, theirs, ours)
        own[part] = jnp.concatenate([first, second], axis=1).astype(BF)

    def piece(same_y, dz, part=half):
        kh, slot = me.slot(same_y, dz)
        return lp.at[kh, slot, part]

    def share(name, same_y, dz, src=None):
        ref = piece(same_y, dz)
        wire.start("c" + name, ref if src is None else src, ref, core)

    keep_left = pltpu.make_async_copy(own, piece(True, 0), local.at[1])
    wire.start("mate", own, piece(True, 0), me.mate())
    wire.start("z+O1", own, piece(True, 0), up)
    wire.start("z-O1", own, piece(True, 0), down)
    keep_left.start()
    share("O0", True, 0, own)

    def through_y():
        above, below = lax.rem(me.yh * 2 + me.yl + 3, 4), lax.rem(me.yh * 2 + me.yl + 1, 4)
        wire.arrived("ya", relay.at[0], north)
        wire.start("ya2", relay.at[0], rp.at[me.x * 2 + above // 2, low], north)
        wire.arrived("yb", relay.at[1], south)
        wire.start("yb2", relay.at[1], rp.at[me.x * 2 + below // 2, high], south)

    def left_step(src, d):
        same = src == "O"
        tag = src + str(d)
        later = src + str(d + 1)
        behind, ahead = piece(same, -d), piece(same, d)
        wire.arrived("z+" + tag, behind, up)
        wire.arrived("z-" + tag, ahead, down)
        if d < 3:
            wire.start("z+" + later, behind, behind, up)
            wire.start("z-" + later, ahead, ahead, down)
        else:
            front = pl.ds(pl.multiple_of(me.e * 64, 32), 32)
            rear = pl.ds(pl.multiple_of(me.e * 64 + 32, 32), 32)
            one, two = piece(same, -3, front), piece(same, 3, rear)
            wire.start("z+" + later, one, one, up)
            wire.start("z-" + later, two, two, down)
        share("+" + tag, same, -d)
        share("-" + tag, same, d)

    def left_last(src):
        same = src == "O"
        front = pl.ds(pl.multiple_of(me.e * 64, 32), 32)
        rear = pl.ds(pl.multiple_of(me.e * 64 + 32, 32), 32)
        wire.arrived("z+" + src + "4", piece(same, 4, front), up)
        wire.arrived("z-" + src + "4", piece(same, 4, rear), down)
        share("+" + src + "4", same, 4)

    def right_step(same, tag):
        west_ref, east_ref = rp.at[me.across(same, -1)], rp.at[me.across(same, 1)]
        wire.arrived("x+a" + tag + "1", west_ref.at[low], east)
        wire.start("x+a" + tag + "2", west_ref.at[low], west_ref.at[low], east)
        wire.arrived("x-b" + tag + "1", east_ref.at[high], west)
        wire.start("x-b" + tag + "2", east_ref.at[high], east_ref.at[high], west)

    def right_rest(same, tag):
        west_ref, east_ref = rp.at[me.across(same, -1)], rp.at[me.across(same, 1)]
        far = rp.at[me.across(same, 2)]
        wire.arrived("x+b" + tag + "1", west_ref.at[high], east)
        wire.arrived("x-a" + tag + "1", east_ref.at[low], west)
        wire.arrived("x+a" + tag + "2", far.at[low], east)
        wire.arrived("x-b" + tag + "2", far.at[high], west)

    wire.arrived("mate", piece(False, 0), me.mate())
    wire.start("z+Y1", piece(False, 0), piece(False, 0), up)
    wire.start("z-Y1", piece(False, 0), piece(False, 0), down)
    share("Y0", False, 0)
    wire.arrived("x+a1", rp.at[me.across(True, -1), low], east)
    wire.start("x+a2", rp.at[me.across(True, -1), low], rp.at[me.across(True, -1), low], east)
    wire.arrived("x-b1", rp.at[me.across(True, 1), high], west)
    wire.start("x-b2", rp.at[me.across(True, 1), high], rp.at[me.across(True, 1), high], west)
    through_y()
    left_step("O", 1)
    left_step("Y", 1)
    pair = rp.at[me.across(False, 0)]
    wire.arrived("ya2", pair.at[low], north)
    wire.start("x+ap1", pair.at[low], pair.at[low], east)
    wire.arrived("yb2", pair.at[high], south)
    wire.start("x-bp1", pair.at[high], pair.at[high], west)
    wire.start("x+bp1", pair.at[high], pair.at[high], east)
    wire.start("x-ap1", pair.at[low], pair.at[low], west)
    left_step("O", 2)
    left_step("Y", 2)
    right_step(False, "p")
    left_step("O", 3)
    left_step("Y", 3)
    right_rest(True, "")
    left_last("O")
    left_last("Y")
    right_rest(False, "p")
    for src in ("O", "Y"):
        same = src == "O"
        wire.arrived("c" + src + "0", piece(same, 0, other), core)
        for d in (1, 2, 3):
            wire.arrived("c+" + src + str(d), piece(same, -d, other), core)
            wire.arrived("c-" + src + str(d), piece(same, d, other), core)
        wire.arrived("c+" + src + "4", piece(same, 4, other), core)
    keep_right.wait()
    keep_left.wait()
    wire.finish()


def gather(left, right):
    return pl.pallas_call(
        gather_kernel,
        out_shape=(
            jax.ShapeDtypeStruct((2, 8, 128, 16, 128), BF),
            jax.ShapeDtypeStruct((8, 128, 16, 128), BF),
        ),
        in_specs=[VMEM, VMEM],
        out_specs=(ANY, ANY),
        scratch_shapes=[
            pltpu.VMEM((64, 8, 128), F32),
            pltpu.VMEM((64, 16, 128), BF),
            pltpu.VMEM((2, 64, 16, 128), BF),
            pltpu.SemaphoreType.DMA((56,)),
            pltpu.SemaphoreType.DMA((56,)),
            pltpu.SemaphoreType.DMA((2,)),
        ],
        compiler_params=pltpu.CompilerParams(
            collective_id=0, has_side_effects=True, vmem_limit_bytes=LIMIT
        ),
        name="gather_panels",
    )(left, right)


def scatter_kernel(
    dl, dr, left_out, right_out,
    ls, core_in, z_in, mate_in, give, got, rs, x_in, relay, pair_in,
    send, recv, local,
):
    me = Place()
    wire = Wire(send, recv)
    half = pl.ds(pl.multiple_of(me.e * 64, 64), 64)
    other = pl.ds(pl.multiple_of((1 - me.e) * 64, 64), 64)
    core, up, down = me.at(e=1), me.at(z=1), me.at(z=-1)
    east, west, north, south = me.at(x=1), me.at(x=-1), me.at(y=1), me.at(y=-1)
    low, high = pl.ds(0, 64), pl.ds(64, 64)
    greet(me)

    loads = {}
    for count, dz in enumerate((4, 3, 5, 2, 6, 1, 7, 0)):
        for which in (0, 1):
            kh, slot = me.slot(which == 1, dz)
            wire.start(
                f"c{which}{dz}", dl.at[kh, slot, other], core_in.at[which, dz], core
            )
            load = pltpu.make_async_copy(
                dl.at[kh, slot, half], ls.at[which, dz], local.at[which * 8 + dz]
            )
            load.start()
            loads[which, dz] = load
        if count < 4:
            dx = (2, 1, 3, 0)[count]
            for which in (0, 1):
                load = pltpu.make_async_copy(
                    dr.at[me.across(which == 1, dx)], rs.at[which, dx],
                    local.at[16 + which * 4 + dx],
                )
                load.start()
                loads["r", which, dx] = load

    def add(target, terms, count, start=0, out=None):
        @pl.loop(start // 8, (start + count) // 8)
        def _(t):
            part = pl.ds(pl.multiple_of(t * 8, 8), 8)
            total = target[part].astype(F32)
            for term in terms:
                total = total + term[part].astype(F32)
            if out is None:
                target[part] = total.astype(BF)
            else:
                out(part, total)

    def combine(which, dz):
        loads[which, dz].wait()
        wire.arrived(f"c{which}{dz}", core_in.at[which, dz], core)

    def left_first(which):
        combine(which, 4)
        block = ls.at[which, 4]
        add(block, [core_in.at[which, 4]], 64)
        front, rear = pl.ds(0, 32), pl.ds(32, 32)
        wire.start(f"z+{which}0", block.at[front], z_in.at[0, which, 0, front], up)
        wire.start(f"z-{which}0", block.at[rear], z_in.at[1, which, 0, rear], down)

    def left_step(which, d):
        for way, sign, to, dz in ((0, "+", up, 4 - d), (1, "-", down, 4 + d)):
            combine(which, dz)
            block, given = ls.at[which, dz], core_in.at[which, dz]
            came = z_in.at[way, which, d - 1]
            if d == 1:
                part = pl.ds(way * 32, 32)
                wire.arrived(f"z{sign}{which}0", came.at[part], to)
                add(block, [given, came], 32, way * 32)
                add(block, [given], 32, 32 - way * 32)
            else:
                wire.arrived(f"z{sign}{which}{d - 1}", came, to)
                add(block, [given, came], 64)
            wire.start(f"z{sign}{which}{d}", block, z_in.at[way, which, d], to)

    def left_last(which):
        combine(which, 0)
        wire.arrived(f"z+{which}3", z_in.at[0, which, 3], up)
        wire.arrived(f"z-{which}3", z_in.at[1, which, 3], down)
        return [core_in.at[which, 0], z_in.at[0, which, 3], z_in.at[1, which, 3]]

    def right_first(which):
        loads["r", which, 2].wait()
        block = rs.at[which, 2]
        wire.start(f"x+{which}0", block.at[low], x_in.at[0, which, 0, low], east)
        wire.start(f"x-{which}0", block.at[high], x_in.at[1, which, 0, high], west)

    def right_step(which):
        for way, sign, to, dx, part in (
            (0, "+", east, 1, low), (1, "-", west, 3, high),
        ):
            loads["r", which, dx].wait()
            came, block = x_in.at[way, which, 0], rs.at[which, dx]
            wire.arrived(f"x{sign}{which}0", came.at[part], to)
            add(block, [came], 64, way * 64)
            wire.start(f"x{sign}{which}1", block, x_in.at[way, which, 1], to)

    def right_last(which):
        loads["r", which, 0].wait()
        wire.arrived(f"x+{which}1", x_in.at[0, which, 1], east)
        wire.arrived(f"x-{which}1", x_in.at[1, which, 1], west)
        return [x_in.at[0, which, 1], x_in.at[1, which, 1]]

    left_first(0)
    right_first(0)
    left_first(1)
    right_first(1)
    left_step(0, 1)
    left_step(1, 1)
    right_step(0)
    right_step(1)
    left_step(0, 2)
    left_step(1, 2)
    left_step(0, 3)
    add(rs.at[0, 0], right_last(0), 128)
    wire.start("ya", rs.at[0, 0, low], relay.at[0], north)
    wire.start("yb", rs.at[0, 0, high], relay.at[1], south)
    left_step(1, 3)
    wire.arrived("ya", relay.at[0], north)
    wire.start("ya2", relay.at[0], pair_in.at[low], north)
    wire.arrived("yb", relay.at[1], south)
    wire.start("yb2", relay.at[1], pair_in.at[high], south)
    add(ls.at[0, 0], left_last(0), 64)
    wire.start("mate", ls.at[0, 0], mate_in, me.mate())
    terms = right_last(1)
    wire.arrived("ya2", pair_in.at[low], north)
    wire.arrived("yb2", pair_in.at[high], south)

    def put_right(part, total):
        right_out[part] = total

    add(rs.at[1, 0], terms + [pair_in], 128, out=put_right)
    terms = left_last(1)
    wire.arrived("mate", mate_in, me.mate())

    def put_left(part, total):
        first, second = total[:, :8], total[:, 8:]
        left_out[pl.ds(pl.multiple_of(me.e * 64 + part.start, 8), 8)] = jnp.where(
            me.e == 0, first, second
        )
        give[part] = jnp.where(me.e == 0, second, first)

    add(ls.at[1, 0], terms + [mate_in], 64, out=put_left)
    wire.start("last", give, got, core)
    wire.arrived("last", got, core)

    @pl.loop(0, 8)
    def _(t):
        part = pl.ds(pl.multiple_of(t * 8, 8), 8)
        left_out[pl.ds(pl.multiple_of((1 - me.e) * 64 + t * 8, 8), 8)] = got[part]

    wire.finish()


def scatter(dl, dr):
    return pl.pallas_call(
        scatter_kernel,
        out_shape=(
            jax.ShapeDtypeStruct((128, 8, 128), F32),
            jax.ShapeDtypeStruct((128, 16, 128), F32),
        ),
        in_specs=[ANY, ANY],
        out_specs=(VMEM, VMEM),
        scratch_shapes=[
            pltpu.VMEM((2, 8, 64, 16, 128), BF),
            pltpu.VMEM((2, 8, 64, 16, 128), BF),
            pltpu.VMEM((2, 2, 4, 64, 16, 128), BF),
            pltpu.VMEM((64, 16, 128), BF),
            pltpu.VMEM((64, 8, 128), F32),
            pltpu.VMEM((64, 8, 128), F32),
            pltpu.VMEM((2, 4, 128, 16, 128), BF),
            pltpu.VMEM((2, 2, 2, 128, 16, 128), BF),
            pltpu.VMEM((2, 64, 16, 128), BF),
            pltpu.VMEM((128, 16, 128), BF),
            pltpu.SemaphoreType.DMA((56,)),
            pltpu.SemaphoreType.DMA((56,)),
            pltpu.SemaphoreType.DMA((24,)),
        ],
        compiler_params=pltpu.CompilerParams(
            collective_id=1, has_side_effects=True, vmem_limit_bytes=LIMIT
        ),
        name="scatter_sums",
    )(dl, dr)


CS = 16
NC = 128 // CS
JS = 8
NJ = 64 // JS


def middle_kernel(
    lp, rp, tile_ref, up_ref, in_gain_ref, gate_w_ref, mid_gain_ref, proj_w_ref,
    update_ref, d_tile_ref, dl_ref, dr_ref, tri, flat,
):
    step = pl.program_id(0)

    @pl.when(step < NC)
    def _():
        for c in range(CS):
            right = rp[:, c].reshape(128, 128)
            turned = right.T
            sides = jnp.concatenate([turned[:64], turned[64:]], axis=1)
            left = jnp.concatenate(
                [lp[0, :, c].reshape(128, 128), lp[1, :, c].reshape(128, 128)], axis=0
            )
            result = nn(sides, left)
            rows = pl.ds(pl.multiple_of((step * CS + c) * 8, 8), 8)
            for block in range(NJ):
                tri[block, rows, :] = result[block * 8:(block + 1) * 8]

    @pl.when((step >= NC) & (step < NC + NJ))
    def _():
        block = tri.at[step - NC]
        mid_gain = mid_gain_ref[...]
        in_gain = in_gain_ref[...]
        proj_w = proj_w_ref[...]
        gate_w = gate_w_ref[...]

        for j in range(JS):
            normed, _ = norm(block[pl.ds(j, 128, stride=8), :], 0)
            value = tn((normed * mid_gain).astype(BF), proj_w)
            flat[pl.ds(j, 128, stride=8), :] = value

        for t in range(8):
            rows = pl.ds(t * 128, 128)
            items = pl.ds(t * 16, 16)
            tile = tile_ref[items].astype(F32).reshape(128, 128)
            upstream = up_ref[items].astype(F32).reshape(128, 128)
            normed, rstd = norm(tile, -1)
            gate = sigmoid(nn((normed * in_gain).astype(BF), gate_w))
            value = flat[rows, :]
            update_ref[items] = (gate * value).reshape(16, 8, 128).astype(BF)
            gated = upstream * gate
            flat[rows, :] = gated
            d_gate = (gated * value * (1.0 - gate)).astype(BF)
            d_norm = nt(d_gate, gate_w)
            d_tile = norm_back(normed, rstd, in_gain, d_norm, -1)
            d_tile_ref[items] = d_tile.reshape(16, 8, 128).astype(BF)

        for j in range(JS):
            here = pl.ds(j, 128, stride=8)
            normed, rstd = norm(block[here, :], 0)
            d_norm = nt(proj_w, flat[here, :].astype(BF))
            block[here, :] = norm_back(normed, rstd, mid_gain, d_norm, 0)

    @pl.when(step >= NC + NJ)
    def _():
        for c in range(CS):
            rows = pl.ds(pl.multiple_of(((step - NC - NJ) * CS + c) * 8, 8), 8)
            grad = jnp.concatenate(
                [tri[block, rows, :] for block in range(NJ)], axis=0
            ).astype(BF)
            none = jnp.zeros((64, 128), BF)
            grad = jnp.concatenate(
                [
                    jnp.concatenate([grad, none], axis=1),
                    jnp.concatenate([none, grad], axis=1),
                ],
                axis=0,
            )
            right = rp[:, c].reshape(128, 128)
            left = jnp.concatenate(
                [lp[0, :, c].reshape(128, 128), lp[1, :, c].reshape(128, 128)], axis=1
            )
            d_left = nn(right, grad).astype(BF)
            dl_ref[0, :, c] = d_left[:, :128].reshape(8, 16, 128)
            dl_ref[1, :, c] = d_left[:, 128:].reshape(8, 16, 128)
            dr_ref[:, c] = nt(left, grad).astype(BF).reshape(8, 16, 128)


def middle(lp, rp, tile, upstream, in_gain, gate_w, mid_gain, proj_w):
    def channel(s):
        return jnp.where(s < NC + NJ, jnp.minimum(s, NC - 1), s - NC - NJ)

    def column(s):
        return jnp.clip(s - NC, 0, NJ - 1)

    def later(s):
        return jnp.maximum(s - NC - NJ, 0)

    left = lambda at: pl.BlockSpec((2, 8, CS, 16, 128), lambda s: (0, 0, at(s), 0, 0))
    right = lambda at: pl.BlockSpec((8, CS, 16, 128), lambda s: (0, at(s), 0, 0))
    cell = pl.BlockSpec((128, JS, 128), lambda s: (0, column(s), 0))
    whole = pl.BlockSpec((128, 128), lambda s: (0, 0))
    line = pl.BlockSpec((1, 128), lambda s: (0, 0))
    return pl.pallas_call(
        middle_kernel,
        grid=(NC + NJ + NC,),
        out_shape=(
            jax.ShapeDtypeStruct((128, 64, 128), BF),
            jax.ShapeDtypeStruct((128, 64, 128), BF),
            jax.ShapeDtypeStruct((2, 8, 128, 16, 128), BF),
            jax.ShapeDtypeStruct((8, 128, 16, 128), BF),
        ),
        in_specs=[left(channel), right(channel), cell, cell, line, whole, whole, whole],
        out_specs=(cell, cell, left(later), right(later)),
        scratch_shapes=[
            pltpu.VMEM((NJ, 1024, 128), F32),
            pltpu.VMEM((1024, 128), F32),
        ],
        compiler_params=pltpu.CompilerParams(
            vmem_limit_bytes=LIMIT, dimension_semantics=("arbitrary",)
        ),
        name="middle",
    )(lp, rp, tile, upstream, in_gain, gate_w, mid_gain, proj_w)


def body(
    pair_left,
    pair_right,
    pair_tile,
    d_update,
    mask_rows,
    mask_cols,
    mask_mid,
    ln_in_gain,
    left_gate_w,
    left_proj_w,
    right_gate_w,
    right_proj_w,
    out_gate_w,
    ln_mid_gain,
    out_proj_w,
):
    flat_left = pair_left.reshape(1024, 128)
    flat_right = pair_right.reshape(2048, 128)
    rows = mask_rows.reshape(1, 128)
    cols = jnp.concatenate([mask_cols, mask_cols]).reshape(1, 128)
    gain = ln_in_gain.reshape(1, 128)
    weights = (left_gate_w, left_proj_w, right_gate_w, right_proj_w)
    left, right = pl.pallas_call(
        side_kernel,
        out_shape=(
            jax.ShapeDtypeStruct((1024, 128), F32),
            jax.ShapeDtypeStruct((2048, 128), BF),
        ),
        in_specs=[VMEM] * 4 + [SMEM] + [VMEM] * 5,
        out_specs=(VMEM, VMEM),
        scratch_shapes=[pltpu.VMEM((2048, 128), F32), pltpu.VMEM((2048, 128), F32)],
        compiler_params=pltpu.CompilerParams(vmem_limit_bytes=LIMIT),
        name="sides",
    )(flat_left, flat_right, rows, cols, mask_mid, gain, *weights)
    lp, rp = gather(left.reshape(128, 8, 128), right.reshape(128, 16, 128))
    mid_gain = jnp.broadcast_to(ln_mid_gain[:, None], (128, 128))
    update, d_tile, dl, dr = middle(
        lp, rp, pair_tile, d_update, gain, out_gate_w, mid_gain, out_proj_w
    )
    dl, dr = scatter(dl, dr)
    d_left, d_right = pl.pallas_call(
        side_back_kernel,
        out_shape=(
            jax.ShapeDtypeStruct((1024, 128), BF),
            jax.ShapeDtypeStruct((2048, 128), BF),
        ),
        in_specs=[VMEM] * 6 + [SMEM] + [VMEM] * 5,
        out_specs=(VMEM, VMEM),
        scratch_shapes=[pltpu.VMEM((2048, 128), F32)],
        compiler_params=pltpu.CompilerParams(vmem_limit_bytes=LIMIT),
        name="sides_back",
    )(
        flat_left, flat_right, dl.reshape(1024, 128), dr.reshape(2048, 128),
        rows, cols, mask_mid, gain, *weights,
    )
    return (
        update,
        d_left.reshape(128, 8, 128),
        d_right.reshape(64, 32, 128),
        d_tile,
    )


def solution(mesh):
    in_specs = (
        P("row", "col", None),
        P("col", "row", None),
        P("row", "col", None),
        P("row", "col", None),
        P("row"),
        P("col"),
        P(),
        P(),
        P(),
        P(),
        P(),
        P(),
        P(),
        P(),
        P(),
    )
    out_specs = (
        P("row", "col", None),
        P("row", "col", None),
        P("col", "row", None),
        P("row", "col", None),
    )
    return jax.shard_map(body, mesh=mesh, in_specs=in_specs, out_specs=out_specs, check_vma=False)
```

```python
import functools

import jax
import jax.numpy as jnp
from jax import lax
from jax.experimental import pallas as pl
from jax.experimental.pallas import tpu as pltpu
from jax.sharding import PartitionSpec as P

MESH = pl.DeviceIdType.MESH
BF = jnp.bfloat16
F32 = jnp.float32
VMEM = pl.BlockSpec(memory_space=pltpu.VMEM)
SMEM = pl.BlockSpec(memory_space=pltpu.SMEM)
ANY = pl.BlockSpec(memory_space=pl.ANY)
LIMIT = 60 * 1024 * 1024


def nn(a, b):
    return lax.dot_general(a, b, (((1,), (0,)), ((), ())), preferred_element_type=F32)


def nt(a, b):
    return lax.dot_general(a, b, (((1,), (1,)), ((), ())), preferred_element_type=F32)


def tn(a, b):
    return lax.dot_general(a, b, (((0,), (0,)), ((), ())), preferred_element_type=F32)


def sigmoid(v):
    return 0.5 * jnp.tanh(0.5 * v) + 0.5


def norm(values, axis):
    centred = values - jnp.mean(values, axis=axis, keepdims=True)
    rstd = lax.rsqrt(jnp.mean(centred * centred, axis=axis, keepdims=True) + 1e-05)
    return centred * rstd, rstd


def norm_back(normed, rstd, gain, upstream, axis):
    scaled = upstream * gain
    inner = jnp.mean(scaled * normed, axis=axis, keepdims=True)
    return (scaled - jnp.mean(scaled, axis=axis, keepdims=True) - normed * inner) * rstd


def left_mask(mid_ref, rows_ref, k):
    keep = mid_ref[lax.axis_index("col") * 8 + k].astype(F32)
    return rows_ref[...].astype(F32) * keep


def right_mask(mid_ref, cols_ref, k):
    base = lax.axis_index("row") * 32 + k
    low = mid_ref[base].astype(F32)
    high = mid_ref[base + 16].astype(F32)
    cols = cols_ref[...].astype(F32)
    return jnp.concatenate([cols * low, cols * high], axis=1)


def project(ref, t, gain, weights):
    rows = pl.ds(t * 256, 256)
    normed, rstd = norm(ref[rows, :].astype(F32), -1)
    both = nn((normed * gain).astype(BF), weights)
    return rows, normed, rstd, sigmoid(both[:, :128]), both[:, 128:]


class Fill:
    def __init__(self):
        self.todo = []

    def __call__(self, count=1):
        for work in self.todo[:count]:
            work()
        self.todo = self.todo[count:]


class Place:
    def __init__(self):
        row, col = lax.axis_index("row"), lax.axis_index("col")
        self.row, self.col = row, col
        self.x, self.yh = row // 2, lax.rem(row, 2)
        self.yl, self.z = col // 16, lax.rem(col // 2, 8)
        self.e = lax.rem(col, 2)

    def at(self, x=None, y=None, z=None, e=None):
        here = self.yh * 2 + self.yl
        y = here if y is None else lax.rem(here + y + 4, 4)
        x = self.x if x is None else lax.rem(self.x + x + 4, 4)
        z = self.z if z is None else lax.rem(self.z + z + 8, 8)
        e = self.e if e is None else 1 - self.e
        return (x * 2 + y // 2, lax.rem(y, 2) * 16 + z * 2 + e)

    def mate(self):
        return (self.row, (1 - self.yl) * 16 + self.z * 2 + self.e)

    def slot(self, same_y, dz):
        z = lax.rem(self.z + dz + 8, 8)
        yl = self.yl if same_y else 1 - self.yl
        return lax.rem(z, 2), yl * 4 + z // 2

    def across(self, same_y, dx):
        x = lax.rem(self.x + dx + 4, 4)
        yh = self.yh if same_y else 1 - self.yh
        return x * 2 + yh


def greet(place):
    barrier = pltpu.get_barrier_semaphore()
    partners = [
        place.at(e=1), place.at(z=1), place.at(z=-1), place.at(x=1), place.at(x=-1),
        place.at(y=1), place.at(y=-1),
    ]
    for partner in partners:
        pl.semaphore_signal(barrier, inc=1, device_id=partner, device_id_type=MESH)
    return lambda: pl.semaphore_wait(barrier, len(partners))


class Wire:
    def __init__(self, send, recv):
        self.send, self.recv = send, recv
        self.number, self.open = {}, []

    def copy(self, name, src, dst, to):
        index = self.number.setdefault(name, len(self.number))
        return pltpu.make_async_remote_copy(
            src_ref=src, dst_ref=dst, send_sem=self.send.at[index],
            recv_sem=self.recv.at[index], device_id=to, device_id_type=MESH,
        )

    def start(self, name, src, dst, to):
        made = self.copy(name, src, dst, to)
        made.start()
        self.open.append(made)

    def arrived(self, name, dst, to):
        self.copy(name, dst, dst, to).wait_recv()

    def finish(self):
        for made in self.open:
            made.wait_send()


PARTS = {"O0": (0, 32), "O1": (32, 32), "Y0": (0, 24), "Y1": (24, 24)}
LATE = (48, 16)


def gather_kernel(
    left_ref, right_ref, rows_ref, cols_ref, mid_ref, gain_ref, lg, lpw, rg, rpw,
    lp, rp, flat, turned_left, wide, right_bf, given, own, relay, send, recv, local,
):
    me = Place()
    wire = Wire(send, recv)
    met = greet(me)
    core, up, down, mate = me.at(e=1), me.at(z=1), me.at(z=-1), me.mate()
    east, west, north, south = me.at(x=1), me.at(x=-1), me.at(y=1), me.at(y=-1)
    low, high = pl.ds(0, 64), pl.ds(64, 64)
    base = me.e * 64
    gain = gain_ref[...]

    def channels(start, count):
        return pl.ds(pl.multiple_of(base + start, 8), count)

    def piece(same_y, dz, part=(0, 64)):
        kh, slot = me.slot(same_y, dz)
        return lp.at[kh, slot, channels(*part)]

    left_w = jnp.concatenate([lg[...], lpw[...]], axis=1)
    for t in range(4):
        rows, _, _, gate, value = project(left_ref, t, gain, left_w)
        flat[rows, :] = gate * value

    @pl.loop(0, 8, unroll=4)
    def _(k):
        part = flat[pl.ds(k, 128, stride=8), :].T
        turned_left[pl.ds(k, 128, stride=8), :] = part * left_mask(mid_ref, rows_ref, k)

    met()
    there = pl.ds(pl.multiple_of((1 - me.e) * 512, 512), 512)
    wire.start("core", turned_left.at[there], given, core)
    wire.arrived("core", given, core)

    @pl.loop(0, 8, unroll=2)
    def _(t):
        rows = pl.ds(pl.multiple_of(me.e * 512 + t * 64, 64), 64)
        ours = turned_left[rows, :].reshape(8, 8, 128)
        theirs = given[pl.ds(pl.multiple_of(t * 64, 64), 64), :].reshape(8, 8, 128)
        first = jnp.where(me.e == 0, ours, theirs)
        second = jnp.where(me.e == 0, theirs, ours)
        both = jnp.concatenate([first, second], axis=1)
        own[pl.ds(pl.multiple_of(t * 8, 8), 8)] = both.astype(BF)

    def from_own(name, part, to):
        wire.start(name, own.at[pl.ds(*part)], piece(True, 0, part), to)

    MATE = (("m0", (0, 24)), ("m1", (24, 24)), ("m2", LATE))
    for name in ("O0", "O1"):
        from_own("z+" + name + "1", PARTS[name], up)
        from_own("z-" + name + "1", PARTS[name], down)
        if name == "O0":
            for tag, part in MATE:
                from_own(tag, part, mate)
    keep_left = pltpu.make_async_copy(own, piece(True, 0), local.at[1])
    keep_left.start()
    from_own("cO0", (0, 64), core)

    right_w = jnp.concatenate([rg[...], rpw[...]], axis=1)

    def right_rows(t):
        rows, _, _, gate, value = project(right_ref, t, gain, right_w)
        flat[rows, :] = gate * value

    def right_turn():
        @pl.loop(0, 16, unroll=4)
        def _(k):
            first = flat[pl.ds(k, 64, stride=32), :]
            second = flat[pl.ds(k + 16, 64, stride=32), :]
            part = jnp.concatenate([first, second], axis=0).T
            wide[pl.ds(k, 128, stride=16), :] = part * right_mask(mid_ref, cols_ref, k)

        @pl.loop(0, 16, unroll=4)
        def _(t):
            rows = pl.ds(pl.multiple_of(t * 128, 128), 128)
            part = wide[rows, :].reshape(8, 16, 128).astype(BF)
            right_bf[pl.ds(pl.multiple_of(t * 8, 8), 8)] = part

    def share(name, same_y, dz):
        wire.start("c" + name, piece(same_y, dz), piece(same_y, dz), core)

    def mate_part(index):
        tag, part = MATE[index]
        wire.arrived(tag, piece(False, 0, part), mate)
        if index < 2:
            name = "Y" + str(index)
            ref = piece(False, 0, part)
            wire.start("z+" + name + "1", ref, ref, up)
            wire.start("z-" + name + "1", ref, ref, down)
        else:
            share("Y0", False, 0)

    def left_step(name, d):
        same = name[0] == "O"
        part = PARTS[name]
        for sign, dz, to, last in (("z+", -d, up, "0"), ("z-", d, down, "1")):
            if d == 4 and name[1] != last:
                continue
            ref = piece(same, dz, part)
            wire.arrived(sign + name + str(d), ref, to)
            if d < 3 or (d == 3 and name[1] == last):
                wire.start(sign + name + str(d + 1), ref, ref, to)
        if name == "O1":
            for dz in (-d, d)[d // 4:]:
                ref = piece(True, dz, LATE)
                wire.start("y" + str(dz), ref, ref, mate)
                share("O" + str(dz), True, dz)

    def late(d):
        for dz in (-d, d)[d // 4:]:
            wire.arrived("y" + str(dz), piece(False, dz, LATE), mate)
            share("Y" + str(dz), False, dz)

    def right_send(src, tag):
        to = rp.at[me.across(tag == "", 0)]
        for name, part, way in (
            ("x+a", low, east), ("x-b", high, west), ("x+b", high, east), ("x-a", low, west),
        ):
            wire.start(name + tag + "1", src.at[part], to.at[part], way)

    def right_step(tag):
        behind, ahead = rp.at[me.across(tag == "", -1)], rp.at[me.across(tag == "", 1)]
        wire.arrived("x+a" + tag + "1", behind.at[low], east)
        wire.start("x+a" + tag + "2", behind.at[low], behind.at[low], east)
        wire.arrived("x-b" + tag + "1", ahead.at[high], west)
        wire.start("x-b" + tag + "2", ahead.at[high], ahead.at[high], west)

    def right_rest(tag):
        behind, ahead = rp.at[me.across(tag == "", -1)], rp.at[me.across(tag == "", 1)]
        far = rp.at[me.across(tag == "", 2)]
        wire.arrived("x+b" + tag + "1", behind.at[high], east)
        wire.arrived("x-a" + tag + "1", ahead.at[low], west)
        wire.arrived("x+a" + tag + "2", far.at[low], east)
        wire.arrived("x-b" + tag + "2", far.at[high], west)

    for t in range(3):
        right_rows(t)
    mate_part(0)
    left_step("O0", 1)
    mate_part(1)
    for t in range(3, 6):
        right_rows(t)
    left_step("O1", 1)
    mate_part(2)
    for t in range(6, 8):
        right_rows(t)
    right_turn()
    keep_right = pltpu.make_async_copy(right_bf, rp.at[me.row], local.at[0])
    right_send(right_bf, "")
    wire.start("ya", right_bf.at[low], relay.at[0], north)
    wire.start("yb", right_bf.at[high], relay.at[1], south)
    keep_right.start()
    left_step("Y0", 1)
    left_step("O0", 2)
    left_step("Y1", 1)
    left_step("O1", 2)
    late(1)
    left_step("Y0", 2)
    above, below = lax.rem(me.yh * 2 + me.yl + 3, 4), lax.rem(me.yh * 2 + me.yl + 1, 4)
    wire.arrived("ya", relay.at[0], north)
    wire.start("ya2", relay.at[0], rp.at[me.x * 2 + above // 2, low], north)
    wire.arrived("yb", relay.at[1], south)
    wire.start("yb2", relay.at[1], rp.at[me.x * 2 + below // 2, high], south)
    left_step("Y1", 2)
    right_step("")
    left_step("O0", 3)
    left_step("O1", 3)
    late(2)
    pair = rp.at[me.across(False, 0)]
    wire.arrived("ya2", pair.at[low], north)
    wire.arrived("yb2", pair.at[high], south)
    right_send(pair, "p")
    left_step("Y0", 3)
    left_step("Y1", 3)
    left_step("O0", 4)
    left_step("O1", 4)
    late(3)
    right_step("p")
    right_rest("")
    left_step("Y0", 4)
    left_step("Y1", 4)
    late(4)
    right_rest("p")
    base = (1 - me.e) * 64
    for src in ("O", "Y"):
        for dz in (0, -1, 1, -2, 2, -3, 3, 4):
            wire.arrived("c" + src + str(dz), piece(src == "O", dz), core)
    keep_right.wait()
    keep_left.wait()
    wire.finish()


def gather(*operands):
    return pl.pallas_call(
        gather_kernel,
        out_shape=(
            jax.ShapeDtypeStruct((2, 8, 128, 16, 128), BF),
            jax.ShapeDtypeStruct((8, 128, 16, 128), BF),
        ),
        in_specs=[VMEM] * 4 + [SMEM] + [VMEM] * 5,
        out_specs=(ANY, ANY),
        scratch_shapes=[
            pltpu.VMEM((2048, 128), F32),
            pltpu.VMEM((1024, 128), F32),
            pltpu.VMEM((2048, 128), F32),
            pltpu.VMEM((128, 16, 128), BF),
            pltpu.VMEM((512, 128), F32),
            pltpu.VMEM((64, 16, 128), BF),
            pltpu.VMEM((2, 64, 16, 128), BF),
            pltpu.SemaphoreType.DMA((80,)),
            pltpu.SemaphoreType.DMA((80,)),
            pltpu.SemaphoreType.DMA((2,)),
        ],
        compiler_params=pltpu.CompilerParams(
            collective_id=0, has_side_effects=True, vmem_limit_bytes=LIMIT
        ),
        name="gather_panels",
    )(*operands)


def scatter_kernel(
    dl, dr, left_ref, right_ref, rows_ref, cols_ref, mid_ref, gain_ref, lg, lpw, rg, rpw,
    left_out, right_out,
    ls, core_in, z_in, late_in, mate_in, give, got, rs, x_in, relay, pair_in,
    flat_left, flat_right, back, norms, rstds, gates, values,
    send, recv, local,
):
    me = Place()
    wire = Wire(send, recv)
    met = greet(me)
    core, up, down, mate = me.at(e=1), me.at(z=1), me.at(z=-1), me.mate()
    east, west, north, south = me.at(x=1), me.at(x=-1), me.at(y=1), me.at(y=-1)
    low, high = pl.ds(0, 64), pl.ds(64, 64)
    half = pl.ds(pl.multiple_of(me.e * 64, 64), 64)
    other = pl.ds(pl.multiple_of((1 - me.e) * 64, 64), 64)
    gain = gain_ref[...]

    loads = {}

    def load(key, src, dst):
        made = pltpu.make_async_copy(src, dst, local.at[len(loads)])
        made.start()
        loads[key] = made

    for which in (0, 1):
        load(("r", which, 2), dr.at[me.across(which == 1, 2)], rs.at[which, 2])
    for dz in (4, 3, 5, 2, 6, 1, 7, 0):
        for which in (0, 1):
            kh, slot = me.slot(which == 1, dz)
            load((which, dz), dl.at[kh, slot, half], ls.at[which, dz])
    met()
    for count, dz in enumerate((4, 3, 5, 2, 6, 1, 7, 0)):
        for which in (0, 1):
            kh, slot = me.slot(which == 1, dz)
            wire.start(f"c{which}{dz}", dl.at[kh, slot, other], core_in.at[which, dz], core)
        if count < 3:
            dx = (1, 3, 0)[count]
            for which in (0, 1):
                load(("r", which, dx), dr.at[me.across(which == 1, dx)], rs.at[which, dx])

    fill = Fill()
    left_w = jnp.concatenate([lg[...], lpw[...]], axis=1)
    right_w = jnp.concatenate([rg[...], rpw[...]], axis=1)

    def ahead(ref, t, weights, shift):
        def work():
            _, normed, rstd, gate, value = project(ref, t, gain, weights)
            rows = pl.ds(shift + t * 256, 256)
            norms[rows, :] = normed
            rstds[rows, :] = jnp.broadcast_to(rstd, (256, 128))
            gates[rows, :] = gate
            values[rows, :] = value * gate * (1.0 - gate)

        return work

    for t in range(8):
        fill.todo.append(ahead(right_ref, t, right_w, 1024))
    for t in range(4):
        fill.todo.append(ahead(left_ref, t, left_w, 0))

    def side_back(count, weights, shift, out):
        for t in range(count):
            here, rows = pl.ds(t * 256, 256), pl.ds(shift + t * 256, 256)
            masked = back[here, :]
            d_value = (masked * gates[rows, :]).astype(BF)
            d_gate = (masked * values[rows, :]).astype(BF)
            d_norm = nt(jnp.concatenate([d_gate, d_value], axis=1), weights)
            result = norm_back(norms[rows, :], rstds[rows, :], gain, d_norm, -1)
            out[here, :] = result.astype(BF)

    def add(target, start, count, terms, out=None):
        @pl.loop(0, count // 8, unroll=2)
        def _(t):
            part = pl.ds(pl.multiple_of(start + t * 8, 8), 8)
            total = target[part].astype(F32)
            for term, shift in terms:
                place = pl.ds(pl.multiple_of(start - shift + t * 8, 8), 8)
                total = total + term[place].astype(F32)
            if out is None:
                target[part] = total.astype(BF)
            else:
                out(start // 8 + t, total)

    def ready(which, dz):
        loads[which, dz].wait()
        wire.arrived(f"c{which}{dz}", core_in.at[which, dz], core)
        if which == 0:
            start, count = LATE
            add(ls.at[0, dz], start, count, [(core_in.at[0, dz], 0)])
            wire.start(f"l{dz}", ls.at[0, dz, pl.ds(*LATE)], late_in.at[dz], mate)
        else:
            wire.arrived(f"l{dz}", late_in.at[dz], mate)

    def send_part(name, way, dz, d, more):
        which = 1 if name[0] == "O" else 0
        start, count = PARTS[name]
        block = ls.at[which, dz]
        terms = [(core_in.at[which, dz], 0)] + more
        if name == "O1":
            add(block, start, 16, terms)
            add(block, LATE[0], LATE[1], terms + [(late_in.at[dz], LATE[0])])
        else:
            add(block, start, count, terms)
        part = pl.ds(start, count)
        sign, to = (("+", up), ("-", down))[way]
        wire.start(f"z{sign}{name}{d}", block.at[part], z_in.at[way, which, d, part], to)

    def came(name, way, d):
        which = 1 if name[0] == "O" else 0
        sign, to = (("+", up), ("-", down))[way]
        ref = z_in.at[way, which, d]
        wire.arrived(f"z{sign}{name}{d}", ref.at[pl.ds(*PARTS[name])], to)
        return [(ref, 0)]

    def left_step(which, d):
        names = ("O0", "O1") if which else ("Y0", "Y1")
        if d == 0:
            ready(which, 4)
            for way in (0, 1):
                send_part(names[way], way, 4, 0, [])
            return
        ready(which, 4 - d)
        ready(which, 4 + d)
        for name in names:
            for way in (0, 1):
                dz = 4 + d if way else 4 - d
                more = came(name, way, d - 1) if d > 1 or name[1] == str(way) else []
                send_part(name, way, dz, d, more)

    def right_first(which):
        loads["r", which, 2].wait()
        block = rs.at[which, 2]
        wire.start(f"x+{which}0", block.at[low], x_in.at[0, which, 0, low], east)
        wire.start(f"x-{which}0", block.at[high], x_in.at[1, which, 0, high], west)

    def right_step(which):
        for way, sign, to, dx, part in (
            (0, "+", east, 1, low), (1, "-", west, 3, high),
        ):
            loads["r", which, dx].wait()
            ref, block = x_in.at[way, which, 0], rs.at[which, dx]
            wire.arrived(f"x{sign}{which}0", ref.at[part], to)
            add(block, way * 64, 64, [(ref, 0)])
            wire.start(f"x{sign}{which}1", block, x_in.at[way, which, 1], to)

    def right_last(which):
        loads["r", which, 0].wait()
        wire.arrived(f"x+{which}1", x_in.at[0, which, 1], east)
        wire.arrived(f"x-{which}1", x_in.at[1, which, 1], west)
        return [(x_in.at[0, which, 1], 0), (x_in.at[1, which, 1], 0)]

    right_first(0)
    right_first(1)
    left_step(0, 0)
    left_step(1, 0)
    right_step(0)
    fill(1)
    left_step(0, 1)
    left_step(1, 1)
    fill(2)
    right_step(1)
    fill(2)
    left_step(0, 2)
    fill(2)
    left_step(1, 2)
    fill(2)
    add(rs.at[0, 0], 0, 128, right_last(0))
    wire.start("ya", rs.at[0, 0, low], relay.at[0], north)
    wire.start("yb", rs.at[0, 0, high], relay.at[1], south)
    left_step(0, 3)
    fill(2)
    left_step(1, 3)
    wire.arrived("ya", relay.at[0], north)
    wire.start("ya2", relay.at[0], pair_in.at[low], north)
    wire.arrived("yb", relay.at[1], south)
    wire.start("yb2", relay.at[1], pair_in.at[high], south)
    fill(4)
    ready(0, 0)
    ready(1, 0)
    terms = [(core_in.at[0, 0], 0)]
    for name in ("Y0", "Y1"):
        start, count = PARTS[name]
        more = came(name, 0, 3) + came(name, 1, 3)
        add(ls.at[0, 0], start, count, terms + more)
    wire.start("mate", ls.at[0, 0, pl.ds(0, 48)], mate_in, mate)

    def put_left(t, total):
        first, second = total[:, :8].reshape(64, 128), total[:, 8:].reshape(64, 128)
        rows = pl.ds(pl.multiple_of(me.e * 512 + t * 64, 64), 64)
        flat_left[rows, :] = jnp.where(me.e == 0, first, second)
        give[pl.ds(pl.multiple_of(t * 64, 64), 64), :] = jnp.where(me.e == 0, second, first)

    terms = [(core_in.at[1, 0], 0), (mate_in, 0)]
    wire_terms = came("O0", 0, 3) + came("O0", 1, 3)
    came("O1", 0, 3)
    came("O1", 1, 3)
    wire.arrived("mate", mate_in, mate)
    add(ls.at[1, 0], 0, 48, terms + wire_terms, put_left)
    terms = [(core_in.at[1, 0], 0), (late_in.at[0], LATE[0])]
    add(ls.at[1, 0], LATE[0], LATE[1], terms + wire_terms, put_left)
    wire.start("last", give, got, core)

    terms = right_last(1)
    wire.arrived("ya2", pair_in.at[low], north)
    wire.arrived("yb2", pair_in.at[high], south)

    def put_right(t, total):
        rows = pl.ds(pl.multiple_of(t * 128, 128), 128)
        flat_right[rows, :] = total.reshape(128, 128)

    add(rs.at[1, 0], 0, 128, terms + [(pair_in, 0)], put_right)

    @pl.loop(0, 16, unroll=4)
    def _(k):
        rows = flat_right[pl.ds(k, 128, stride=16), :] * right_mask(mid_ref, cols_ref, k)
        turned = rows.T
        back[pl.ds(k, 64, stride=32), :] = turned[:64, :]
        back[pl.ds(k + 16, 64, stride=32), :] = turned[64:, :]

    side_back(8, right_w, 1024, right_out)

    wire.arrived("last", got, core)
    flat_left[pl.ds(pl.multiple_of((1 - me.e) * 512, 512), 512), :] = got[...]

    @pl.loop(0, 8, unroll=4)
    def _(k):
        rows = flat_left[pl.ds(k, 128, stride=8), :] * left_mask(mid_ref, rows_ref, k)
        back[pl.ds(k, 128, stride=8), :] = rows.T

    side_back(4, left_w, 0, left_out)
    wire.finish()


def scatter(*operands):
    return pl.pallas_call(
        scatter_kernel,
        out_shape=(
            jax.ShapeDtypeStruct((1024, 128), BF),
            jax.ShapeDtypeStruct((2048, 128), BF),
        ),
        in_specs=[ANY, ANY] + [VMEM] * 4 + [SMEM] + [VMEM] * 5,
        out_specs=(VMEM, VMEM),
        scratch_shapes=[
            pltpu.VMEM((2, 8, 64, 16, 128), BF),
            pltpu.VMEM((2, 8, 64, 16, 128), BF),
            pltpu.VMEM((2, 2, 4, 64, 16, 128), BF),
            pltpu.VMEM((8, 16, 16, 128), BF),
            pltpu.VMEM((48, 16, 128), BF),
            pltpu.VMEM((512, 128), F32),
            pltpu.VMEM((512, 128), F32),
            pltpu.VMEM((2, 4, 128, 16, 128), BF),
            pltpu.VMEM((2, 2, 2, 128, 16, 128), BF),
            pltpu.VMEM((2, 64, 16, 128), BF),
            pltpu.VMEM((128, 16, 128), BF),
            pltpu.VMEM((1024, 128), F32),
            pltpu.VMEM((2048, 128), F32),
            pltpu.VMEM((2048, 128), F32),
            pltpu.VMEM((3072, 128), F32),
            pltpu.VMEM((3072, 128), F32),
            pltpu.VMEM((3072, 128), F32),
            pltpu.VMEM((3072, 128), F32),
            pltpu.SemaphoreType.DMA((80,)),
            pltpu.SemaphoreType.DMA((80,)),
            pltpu.SemaphoreType.DMA((24,)),
        ],
        compiler_params=pltpu.CompilerParams(
            collective_id=1, has_side_effects=True, vmem_limit_bytes=LIMIT
        ),
        name="scatter_sums",
    )(*operands)


CS = 16
NC = 128 // CS
JS = 8
NJ = 64 // JS


def middle_kernel(
    lp, rp, tile_ref, up_ref, in_gain_ref, gate_w_ref, mid_gain_ref, proj_w_ref,
    update_ref, d_tile_ref, dl_ref, dr_ref, tri, flat,
):
    step = pl.program_id(0)

    @pl.when(step < NC)
    def _():
        for c in range(CS):
            right = rp[:, c].reshape(128, 128)
            turned = right.T
            sides = jnp.concatenate([turned[:64], turned[64:]], axis=1)
            left = jnp.concatenate(
                [lp[0, :, c].reshape(128, 128), lp[1, :, c].reshape(128, 128)], axis=0
            )
            result = nn(sides, left)
            rows = pl.ds(pl.multiple_of((step * CS + c) * 8, 8), 8)
            for block in range(NJ):
                tri[block, rows, :] = result[block * 8:(block + 1) * 8]

    @pl.when((step >= NC) & (step < NC + NJ))
    def _():
        block = tri.at[step - NC]
        mid_gain = jnp.broadcast_to(mid_gain_ref[...], (128, 128)).T
        in_gain = in_gain_ref[...]
        proj_w = proj_w_ref[...]
        gate_w = gate_w_ref[...]

        for j in range(JS):
            normed, _ = norm(block[pl.ds(j, 128, stride=8), :], 0)
            value = tn((normed * mid_gain).astype(BF), proj_w)
            flat[pl.ds(j, 128, stride=8), :] = value

        for t in range(8):
            rows = pl.ds(t * 128, 128)
            items = pl.ds(t * 16, 16)
            tile = tile_ref[items].astype(F32).reshape(128, 128)
            upstream = up_ref[items].astype(F32).reshape(128, 128)
            normed, rstd = norm(tile, -1)
            gate = sigmoid(nn((normed * in_gain).astype(BF), gate_w))
            value = flat[rows, :]
            update_ref[items] = (gate * value).reshape(16, 8, 128).astype(BF)
            gated = upstream * gate
            flat[rows, :] = gated
            d_gate = (gated * value * (1.0 - gate)).astype(BF)
            d_norm = nt(d_gate, gate_w)
            d_tile = norm_back(normed, rstd, in_gain, d_norm, -1)
            d_tile_ref[items] = d_tile.reshape(16, 8, 128).astype(BF)

        for j in range(JS):
            here = pl.ds(j, 128, stride=8)
            normed, rstd = norm(block[here, :], 0)
            d_norm = nt(proj_w, flat[here, :].astype(BF))
            block[here, :] = norm_back(normed, rstd, mid_gain, d_norm, 0)

    @pl.when(step >= NC + NJ)
    def _():
        for c in range(CS):
            rows = pl.ds(pl.multiple_of(((step - NC - NJ) * CS + c) * 8, 8), 8)
            grad = jnp.concatenate(
                [tri[block, rows, :] for block in range(NJ)], axis=0
            ).astype(BF)
            none = jnp.zeros((64, 128), BF)
            grad = jnp.concatenate(
                [
                    jnp.concatenate([grad, none], axis=1),
                    jnp.concatenate([none, grad], axis=1),
                ],
                axis=0,
            )
            right = rp[:, c].reshape(128, 128)
            left = jnp.concatenate(
                [lp[0, :, c].reshape(128, 128), lp[1, :, c].reshape(128, 128)], axis=1
            )
            d_left = nn(right, grad).astype(BF)
            dl_ref[0, :, c] = d_left[:, :128].reshape(8, 16, 128)
            dl_ref[1, :, c] = d_left[:, 128:].reshape(8, 16, 128)
            dr_ref[:, c] = nt(left, grad).astype(BF).reshape(8, 16, 128)


def middle(lp, rp, tile, upstream, in_gain, gate_w, mid_gain, proj_w):
    def channel(s):
        return jnp.where(s < NC + NJ, jnp.minimum(s, NC - 1), s - NC - NJ)

    def column(s):
        return jnp.clip(s - NC, 0, NJ - 1)

    def later(s):
        return jnp.maximum(s - NC - NJ, 0)

    left = lambda at: pl.BlockSpec((2, 8, CS, 16, 128), lambda s: (0, 0, at(s), 0, 0))
    right = lambda at: pl.BlockSpec((8, CS, 16, 128), lambda s: (0, at(s), 0, 0))
    cell = pl.BlockSpec((128, JS, 128), lambda s: (0, column(s), 0))
    whole = pl.BlockSpec((128, 128), lambda s: (0, 0))
    line = pl.BlockSpec((1, 128), lambda s: (0, 0))
    return pl.pallas_call(
        middle_kernel,
        grid=(NC + NJ + NC,),
        out_shape=(
            jax.ShapeDtypeStruct((128, 64, 128), BF),
            jax.ShapeDtypeStruct((128, 64, 128), BF),
            jax.ShapeDtypeStruct((2, 8, 128, 16, 128), BF),
            jax.ShapeDtypeStruct((8, 128, 16, 128), BF),
        ),
        in_specs=[left(channel), right(channel), cell, cell, line, whole, line, whole],
        out_specs=(cell, cell, left(later), right(later)),
        scratch_shapes=[
            pltpu.VMEM((NJ, 1024, 128), F32),
            pltpu.VMEM((1024, 128), F32),
        ],
        compiler_params=pltpu.CompilerParams(
            vmem_limit_bytes=LIMIT, dimension_semantics=("arbitrary",)
        ),
        name="middle",
    )(lp, rp, tile, upstream, in_gain, gate_w, mid_gain, proj_w)


def body(
    pair_left,
    pair_right,
    pair_tile,
    d_update,
    mask_rows,
    mask_cols,
    mask_mid,
    ln_in_gain,
    left_gate_w,
    left_proj_w,
    right_gate_w,
    right_proj_w,
    out_gate_w,
    ln_mid_gain,
    out_proj_w,
):
    flat_left = pair_left.reshape(1024, 128)
    flat_right = pair_right.reshape(2048, 128)
    gain = ln_in_gain.reshape(1, 128)
    sides = (
        flat_left, flat_right, mask_rows.reshape(1, 128), mask_cols.reshape(1, 64),
        mask_mid, gain, left_gate_w, left_proj_w, right_gate_w, right_proj_w,
    )
    lp, rp = gather(*sides)
    update, d_tile, dl, dr = middle(
        lp, rp, pair_tile, d_update, gain, out_gate_w, ln_mid_gain.reshape(1, 128),
        out_proj_w,
    )
    d_left, d_right = scatter(dl, dr, *sides)
    return (
        update,
        d_left.reshape(128, 8, 128),
        d_right.reshape(64, 32, 128),
        d_tile,
    )


def solution(mesh):
    in_specs = (
        P("row", "col", None),
        P("col", "row", None),
        P("row", "col", None),
        P("row", "col", None),
        P("row"),
        P("col"),
        P(),
        P(),
        P(),
        P(),
        P(),
        P(),
        P(),
        P(),
        P(),
    )
    out_specs = (
        P("row", "col", None),
        P("row", "col", None),
        P("col", "row", None),
        P("row", "col", None),
    )
    return jax.shard_map(body, mesh=mesh, in_specs=in_specs, out_specs=out_specs, check_vma=False)
```

```python
import functools

import jax
import jax.numpy as jnp
from jax import lax
from jax.experimental import pallas as pl
from jax.experimental.pallas import tpu as pltpu
from jax.sharding import PartitionSpec as P

MESH = pl.DeviceIdType.MESH
BF = jnp.bfloat16
F32 = jnp.float32
VMEM = pl.BlockSpec(memory_space=pltpu.VMEM)
SMEM = pl.BlockSpec(memory_space=pltpu.SMEM)
ANY = pl.BlockSpec(memory_space=pl.ANY)
LIMIT = 60 * 1024 * 1024


def nn(a, b):
    return lax.dot_general(a, b, (((1,), (0,)), ((), ())), preferred_element_type=F32)


def nt(a, b):
    return lax.dot_general(a, b, (((1,), (1,)), ((), ())), preferred_element_type=F32)


def tn(a, b):
    return lax.dot_general(a, b, (((0,), (0,)), ((), ())), preferred_element_type=F32)


def sigmoid(v):
    return 0.5 * jnp.tanh(0.5 * v) + 0.5


def norm(values, axis):
    centred = values - jnp.mean(values, axis=axis, keepdims=True)
    rstd = lax.rsqrt(jnp.mean(centred * centred, axis=axis, keepdims=True) + 1e-05)
    return centred * rstd, rstd


def norm_back(normed, rstd, gain, upstream, axis):
    scaled = upstream * gain
    inner = jnp.mean(scaled * normed, axis=axis, keepdims=True)
    return (scaled - jnp.mean(scaled, axis=axis, keepdims=True) - normed * inner) * rstd


def left_mask(mid_ref, rows_ref, k):
    keep = mid_ref[lax.axis_index("col") * 8 + k].astype(F32)
    return rows_ref[...].astype(F32) * keep


def right_mask(mid_ref, cols_ref, k):
    base = lax.axis_index("row") * 32 + k
    low = mid_ref[base].astype(F32)
    high = mid_ref[base + 16].astype(F32)
    cols = cols_ref[...].astype(F32)
    return jnp.concatenate([cols * low, cols * high], axis=1)


def project(ref, t, gain, weights):
    rows = pl.ds(t * 256, 256)
    normed, rstd = norm(ref[rows, :].astype(F32), -1)
    both = nn((normed * gain).astype(BF), weights)
    return rows, normed, rstd, sigmoid(both[:, :128]), both[:, 128:]


class Fill:
    def __init__(self):
        self.todo = []

    def __call__(self, count=1):
        for work in self.todo[:count]:
            work()
        self.todo = self.todo[count:]


class Place:
    def __init__(self):
        row, col = lax.axis_index("row"), lax.axis_index("col")
        self.row, self.col = row, col
        self.x, self.yh = row // 2, lax.rem(row, 2)
        self.yl, self.z = col // 16, lax.rem(col // 2, 8)
        self.e = lax.rem(col, 2)

    def at(self, x=None, y=None, z=None, e=None):
        here = self.yh * 2 + self.yl
        y = here if y is None else lax.rem(here + y + 4, 4)
        x = self.x if x is None else lax.rem(self.x + x + 4, 4)
        z = self.z if z is None else lax.rem(self.z + z + 8, 8)
        e = self.e if e is None else 1 - self.e
        return (x * 2 + y // 2, lax.rem(y, 2) * 16 + z * 2 + e)

    def mate(self):
        return (self.row, (1 - self.yl) * 16 + self.z * 2 + self.e)

    def slot(self, same_y, dz):
        z = lax.rem(self.z + dz + 8, 8)
        yl = self.yl if same_y else 1 - self.yl
        return lax.rem(z, 2), yl * 4 + z // 2

    def across(self, same_y, dx):
        x = lax.rem(self.x + dx + 4, 4)
        yh = self.yh if same_y else 1 - self.yh
        return x * 2 + yh


def greet(place):
    barrier = pltpu.get_barrier_semaphore()
    partners = [
        place.at(e=1), place.at(z=1), place.at(z=-1), place.at(x=1), place.at(x=-1),
        place.at(y=1), place.at(y=-1),
    ]
    for partner in partners:
        pl.semaphore_signal(barrier, inc=1, device_id=partner, device_id_type=MESH)
    return lambda: pl.semaphore_wait(barrier, len(partners))


class Wire:
    def __init__(self, send, recv):
        self.send, self.recv = send, recv
        self.number, self.open = {}, []

    def copy(self, name, src, dst, to):
        index = self.number.setdefault(name, len(self.number))
        return pltpu.make_async_remote_copy(
            src_ref=src, dst_ref=dst, send_sem=self.send.at[index],
            recv_sem=self.recv.at[index], device_id=to, device_id_type=MESH,
        )

    def start(self, name, src, dst, to):
        made = self.copy(name, src, dst, to)
        made.start()
        self.open.append(made)

    def arrived(self, name, dst, to):
        self.copy(name, dst, dst, to).wait_recv()

    def finish(self):
        for made in self.open:
            made.wait_send()


def part_of(name, group):
    return (32 * group, 32 if name == "O" else 24)


def late_of(group):
    return (32 * group + 24, 8)


def halves_of(name, group):
    start, count = part_of(name, group)
    return (start, 16), (start + 16, count - 16)


def group_rows(group):
    return pl.ds(32 * group, 32), pl.ds(64 + 32 * group, 32)


def gather_kernel(
    left_ref, right_ref, rows_ref, cols_ref, mid_ref, gain_ref, lg, lpw, rg, rpw,
    lp_out, rp_out, tri_out, lp, rp, tri, flat, turned, turned_left, given, relay, send, recv, local,
):
    me = Place()
    wire = Wire(send, recv)
    met = greet(me)
    core, up, down, mate = me.at(e=1), me.at(z=1), me.at(z=-1), me.mate()
    east, west, north, south = me.at(x=1), me.at(x=-1), me.at(y=1), me.at(y=-1)
    gain = gain_ref[...]
    outs = []

    def channels(start, count, half):
        return pl.ds(pl.multiple_of(half * 64 + start, 8), count)

    def piece(same_y, dz, part, half=None):
        kh, slot = me.slot(same_y, dz)
        return lp.at[kh, slot, channels(*part, me.e if half is None else half)]

    def normed_rows(ref, t):
        rows = pl.ds(t * 256, 256)
        normed, _ = norm(ref[rows, :].astype(F32), -1)
        flat[rows, :] = normed * gain

    def gated(weights, rows, mask):
        both = nt(weights, rows.astype(BF))
        return sigmoid(both[:128]) * both[128:] * mask

    left_w = jnp.concatenate([lg[...].T, lpw[...].T], axis=0)
    for t in range(4):
        normed_rows(left_ref, t)

    @pl.loop(0, 8, unroll=4)
    def _(k):
        rows = flat[pl.ds(k, 128, stride=8), :]
        turned_left[pl.ds(k, 128, stride=8), :] = gated(
            left_w, rows, left_mask(mid_ref, rows_ref, k)
        )

    met()
    there = pl.ds(pl.multiple_of((1 - me.e) * 512, 512), 512)
    wire.start("core", turned_left.at[there], given, core)
    wire.arrived("core", given, core)
    own_kh, own_slot = me.slot(True, 0)

    @pl.loop(0, 8, unroll=2)
    def _(t):
        rows = pl.ds(pl.multiple_of(me.e * 512 + t * 64, 64), 64)
        ours = turned_left[rows, :].reshape(8, 8, 128)
        theirs = given[pl.ds(pl.multiple_of(t * 64, 64), 64), :].reshape(8, 8, 128)
        first = jnp.where(me.e == 0, ours, theirs)
        second = jnp.where(me.e == 0, theirs, ours)
        both = jnp.concatenate([first, second], axis=1)
        lp[own_kh, own_slot, channels(t * 8, 8, me.e)] = both.astype(BF)

    def copy(name, ref, to):
        wire.start(name, ref, ref, to)

    def left_send(g):
        ref = piece(True, 0, part_of("O", g))
        copy(f"z+O{g}1", ref, up)
        copy(f"z-O{g}1", ref, down)
        copy(f"m{g}", ref, mate)
        copy(f"cO{g}0", ref, core)

    def share(name, g, dz):
        copy(f"c{name}{g}{dz}", piece(name == "O", dz, (32 * g, 32)), core)

    def mate_step(g):
        wire.arrived(f"m{g}", piece(False, 0, (32 * g, 32)), mate)
        ref = piece(False, 0, part_of("Y", g))
        copy(f"z+Y{g}1", ref, up)
        copy(f"z-Y{g}1", ref, down)
        share("Y", g, 0)

    def left_step(name, g, d):
        same = name == "O"
        part, halves = part_of(name, g), halves_of(name, g)
        for way, sign, dz, to in ((0, "z+", -d, up), (1, "z-", d, down)):
            if d < 4:
                wire.arrived(f"{sign}{name}{g}{d}", piece(same, dz, part), to)
                on = part if d < 3 else halves[way]
                copy(f"{sign}{name}{g}{d + 1}", piece(same, dz, on), to)
            else:
                wire.arrived(f"{sign}{name}{g}{d}", piece(same, dz, halves[way]), to)
        if same:
            for dz in (-d, d)[d // 4:]:
                copy(f"y{g}{dz}", piece(True, dz, late_of(g)), mate)
                share("O", g, dz)

    def late(g, d):
        for dz in (-d, d)[d // 4:]:
            wire.arrived(f"y{g}{dz}", piece(False, dz, late_of(g)), mate)
            share("Y", g, dz)

    def shared(g):
        for name in ("O", "Y"):
            for dz in (0, -1, 1, -2, 2, -3, 3, 4):
                ref = piece(name == "O", dz, (32 * g, 32), 1 - me.e)
                wire.arrived(f"c{name}{g}{dz}", ref, core)

    right_w = jnp.concatenate([rg[...].T, rpw[...].T], axis=0)

    def right_turn():
        @pl.loop(0, 16, unroll=4)
        def _(k):
            first = flat[pl.ds(k, 64, stride=32), :]
            second = flat[pl.ds(k + 16, 64, stride=32), :]
            turned[pl.ds(k, 128, stride=16), :] = gated(
                right_w, jnp.concatenate([first, second], axis=0),
                right_mask(mid_ref, cols_ref, k),
            )

        @pl.loop(0, 16, unroll=4)
        def _(t):
            rows = pl.ds(pl.multiple_of(t * 128, 128), 128)
            part = turned[rows, :].reshape(8, 16, 128).astype(BF)
            rp[me.row, pl.ds(pl.multiple_of(t * 8, 8), 8)] = part

    def right_send(own, g):
        low, high = group_rows(g)
        ref = rp.at[me.across(own, 0)]
        tag = f"{own:d}{g}1"
        copy("x+a" + tag, ref.at[low], east)
        copy("x-b" + tag, ref.at[high], west)
        copy("x+b" + tag, ref.at[high], east)
        copy("x-a" + tag, ref.at[low], west)

    def right_step(own, g):
        low, high = group_rows(g)
        behind, ahead = rp.at[me.across(own, -1), low], rp.at[me.across(own, 1), high]
        wire.arrived(f"x+a{own:d}{g}1", behind, east)
        copy(f"x+a{own:d}{g}2", behind, east)
        wire.arrived(f"x-b{own:d}{g}1", ahead, west)
        copy(f"x-b{own:d}{g}2", ahead, west)

    def right_rest(own, g):
        low, high = group_rows(g)
        behind, ahead = rp.at[me.across(own, -1), high], rp.at[me.across(own, 1), low]
        far = rp.at[me.across(own, 2)]
        wire.arrived(f"x+b{own:d}{g}1", behind, east)
        wire.arrived(f"x-a{own:d}{g}1", ahead, west)
        wire.arrived(f"x+a{own:d}{g}2", far.at[low], east)
        wire.arrived(f"x-b{own:d}{g}2", far.at[high], west)

    def over_y(g):
        low, high = group_rows(g)
        wire.start(f"ya{g}", rp.at[me.row, low], relay.at[0, g], north)
        wire.start(f"yb{g}", rp.at[me.row, high], relay.at[1, g], south)

    def over_y_on(g):
        low, high = group_rows(g)
        here = me.yh * 2 + me.yl
        above, below = lax.rem(here + 3, 4), lax.rem(here + 1, 4)
        wire.arrived(f"ya{g}", relay.at[0, g], north)
        wire.start(f"ya{g}2", relay.at[0, g], rp.at[me.x * 2 + above // 2, low], north)
        wire.arrived(f"yb{g}", relay.at[1, g], south)
        wire.start(f"yb{g}2", relay.at[1, g], rp.at[me.x * 2 + below // 2, high], south)

    def pair_step(g):
        low, high = group_rows(g)
        pair = rp.at[me.across(False, 0)]
        wire.arrived(f"ya{g}2", pair.at[low], north)
        wire.arrived(f"yb{g}2", pair.at[high], south)
        right_send(False, g)

    def keep(g):
        for part in group_rows(g):
            for src, dst in ((lp.at[:, :, part], lp_out.at[:, :, part]),
                             (rp.at[:, part], rp_out.at[:, part])):
                made = pltpu.make_async_copy(src, dst, local.at[len(outs)])
                made.start()
                outs.append(made)

    def triangle(start):
        @pl.loop(0, 16, unroll=8)
        def _(t):
            c = start + t
            right = rp[:, c].reshape(128, 128).T
            right = jnp.concatenate([right[:64], right[64:]], axis=1)
            left = jnp.concatenate(
                [lp[0, :, c].reshape(128, 128), lp[1, :, c].reshape(128, 128)], axis=0
            )
            rows = pl.ds(pl.multiple_of(c * 8, 8), 8)
            tri[:, rows, :] = nn(right, left).reshape(8, 8, 128)

    def keep_triangle(g):
        for part in (pl.ds(256 * g, 256), pl.ds(512 + 256 * g, 256)):
            made = pltpu.make_async_copy(
                tri.at[:, part], tri_out.at[:, part], local.at[len(outs)]
            )
            made.start()
            outs.append(made)

    left_send(0)
    for t in range(4):
        normed_rows(right_ref, t)
    mate_step(0)
    for t in range(4, 8):
        normed_rows(right_ref, t)
    left_step("O", 0, 1)
    right_turn()
    right_send(True, 0)
    over_y(0)
    left_step("Y", 0, 1)
    left_step("O", 0, 2)
    late(0, 1)
    over_y_on(0)
    left_step("Y", 0, 2)
    right_step(True, 0)
    left_step("O", 0, 3)
    late(0, 2)
    pair_step(0)
    right_send(True, 1)
    over_y(1)
    left_step("Y", 0, 3)
    left_send(1)
    left_step("O", 0, 4)
    mate_step(1)
    late(0, 3)
    left_step("Y", 0, 4)
    late(0, 4)
    right_step(False, 0)
    left_step("O", 1, 1)
    over_y_on(1)
    right_rest(True, 0)
    left_step("Y", 1, 1)
    right_rest(False, 0)
    shared(0)
    keep(0)
    left_step("O", 1, 2)
    triangle(0)
    late(1, 1)
    right_step(True, 1)
    left_step("Y", 1, 2)
    triangle(16)
    pair_step(1)
    left_step("O", 1, 3)
    late(1, 2)
    triangle(64)
    left_step("Y", 1, 3)
    triangle(80)
    keep_triangle(0)
    right_step(False, 1)
    left_step("O", 1, 4)
    late(1, 3)
    left_step("Y", 1, 4)
    late(1, 4)
    right_rest(True, 1)
    right_rest(False, 1)
    shared(1)
    keep(1)
    for start in (32, 48, 96, 112):
        triangle(start)
    keep_triangle(1)
    for made in outs:
        made.wait()
    wire.finish()


def gather(*operands):
    return pl.pallas_call(
        gather_kernel,
        out_shape=(
            jax.ShapeDtypeStruct((2, 8, 128, 16, 128), BF),
            jax.ShapeDtypeStruct((8, 128, 16, 128), BF),
            jax.ShapeDtypeStruct((8, 1024, 128), F32),
        ),
        in_specs=[VMEM] * 4 + [SMEM] + [VMEM] * 5,
        out_specs=(ANY, ANY, ANY),
        scratch_shapes=[
            pltpu.VMEM((2, 8, 128, 16, 128), BF),
            pltpu.VMEM((8, 128, 16, 128), BF),
            pltpu.VMEM((8, 1024, 128), F32),
            pltpu.VMEM((2048, 128), F32),
            pltpu.VMEM((2048, 128), F32),
            pltpu.VMEM((1024, 128), F32),
            pltpu.VMEM((512, 128), F32),
            pltpu.VMEM((2, 2, 32, 16, 128), BF),
            pltpu.SemaphoreType.DMA((128,)),
            pltpu.SemaphoreType.DMA((128,)),
            pltpu.SemaphoreType.DMA((12,)),
        ],
        compiler_params=pltpu.CompilerParams(
            collective_id=0, has_side_effects=True, vmem_limit_bytes=LIMIT
        ),
        name="gather_panels",
    )(*operands)


def scatter_kernel(
    lp_hbm, rp_hbm, tri_hbm, left_ref, right_ref, rows_ref, cols_ref, mid_ref, gain_ref,
    lg, lpw, rg, rpw, left_out, right_out,
    lp, rp, tri, dl, dr,
    core_in, z_in, late_in, mate_in, give, got, x_in, relay, pair_in,
    flat_left, flat_right, back, norms, rstds, gates, values,
    send, recv, local,
):
    me = Place()
    wire = Wire(send, recv)
    met = greet(me)
    core, up, down, mate = me.at(e=1), me.at(z=1), me.at(z=-1), me.mate()
    east, west, north, south = me.at(x=1), me.at(x=-1), me.at(y=1), me.at(y=-1)
    gain = gain_ref[...]
    loads = ([], [])

    def load(g, src, dst):
        made = pltpu.make_async_copy(src, dst, local.at[len(loads[0]) + len(loads[1])])
        made.start()
        loads[g].append(made)

    for g in (0, 1):
        for part in group_rows(g):
            rows = pl.ds(part.start * 8, 256)
            load(g, tri_hbm.at[:, rows], tri.at[:, rows])
            load(g, rp_hbm.at[:, part], rp.at[:, part])
            load(g, lp_hbm.at[:, :, part], lp.at[:, :, part])

    fill = Fill()
    left_w = jnp.concatenate([lg[...], lpw[...]], axis=1)
    right_w = jnp.concatenate([rg[...], rpw[...]], axis=1)

    def ahead(ref, t, weights, shift):
        def work():
            _, normed, rstd, gate, value = project(ref, t, gain, weights)
            rows = pl.ds(shift + t * 256, 256)
            norms[rows, :] = normed
            rstds[rows, :] = jnp.broadcast_to(rstd, (256, 128))
            gates[rows, :] = gate
            values[rows, :] = value * gate * (1.0 - gate)

        return work

    for t in range(8):
        fill.todo.append(ahead(right_ref, t, right_w, 1024))
    for t in range(4):
        fill.todo.append(ahead(left_ref, t, left_w, 0))

    def side_back(count, weights, shift, out):
        for t in range(count):
            here, rows = pl.ds(t * 256, 256), pl.ds(shift + t * 256, 256)
            masked = back[here, :]
            d_value = (masked * gates[rows, :]).astype(BF)
            d_gate = (masked * values[rows, :]).astype(BF)
            d_norm = nt(jnp.concatenate([d_gate, d_value], axis=1), weights)
            result = norm_back(norms[rows, :], rstds[rows, :], gain, d_norm, -1)
            out[here, :] = result.astype(BF)

    def panels_back(half, start):
        @pl.loop(0, 16, unroll=8)
        def _(t):
            c = half * 64 + start + t
            rows = pl.ds(pl.multiple_of(c * 8, 8), 8)
            grad = tri[:, rows, :].reshape(64, 128).astype(BF)
            none = jnp.zeros((64, 128), BF)
            grad = jnp.concatenate(
                [
                    jnp.concatenate([grad, none], axis=1),
                    jnp.concatenate([none, grad], axis=1),
                ],
                axis=0,
            )
            right = rp[:, c].reshape(128, 128)
            left = jnp.concatenate(
                [lp[0, :, c].reshape(128, 128), lp[1, :, c].reshape(128, 128)], axis=1
            )
            d_left = nn(right, grad).astype(BF)
            dl[0, :, c] = d_left[:, :128].reshape(8, 16, 128)
            dl[1, :, c] = d_left[:, 128:].reshape(8, 16, 128)
            dr[:, c] = nt(left, grad).astype(BF).reshape(8, 16, 128)

    def block(which, dz, half=None):
        kh, slot = me.slot(which == 1, dz)
        start = (me.e if half is None else half) * 64
        return dl.at[kh, slot, pl.ds(pl.multiple_of(start, 64), 64)]

    def core_send(g):
        part = pl.ds(32 * g, 32)
        for dz in (4, 3, 5, 2, 6, 1, 7, 0):
            for which in (0, 1):
                wire.start(
                    f"c{which}{g}{dz}", block(which, dz, 1 - me.e).at[part],
                    core_in.at[which, dz, part], core,
                )

    def add(target, start, count, terms, out=None):
        def body(t):
            part = pl.ds(pl.multiple_of(start + t * 8, 8), 8)
            total = target[part].astype(F32)
            for term, shift in terms:
                place = pl.ds(pl.multiple_of(start - shift + t * 8, 8), 8)
                total = total + term[place].astype(F32)
            if out is None:
                target[part] = total.astype(BF)
            else:
                out(start // 8 + t, total)

        steps = count // 8
        if steps < 4:
            for t in range(steps):
                body(t)
        else:
            pl.loop(0, steps, unroll=4)(body)

    def ready(which, g, dz):
        part = pl.ds(32 * g, 32)
        wire.arrived(f"c{which}{g}{dz}", core_in.at[which, dz, part], core)
        start, count = late_of(g)
        if which == 0:
            add(block(0, dz), start, count, [(core_in.at[0, dz], 0)])
            wire.start(
                f"l{g}{dz}", block(0, dz).at[pl.ds(start, count)], late_in.at[g, dz], mate
            )
        else:
            wire.arrived(f"l{g}{dz}", late_in.at[g, dz], mate)

    def sum_part(which, g, dz, start, count, more, out=None):
        terms = [(core_in.at[which, dz], 0)] + more
        first, _ = late_of(g)
        plain = min(count, max(0, first - start))
        if plain:
            add(block(which, dz), start, plain, terms, out)
        if which == 1 and start + count > first:
            late = [(late_in.at[g, dz], first)]
            add(block(which, dz), first, start + count - first, terms + late, out)

    def put(name, way, ref, dst, part):
        sign, to = (("+", up), ("-", down))[way]
        wire.start(f"z{sign}{name}", ref.at[pl.ds(*part)], dst.at[pl.ds(*part)], to)

    def came(which, g, way, d):
        name = "O" if which else "Y"
        sign, to = (("+", up), ("-", down))[way]
        part = halves_of(name, g)[way] if d == 0 else part_of(name, g)
        ref = z_in.at[way, which, d]
        wire.arrived(f"z{sign}{name}{g}{d}", ref.at[pl.ds(*part)], to)
        return [(ref, 0)]

    def left_step(which, g, d):
        name = "O" if which else "Y"
        halves = halves_of(name, g)
        if d == 0:
            ready(which, g, 4)
            for way in (0, 1):
                sum_part(which, g, 4, *halves[way], [])
                put(f"{name}{g}0", way, block(which, 4), z_in.at[way, which, 0], halves[way])
            return
        for way in (0, 1):
            dz = 4 + d if way else 4 - d
            ready(which, g, dz)
            more = came(which, g, way, d - 1)
            if d == 1:
                sum_part(which, g, dz, *halves[way], more)
                sum_part(which, g, dz, *halves[1 - way], [])
            else:
                sum_part(which, g, dz, *part_of(name, g), more)
            put(
                f"{name}{g}{d}", way, block(which, dz), z_in.at[way, which, d],
                part_of(name, g),
            )

    def left_last_other(g):
        ready(0, g, 0)
        more = came(0, g, 0, 3) + came(0, g, 1, 3)
        start, count = part_of("Y", g)
        sum_part(0, g, 0, start, count, more)
        wire.start(
            f"mate{g}", block(0, 0).at[pl.ds(start, count)], mate_in.at[g], mate
        )

    def put_left(t, total):
        first, second = total[:, :8].reshape(64, 128), total[:, 8:].reshape(64, 128)
        rows = pl.ds(pl.multiple_of(me.e * 512 + t * 64, 64), 64)
        flat_left[rows, :] = jnp.where(me.e == 0, first, second)
        give[pl.ds(pl.multiple_of(t * 64, 64), 64), :] = jnp.where(me.e == 0, second, first)

    def left_last(g):
        ready(1, g, 0)
        more = came(1, g, 0, 3) + came(1, g, 1, 3)
        wire.arrived(f"mate{g}", mate_in.at[g], mate)
        start, count = part_of("Y", g)
        sum_part(1, g, 0, start, count, more + [(mate_in.at[g], start)], put_left)
        sum_part(1, g, 0, start + count, 8, more, put_left)
        rows = pl.ds(256 * g, 256)
        wire.start(f"last{g}", give.at[rows], got.at[rows], core)

    def column(which, dx):
        return dr.at[me.across(which == 1, dx)]

    def right_first(which, g):
        low, high = group_rows(g)
        ref = column(which, 2)
        wire.start(f"x+{which}{g}0", ref.at[low], x_in.at[0, which, 0, low], east)
        wire.start(f"x-{which}{g}0", ref.at[high], x_in.at[1, which, 0, high], west)

    def right_step(which, g):
        parts = group_rows(g)
        for way, sign, to, dx in ((0, "+", east, 1), (1, "-", west, 3)):
            ref = x_in.at[way, which, 0]
            wire.arrived(f"x{sign}{which}{g}0", ref.at[parts[way]], to)
            add(column(which, dx), parts[way].start, 32, [(ref, 0)])
            for part, tag in zip(parts, "ab"):
                wire.start(
                    f"x{sign}{which}{g}1{tag}", column(which, dx).at[part],
                    x_in.at[way, which, 1, part], to,
                )

    def right_came(which, g):
        for way, sign, to in ((0, "+", east), (1, "-", west)):
            for part, tag in zip(group_rows(g), "ab"):
                ref = x_in.at[way, which, 1, part]
                wire.arrived(f"x{sign}{which}{g}1{tag}", ref, to)
        return [(x_in.at[0, which, 1], 0), (x_in.at[1, which, 1], 0)]

    def right_last_other(g):
        terms = right_came(0, g)
        low, high = group_rows(g)
        for part in (low, high):
            add(column(0, 0), part.start, 32, terms)
        wire.start(f"ya{g}", column(0, 0).at[low], relay.at[0, g], north)
        wire.start(f"yb{g}", column(0, 0).at[high], relay.at[1, g], south)

    def over_y_on(g):
        low, high = group_rows(g)
        wire.arrived(f"ya{g}", relay.at[0, g], north)
        wire.start(f"ya{g}2", relay.at[0, g], pair_in.at[low], north)
        wire.arrived(f"yb{g}", relay.at[1, g], south)
        wire.start(f"yb{g}2", relay.at[1, g], pair_in.at[high], south)

    def put_right(t, total):
        rows = pl.ds(pl.multiple_of(t * 128, 128), 128)
        flat_right[rows, :] = total.reshape(128, 128)

    def right_last(g):
        terms = right_came(1, g)
        low, high = group_rows(g)
        wire.arrived(f"ya{g}2", pair_in.at[low], north)
        wire.arrived(f"yb{g}2", pair_in.at[high], south)
        for part in (low, high):
            add(column(1, 0), part.start, 32, terms + [(pair_in, 0)], put_right)

    for made in loads[0]:
        made.wait()
    for start in (0, 16):
        panels_back(1 - me.e, start)
    met()
    core_send(0)
    for start in (0, 16):
        panels_back(me.e, start)
    right_first(0, 0)
    right_first(1, 0)
    left_step(0, 0, 0)
    left_step(1, 0, 0)
    for made in loads[1]:
        made.wait()
    panels_back(1 - me.e, 32)
    left_step(0, 0, 1)
    right_step(0, 0)
    panels_back(1 - me.e, 48)
    core_send(1)
    left_step(1, 0, 1)
    right_step(1, 0)
    panels_back(me.e, 32)
    left_step(0, 0, 2)
    panels_back(me.e, 48)
    right_first(0, 1)
    right_first(1, 1)
    left_step(1, 0, 2)
    fill(1)
    left_step(0, 0, 3)
    left_step(0, 1, 0)
    right_last_other(0)
    left_step(1, 0, 3)
    left_step(1, 1, 0)
    fill(2)
    right_step(0, 1)
    left_step(0, 1, 1)
    over_y_on(0)
    left_last_other(0)
    left_step(1, 1, 1)
    right_step(1, 1)
    fill(2)
    left_last(0)
    right_last(0)
    fill(1)
    left_step(0, 1, 2)
    fill(2)
    left_step(1, 1, 2)
    right_last_other(1)
    fill(2)
    left_step(0, 1, 3)
    over_y_on(1)
    left_step(1, 1, 3)
    fill(2)
    left_last_other(1)
    right_last(1)

    @pl.loop(0, 16, unroll=4)
    def _(k):
        rows = flat_right[pl.ds(k, 128, stride=16), :] * right_mask(mid_ref, cols_ref, k)
        turned = rows.T
        back[pl.ds(k, 64, stride=32), :] = turned[:64, :]
        back[pl.ds(k + 16, 64, stride=32), :] = turned[64:, :]

    left_last(1)
    side_back(8, right_w, 1024, right_out)
    for g in (0, 1):
        rows = pl.ds(256 * g, 256)
        wire.arrived(f"last{g}", got.at[rows], core)
    flat_left[pl.ds(pl.multiple_of((1 - me.e) * 512, 512), 512), :] = got[...]

    @pl.loop(0, 8, unroll=4)
    def _(k):
        rows = flat_left[pl.ds(k, 128, stride=8), :] * left_mask(mid_ref, rows_ref, k)
        back[pl.ds(k, 128, stride=8), :] = rows.T

    side_back(4, left_w, 0, left_out)
    wire.finish()


def scatter(*operands):
    return pl.pallas_call(
        scatter_kernel,
        out_shape=(
            jax.ShapeDtypeStruct((1024, 128), BF),
            jax.ShapeDtypeStruct((2048, 128), BF),
        ),
        in_specs=[ANY, ANY, ANY] + [VMEM] * 4 + [SMEM] + [VMEM] * 5,
        out_specs=(VMEM, VMEM),
        scratch_shapes=[
            pltpu.VMEM((2, 8, 128, 16, 128), BF),
            pltpu.VMEM((8, 128, 16, 128), BF),
            pltpu.VMEM((8, 1024, 128), F32),
            pltpu.VMEM((2, 8, 128, 16, 128), BF),
            pltpu.VMEM((8, 128, 16, 128), BF),
            pltpu.VMEM((2, 8, 64, 16, 128), BF),
            pltpu.VMEM((2, 2, 4, 64, 16, 128), BF),
            pltpu.VMEM((2, 8, 8, 16, 128), BF),
            pltpu.VMEM((2, 24, 16, 128), BF),
            pltpu.VMEM((512, 128), F32),
            pltpu.VMEM((512, 128), F32),
            pltpu.VMEM((2, 2, 2, 128, 16, 128), BF),
            pltpu.VMEM((2, 2, 32, 16, 128), BF),
            pltpu.VMEM((128, 16, 128), BF),
            pltpu.VMEM((1024, 128), F32),
            pltpu.VMEM((2048, 128), F32),
            pltpu.VMEM((2048, 128), F32),
            pltpu.VMEM((3072, 128), F32),
            pltpu.VMEM((3072, 128), F32),
            pltpu.VMEM((3072, 128), F32),
            pltpu.VMEM((3072, 128), F32),
            pltpu.SemaphoreType.DMA((128,)),
            pltpu.SemaphoreType.DMA((128,)),
            pltpu.SemaphoreType.DMA((12,)),
        ],
        compiler_params=pltpu.CompilerParams(
            collective_id=1, has_side_effects=True, vmem_limit_bytes=LIMIT
        ),
        name="scatter_sums",
    )(*operands)


JS = 8


def middle_kernel(
    tri_ref, tile_ref, up_ref, in_gain_ref, gate_w_ref, mid_gain_ref, proj_w_ref,
    update_ref, d_tile_ref, d_tri_ref, flat,
):
    mid_gain = jnp.broadcast_to(mid_gain_ref[...], (128, 128)).T
    in_gain = in_gain_ref[...]
    proj_w = proj_w_ref[...]
    gate_w = gate_w_ref[...]

    for j in range(JS):
        normed, _ = norm(tri_ref[0, pl.ds(j, 128, stride=8), :], 0)
        value = tn((normed * mid_gain).astype(BF), proj_w)
        flat[pl.ds(j, 128, stride=8), :] = value

    for t in range(8):
        rows = pl.ds(t * 128, 128)
        items = pl.ds(t * 16, 16)
        tile = tile_ref[items].astype(F32).reshape(128, 128)
        upstream = up_ref[items].astype(F32).reshape(128, 128)
        normed, rstd = norm(tile, -1)
        gate = sigmoid(nn((normed * in_gain).astype(BF), gate_w))
        value = flat[rows, :]
        update_ref[items] = (gate * value).reshape(16, 8, 128).astype(BF)
        gated = upstream * gate
        flat[rows, :] = gated
        d_gate = (gated * value * (1.0 - gate)).astype(BF)
        d_norm = nt(d_gate, gate_w)
        d_tile = norm_back(normed, rstd, in_gain, d_norm, -1)
        d_tile_ref[items] = d_tile.reshape(16, 8, 128).astype(BF)

    for j in range(JS):
        here = pl.ds(j, 128, stride=8)
        normed, rstd = norm(tri_ref[0, here, :], 0)
        d_norm = nt(proj_w, flat[here, :].astype(BF))
        d_tri_ref[0, here, :] = norm_back(normed, rstd, mid_gain, d_norm, 0)


def middle(tri, tile, upstream, in_gain, gate_w, mid_gain, proj_w):
    cell = pl.BlockSpec((128, JS, 128), lambda s: (0, s, 0))
    cube = pl.BlockSpec((1, 1024, 128), lambda s: (s, 0, 0))
    whole = pl.BlockSpec((128, 128), lambda s: (0, 0))
    line = pl.BlockSpec((1, 128), lambda s: (0, 0))
    return pl.pallas_call(
        middle_kernel,
        grid=(64 // JS,),
        out_shape=(
            jax.ShapeDtypeStruct((128, 64, 128), BF),
            jax.ShapeDtypeStruct((128, 64, 128), BF),
            jax.ShapeDtypeStruct((8, 1024, 128), F32),
        ),
        in_specs=[cube, cell, cell, line, whole, line, whole],
        out_specs=(cell, cell, cube),
        scratch_shapes=[pltpu.VMEM((1024, 128), F32)],
        compiler_params=pltpu.CompilerParams(
            vmem_limit_bytes=LIMIT, dimension_semantics=("arbitrary",)
        ),
        name="middle",
    )(tri, tile, upstream, in_gain, gate_w, mid_gain, proj_w)


def body(
    pair_left,
    pair_right,
    pair_tile,
    d_update,
    mask_rows,
    mask_cols,
    mask_mid,
    ln_in_gain,
    left_gate_w,
    left_proj_w,
    right_gate_w,
    right_proj_w,
    out_gate_w,
    ln_mid_gain,
    out_proj_w,
):
    flat_left = pair_left.reshape(1024, 128)
    flat_right = pair_right.reshape(2048, 128)
    gain = ln_in_gain.reshape(1, 128)
    sides = (
        flat_left, flat_right, mask_rows.reshape(1, 128), mask_cols.reshape(1, 64),
        mask_mid, gain, left_gate_w, left_proj_w, right_gate_w, right_proj_w,
    )
    lp, rp, tri = gather(*sides)
    update, d_tile, d_tri = middle(
        tri, pair_tile, d_update, gain, out_gate_w, ln_mid_gain.reshape(1, 128), out_proj_w
    )
    d_left, d_right = scatter(lp, rp, d_tri, *sides)
    return (
        update,
        d_left.reshape(128, 8, 128),
        d_right.reshape(64, 32, 128),
        d_tile,
    )


def solution(mesh):
    in_specs = (
        P("row", "col", None),
        P("col", "row", None),
        P("row", "col", None),
        P("row", "col", None),
        P("row"),
        P("col"),
        P(),
        P(),
        P(),
        P(),
        P(),
        P(),
        P(),
        P(),
        P(),
    )
    out_specs = (
        P("row", "col", None),
        P("row", "col", None),
        P("col", "row", None),
        P("row", "col", None),
    )
    return jax.shard_map(body, mesh=mesh, in_specs=in_specs, out_specs=out_specs, check_vma=False)
```

```python
import functools

import jax
import jax.numpy as jnp
from jax import lax
from jax.experimental import pallas as pl
from jax.experimental.pallas import tpu as pltpu
from jax.sharding import PartitionSpec as P

MESH = pl.DeviceIdType.MESH
BF = jnp.bfloat16
F32 = jnp.float32
VMEM = pl.BlockSpec(memory_space=pltpu.VMEM)
SMEM = pl.BlockSpec(memory_space=pltpu.SMEM)
ANY = pl.BlockSpec(memory_space=pl.ANY)
LIMIT = 60 * 1024 * 1024


def nn(a, b):
    return lax.dot_general(a, b, (((1,), (0,)), ((), ())), preferred_element_type=F32)


def nt(a, b):
    return lax.dot_general(a, b, (((1,), (1,)), ((), ())), preferred_element_type=F32)


def tn(a, b):
    return lax.dot_general(a, b, (((0,), (0,)), ((), ())), preferred_element_type=F32)


def sigmoid(v):
    return 0.5 * jnp.tanh(0.5 * v) + 0.5


def norm(values, axis):
    centred = values - jnp.mean(values, axis=axis, keepdims=True)
    rstd = lax.rsqrt(jnp.mean(centred * centred, axis=axis, keepdims=True) + 1e-05)
    return centred * rstd, rstd


def norm_back(normed, rstd, gain, upstream, axis):
    scaled = upstream * gain
    inner = jnp.mean(scaled * normed, axis=axis, keepdims=True)
    return (scaled - jnp.mean(scaled, axis=axis, keepdims=True) - normed * inner) * rstd


def left_mask(mid_ref, rows_ref, k):
    keep = mid_ref[lax.axis_index("col") * 8 + k].astype(F32)
    return rows_ref[...].astype(F32) * keep


def right_mask(mid_ref, cols_ref, k):
    base = lax.axis_index("row") * 32 + k
    low = mid_ref[base].astype(F32)
    high = mid_ref[base + 16].astype(F32)
    cols = cols_ref[...].astype(F32)
    return jnp.concatenate([cols * low, cols * high], axis=1)


def project(ref, t, gain, weights):
    rows = pl.ds(t * 256, 256)
    normed, rstd = norm(ref[rows, :].astype(F32), -1)
    both = nn((normed * gain).astype(BF), weights)
    return rows, normed, rstd, sigmoid(both[:, :128]), both[:, 128:]


class Fill:
    def __init__(self):
        self.todo = []

    def __call__(self, count=1):
        for work in self.todo[:count]:
            work()
        self.todo = self.todo[count:]


class Place:
    def __init__(self):
        row, col = lax.axis_index("row"), lax.axis_index("col")
        self.row, self.col = row, col
        self.x, self.yh = row // 2, lax.rem(row, 2)
        self.yl, self.z = col // 16, lax.rem(col // 2, 8)
        self.e = lax.rem(col, 2)

    def at(self, x=None, y=None, z=None, e=None):
        here = self.yh * 2 + self.yl
        y = here if y is None else lax.rem(here + y + 4, 4)
        x = self.x if x is None else lax.rem(self.x + x + 4, 4)
        z = self.z if z is None else lax.rem(self.z + z + 8, 8)
        e = self.e if e is None else 1 - self.e
        return (x * 2 + y // 2, lax.rem(y, 2) * 16 + z * 2 + e)

    def mate(self):
        return (self.row, (1 - self.yl) * 16 + self.z * 2 + self.e)

    def slot(self, same_y, dz):
        z = lax.rem(self.z + dz + 8, 8)
        yl = self.yl if same_y else 1 - self.yl
        return lax.rem(z, 2), yl * 4 + z // 2

    def across(self, same_y, dx):
        x = lax.rem(self.x + dx + 4, 4)
        yh = self.yh if same_y else 1 - self.yh
        return x * 2 + yh


def greet(place):
    barrier = pltpu.get_barrier_semaphore()
    partners = [
        place.at(e=1), place.at(z=1), place.at(z=-1), place.at(x=1), place.at(x=-1),
        place.at(y=1), place.at(y=-1),
    ]
    for partner in partners:
        pl.semaphore_signal(barrier, inc=1, device_id=partner, device_id_type=MESH)
    return lambda: pl.semaphore_wait(barrier, len(partners))


class Wire:
    def __init__(self, send, recv):
        self.send, self.recv = send, recv
        self.number, self.open = {}, []

    def copy(self, name, src, dst, to):
        index = self.number.setdefault(name, len(self.number))
        return pltpu.make_async_remote_copy(
            src_ref=src, dst_ref=dst, send_sem=self.send.at[index],
            recv_sem=self.recv.at[index], device_id=to, device_id_type=MESH,
        )

    def start(self, name, src, dst, to):
        made = self.copy(name, src, dst, to)
        made.start()
        self.open.append(made)

    def arrived(self, name, dst, to):
        self.copy(name, dst, dst, to).wait_recv()

    def finish(self):
        for made in self.open:
            made.wait_send()


class Groups:
    def __init__(self, *sizes):
        self.size = sizes
        self.start = tuple(sum(sizes[:g]) for g in range(len(sizes)))

    def whole(self, g):
        return (self.start[g], self.size[g])

    def part(self, name, g):
        return (self.start[g], self.size[g] - (0 if name == "O" else 8))

    def late(self, g):
        return (self.start[g] + self.size[g] - 8, 8)

    def halves(self, name, g):
        start, count = self.part(name, g)
        first = count - 16 if name == "O" else count // 2
        return (start, first), (start + first, count - first)

    def rows(self, g):
        start, size = self.whole(g)
        return pl.ds(start, size), pl.ds(64 + start, size)


FORTH = Groups(40, 24)
BACK = Groups(24, 40)


def gather_kernel(
    left_ref, right_ref, rows_ref, cols_ref, mid_ref, gain_ref, lg, lpw, rg, rpw,
    lp_out, rp_out, tri_out, lp, rp, tri, flat, turned, turned_left, given, relay, send, recv, local,
):
    me = Place()
    wire = Wire(send, recv)
    met = greet(me)
    core, up, down, mate = me.at(e=1), me.at(z=1), me.at(z=-1), me.mate()
    east, west, north, south = me.at(x=1), me.at(x=-1), me.at(y=1), me.at(y=-1)
    gain = gain_ref[...]
    outs = []

    def channels(start, count, half):
        return pl.ds(pl.multiple_of(half * 64 + start, 8), count)

    def piece(same_y, dz, part, half=None):
        kh, slot = me.slot(same_y, dz)
        return lp.at[kh, slot, channels(*part, me.e if half is None else half)]

    def normed_rows(ref, t):
        rows = pl.ds(t * 256, 256)
        normed, _ = norm(ref[rows, :].astype(F32), -1)
        flat[rows, :] = normed * gain

    def gated(weights, rows, mask):
        both = nt(weights, rows.astype(BF))
        return sigmoid(both[:128]) * both[128:] * mask

    left_w = jnp.concatenate([lg[...].T, lpw[...].T], axis=0)
    for t in range(4):
        normed_rows(left_ref, t)

    @pl.loop(0, 8, unroll=4)
    def _(k):
        rows = flat[pl.ds(k, 128, stride=8), :]
        turned_left[pl.ds(k, 128, stride=8), :] = gated(
            left_w, rows, left_mask(mid_ref, rows_ref, k)
        )

    met()
    there = pl.ds(pl.multiple_of((1 - me.e) * 512, 512), 512)
    wire.start("core", turned_left.at[there], given, core)
    for t in range(4):
        normed_rows(right_ref, t)
    wire.arrived("core", given, core)
    own_kh, own_slot = me.slot(True, 0)

    @pl.loop(0, 8, unroll=2)
    def _(t):
        rows = pl.ds(pl.multiple_of(me.e * 512 + t * 64, 64), 64)
        ours = turned_left[rows, :].reshape(8, 8, 128)
        theirs = given[pl.ds(pl.multiple_of(t * 64, 64), 64), :].reshape(8, 8, 128)
        first = jnp.where(me.e == 0, ours, theirs)
        second = jnp.where(me.e == 0, theirs, ours)
        both = jnp.concatenate([first, second], axis=1)
        lp[own_kh, own_slot, channels(t * 8, 8, me.e)] = both.astype(BF)

    def copy(name, ref, to):
        wire.start(name, ref, ref, to)

    def left_send(g):
        ref = piece(True, 0, FORTH.part("O", g))
        copy(f"z+O{g}1", ref, up)
        copy(f"z-O{g}1", ref, down)
        copy(f"m{g}", ref, mate)
        copy(f"cO{g}0", ref, core)

    def share(name, g, dz):
        copy(f"c{name}{g}{dz}", piece(name == "O", dz, FORTH.whole(g)), core)

    def mate_step(g):
        wire.arrived(f"m{g}", piece(False, 0, FORTH.whole(g)), mate)
        ref = piece(False, 0, FORTH.part("Y", g))
        copy(f"z+Y{g}1", ref, up)
        copy(f"z-Y{g}1", ref, down)
        share("Y", g, 0)

    def left_step(name, g, d):
        same = name == "O"
        part, halves = FORTH.part(name, g), FORTH.halves(name, g)
        for way, sign, dz, to in ((0, "z+", -d, up), (1, "z-", d, down)):
            if d < 4:
                wire.arrived(f"{sign}{name}{g}{d}", piece(same, dz, part), to)
                on = part if d < 3 else halves[way]
                copy(f"{sign}{name}{g}{d + 1}", piece(same, dz, on), to)
            else:
                wire.arrived(f"{sign}{name}{g}{d}", piece(same, dz, halves[way]), to)
        if same:
            for dz in (-d, d)[d // 4:]:
                copy(f"y{g}{dz}", piece(True, dz, FORTH.late(g)), mate)
                share("O", g, dz)

    def late(g, d):
        for dz in (-d, d)[d // 4:]:
            wire.arrived(f"y{g}{dz}", piece(False, dz, FORTH.late(g)), mate)
            share("Y", g, dz)

    def shared(g):
        for name in ("O", "Y"):
            for dz in (0, -1, 1, -2, 2, -3, 3, 4):
                ref = piece(name == "O", dz, FORTH.whole(g), 1 - me.e)
                wire.arrived(f"c{name}{g}{dz}", ref, core)

    right_w = jnp.concatenate([rg[...].T, rpw[...].T], axis=0)

    def right_turn():
        @pl.loop(0, 16, unroll=4)
        def _(k):
            first = flat[pl.ds(k, 64, stride=32), :]
            second = flat[pl.ds(k + 16, 64, stride=32), :]
            turned[pl.ds(k, 128, stride=16), :] = gated(
                right_w, jnp.concatenate([first, second], axis=0),
                right_mask(mid_ref, cols_ref, k),
            )

        @pl.loop(0, 16, unroll=4)
        def _(t):
            rows = pl.ds(pl.multiple_of(t * 128, 128), 128)
            part = turned[rows, :].reshape(8, 16, 128).astype(BF)
            rp[me.row, pl.ds(pl.multiple_of(t * 8, 8), 8)] = part

    def right_send(own, g):
        low, high = FORTH.rows(g)
        ref = rp.at[me.across(own, 0)]
        tag = f"{own:d}{g}1"
        copy("x+a" + tag, ref.at[low], east)
        copy("x-b" + tag, ref.at[high], west)
        copy("x+b" + tag, ref.at[high], east)
        copy("x-a" + tag, ref.at[low], west)

    def right_step(own, g):
        low, high = FORTH.rows(g)
        behind, ahead = rp.at[me.across(own, -1), low], rp.at[me.across(own, 1), high]
        wire.arrived(f"x+a{own:d}{g}1", behind, east)
        copy(f"x+a{own:d}{g}2", behind, east)
        wire.arrived(f"x-b{own:d}{g}1", ahead, west)
        copy(f"x-b{own:d}{g}2", ahead, west)

    def right_rest(own, g):
        low, high = FORTH.rows(g)
        behind, ahead = rp.at[me.across(own, -1), high], rp.at[me.across(own, 1), low]
        far = rp.at[me.across(own, 2)]
        wire.arrived(f"x+b{own:d}{g}1", behind, east)
        wire.arrived(f"x-a{own:d}{g}1", ahead, west)
        wire.arrived(f"x+a{own:d}{g}2", far.at[low], east)
        wire.arrived(f"x-b{own:d}{g}2", far.at[high], west)

    def over_y(g):
        low, high = FORTH.rows(g)
        wire.start(f"ya{g}", rp.at[me.row, low], relay.at[0, g, pl.ds(0, FORTH.size[g])], north)
        wire.start(f"yb{g}", rp.at[me.row, high], relay.at[1, g, pl.ds(0, FORTH.size[g])], south)

    def over_y_on(g):
        low, high = FORTH.rows(g)
        here = me.yh * 2 + me.yl
        above, below = lax.rem(here + 3, 4), lax.rem(here + 1, 4)
        wire.arrived(f"ya{g}", relay.at[0, g, pl.ds(0, FORTH.size[g])], north)
        wire.start(f"ya{g}2", relay.at[0, g, pl.ds(0, FORTH.size[g])], rp.at[me.x * 2 + above // 2, low], north)
        wire.arrived(f"yb{g}", relay.at[1, g, pl.ds(0, FORTH.size[g])], south)
        wire.start(f"yb{g}2", relay.at[1, g, pl.ds(0, FORTH.size[g])], rp.at[me.x * 2 + below // 2, high], south)

    def pair_step(g):
        low, high = FORTH.rows(g)
        pair = rp.at[me.across(False, 0)]
        wire.arrived(f"ya{g}2", pair.at[low], north)
        wire.arrived(f"yb{g}2", pair.at[high], south)
        right_send(False, g)

    def keep(g):
        for part in FORTH.rows(g):
            for src, dst in ((lp.at[:, :, part], lp_out.at[:, :, part]),
                             (rp.at[:, part], rp_out.at[:, part])):
                made = pltpu.make_async_copy(src, dst, local.at[len(outs)])
                made.start()
                outs.append(made)

    def triangle(start, count):
        @pl.loop(0, count, unroll=8)
        def _(t):
            c = start + t
            right = rp[:, c].reshape(128, 128).T
            right = jnp.concatenate([right[:64], right[64:]], axis=1)
            left = jnp.concatenate(
                [lp[0, :, c].reshape(128, 128), lp[1, :, c].reshape(128, 128)], axis=0
            )
            rows = pl.ds(pl.multiple_of(c * 8, 8), 8)
            tri[:, rows, :] = nn(right, left).reshape(8, 8, 128)

    def keep_triangle(g):
        for rows in FORTH.rows(g):
            part = pl.ds(rows.start * 8, rows.size * 8)
            made = pltpu.make_async_copy(
                tri.at[:, part], tri_out.at[:, part], local.at[len(outs)]
            )
            made.start()
            outs.append(made)

    left_send(0)
    left_send(1)
    for t in range(4, 8):
        normed_rows(right_ref, t)
    right_turn()
    right_send(True, 0)
    over_y(0)
    mate_step(0)
    left_step("O", 0, 1)
    left_step("Y", 0, 1)
    left_step("O", 0, 2)
    late(0, 1)
    over_y_on(0)
    left_step("Y", 0, 2)
    right_step(True, 0)
    right_send(True, 1)
    mate_step(1)
    left_step("O", 0, 3)
    late(0, 2)
    pair_step(0)
    over_y(1)
    left_step("Y", 0, 3)
    left_step("O", 1, 1)
    left_step("O", 0, 4)
    late(0, 3)
    left_step("Y", 0, 4)
    left_step("Y", 1, 1)
    late(0, 4)
    right_step(False, 0)
    over_y_on(1)
    left_step("O", 1, 2)
    right_rest(True, 0)
    late(1, 1)
    right_step(True, 1)
    left_step("Y", 1, 2)
    right_rest(False, 0)
    shared(0)
    keep(0)
    triangle(0, 16)
    left_step("O", 1, 3)
    pair_step(1)
    triangle(16, 24)
    late(1, 2)
    left_step("Y", 1, 3)
    triangle(64, 16)
    left_step("O", 1, 4)
    late(1, 3)
    right_step(False, 1)
    triangle(80, 24)
    keep_triangle(0)
    left_step("Y", 1, 4)
    late(1, 4)
    right_rest(True, 1)
    right_rest(False, 1)
    shared(1)
    keep(1)
    triangle(40, 24)
    triangle(104, 24)
    keep_triangle(1)
    for made in outs:
        made.wait()
    wire.finish()


def gather(*operands):
    return pl.pallas_call(
        gather_kernel,
        out_shape=(
            jax.ShapeDtypeStruct((2, 8, 128, 16, 128), BF),
            jax.ShapeDtypeStruct((8, 128, 16, 128), BF),
            jax.ShapeDtypeStruct((8, 1024, 128), F32),
        ),
        in_specs=[VMEM] * 4 + [SMEM] + [VMEM] * 5,
        out_specs=(ANY, ANY, ANY),
        scratch_shapes=[
            pltpu.VMEM((2, 8, 128, 16, 128), BF),
            pltpu.VMEM((8, 128, 16, 128), BF),
            pltpu.VMEM((8, 1024, 128), F32),
            pltpu.VMEM((2048, 128), F32),
            pltpu.VMEM((2048, 128), F32),
            pltpu.VMEM((1024, 128), F32),
            pltpu.VMEM((512, 128), F32),
            pltpu.VMEM((2, 2, 40, 16, 128), BF),
            pltpu.SemaphoreType.DMA((128,)),
            pltpu.SemaphoreType.DMA((128,)),
            pltpu.SemaphoreType.DMA((12,)),
        ],
        compiler_params=pltpu.CompilerParams(
            collective_id=0, has_side_effects=True, vmem_limit_bytes=LIMIT
        ),
        name="gather_panels",
    )(*operands)


def scatter_kernel(
    lp_hbm, rp_hbm, tri_hbm, left_ref, right_ref, rows_ref, cols_ref, mid_ref, gain_ref,
    lg, lpw, rg, rpw, both_out,
    lp, rp, tri, dl, dr,
    core_in, z_in, late_in, mate_in, give, got, x_in, relay, pair_in,
    flat_left, flat_right, back, norms, rstds, gates, values,
    send, recv, local,
):
    me = Place()
    wire = Wire(send, recv)
    met = greet(me)
    core, up, down, mate = me.at(e=1), me.at(z=1), me.at(z=-1), me.mate()
    east, west, north, south = me.at(x=1), me.at(x=-1), me.at(y=1), me.at(y=-1)
    gain = gain_ref[...]
    loads = ([], [])

    def load(g, src, dst):
        made = pltpu.make_async_copy(src, dst, local.at[len(loads[0]) + len(loads[1])])
        made.start()
        loads[g].append(made)

    for g in (0, 1):
        for part in BACK.rows(g):
            rows = pl.ds(part.start * 8, part.size * 8)
            load(g, tri_hbm.at[:, rows], tri.at[:, rows])
            load(g, rp_hbm.at[:, part], rp.at[:, part])
            load(g, lp_hbm.at[:, :, part], lp.at[:, :, part])

    fill = Fill()
    left_w = jnp.concatenate([lg[...], lpw[...]], axis=1)
    right_w = jnp.concatenate([rg[...], rpw[...]], axis=1)

    def ahead(ref, t, weights, shift):
        def work():
            _, normed, rstd, gate, value = project(ref, t, gain, weights)
            rows = pl.ds(shift + t * 256, 256)
            norms[rows, :] = normed
            rstds[rows, :] = jnp.broadcast_to(rstd, (256, 128))
            gates[rows, :] = gate
            values[rows, :] = value * gate * (1.0 - gate)

        return work

    for t in range(8):
        fill.todo.append(ahead(right_ref, t, right_w, 1024))
    for t in range(4):
        fill.todo.append(ahead(left_ref, t, left_w, 0))

    def side_back(steps, weights, shift):
        for t in steps:
            here, rows = pl.ds(t * 256, 256), pl.ds(shift + t * 256, 256)
            masked = back[here, :]
            d_value = (masked * gates[rows, :]).astype(BF)
            d_gate = (masked * values[rows, :]).astype(BF)
            d_norm = nt(jnp.concatenate([d_gate, d_value], axis=1), weights)
            result = norm_back(norms[rows, :], rstds[rows, :], gain, d_norm, -1)
            both_out[rows, :] = result.astype(BF)

    def panels_back(half, start, count):
        @pl.loop(0, count, unroll=8)
        def _(t):
            c = half * 64 + start + t
            rows = pl.ds(pl.multiple_of(c * 8, 8), 8)
            grad = tri[:, rows, :].reshape(64, 128).astype(BF)
            none = jnp.zeros((64, 128), BF)
            grad = jnp.concatenate(
                [
                    jnp.concatenate([grad, none], axis=1),
                    jnp.concatenate([none, grad], axis=1),
                ],
                axis=0,
            )
            right = rp[:, c].reshape(128, 128)
            left = jnp.concatenate(
                [lp[0, :, c].reshape(128, 128), lp[1, :, c].reshape(128, 128)], axis=1
            )
            d_left = nn(right, grad).astype(BF)
            dl[0, :, c] = d_left[:, :128].reshape(8, 16, 128)
            dl[1, :, c] = d_left[:, 128:].reshape(8, 16, 128)
            dr[:, c] = nt(left, grad).astype(BF).reshape(8, 16, 128)

    def block(which, dz, half=None):
        kh, slot = me.slot(which == 1, dz)
        start = (me.e if half is None else half) * 64
        return dl.at[kh, slot, pl.ds(pl.multiple_of(start, 64), 64)]

    def core_send(g):
        part = pl.ds(*BACK.whole(g))
        for dz in (4, 3, 5, 2, 6, 1, 7, 0):
            for which in (0, 1):
                wire.start(
                    f"c{which}{g}{dz}", block(which, dz, 1 - me.e).at[part],
                    core_in.at[which, dz, part], core,
                )

    def add(target, start, count, terms, out=None):
        def body(t):
            part = pl.ds(pl.multiple_of(start + t * 8, 8), 8)
            total = target[part].astype(F32)
            for term, shift in terms:
                place = pl.ds(pl.multiple_of(start - shift + t * 8, 8), 8)
                total = total + term[place].astype(F32)
            if out is None:
                target[part] = total.astype(BF)
            else:
                out(start // 8 + t, total)

        steps = count // 8
        if steps < 6:
            for t in range(steps):
                body(t)
        else:
            pl.loop(0, steps, unroll=4)(body)

    def ready(which, g, dz):
        part = pl.ds(*BACK.whole(g))
        wire.arrived(f"c{which}{g}{dz}", core_in.at[which, dz, part], core)
        start, count = BACK.late(g)
        if which == 0:
            add(block(0, dz), start, count, [(core_in.at[0, dz], 0)])
            wire.start(
                f"l{g}{dz}", block(0, dz).at[pl.ds(start, count)], late_in.at[g, dz], mate
            )
        else:
            wire.arrived(f"l{g}{dz}", late_in.at[g, dz], mate)

    def sum_part(which, g, dz, start, count, more, out=None):
        terms = [(core_in.at[which, dz], 0)] + more
        first, _ = BACK.late(g)
        plain = min(count, max(0, first - start))
        if plain:
            add(block(which, dz), start, plain, terms, out)
        if which == 1 and start + count > first:
            late = [(late_in.at[g, dz], first)]
            add(block(which, dz), first, start + count - first, terms + late, out)

    def put(name, way, ref, dst, part):
        sign, to = (("+", up), ("-", down))[way]
        wire.start(f"z{sign}{name}", ref.at[pl.ds(*part)], dst.at[pl.ds(*part)], to)

    def came(which, g, way, d):
        name = "O" if which else "Y"
        sign, to = (("+", up), ("-", down))[way]
        part = BACK.halves(name, g)[way] if d == 0 else BACK.part(name, g)
        ref = z_in.at[way, which, d]
        wire.arrived(f"z{sign}{name}{g}{d}", ref.at[pl.ds(*part)], to)
        return [(ref, 0)]

    def left_step(which, g, d):
        name = "O" if which else "Y"
        halves = BACK.halves(name, g)
        if d == 0:
            ready(which, g, 4)
            for way in (0, 1):
                sum_part(which, g, 4, *halves[way], [])
                put(f"{name}{g}0", way, block(which, 4), z_in.at[way, which, 0], halves[way])
            return
        for way in (0, 1):
            dz = 4 + d if way else 4 - d
            ready(which, g, dz)
            more = came(which, g, way, d - 1)
            if d == 1:
                sum_part(which, g, dz, *halves[way], more)
                sum_part(which, g, dz, *halves[1 - way], [])
            else:
                sum_part(which, g, dz, *BACK.part(name, g), more)
            put(
                f"{name}{g}{d}", way, block(which, dz), z_in.at[way, which, d],
                BACK.part(name, g),
            )

    def left_last_other(g):
        ready(0, g, 0)
        more = came(0, g, 0, 3) + came(0, g, 1, 3)
        start, count = BACK.part("Y", g)
        sum_part(0, g, 0, start, count, more)
        wire.start(
            f"mate{g}", block(0, 0).at[pl.ds(start, count)],
            mate_in.at[g, pl.ds(0, count)], mate,
        )

    def put_left(t, total):
        first, second = total[:, :8].reshape(64, 128), total[:, 8:].reshape(64, 128)
        rows = pl.ds(pl.multiple_of(me.e * 512 + t * 64, 64), 64)
        flat_left[rows, :] = jnp.where(me.e == 0, first, second)
        give[pl.ds(pl.multiple_of(t * 64, 64), 64), :] = jnp.where(me.e == 0, second, first)

    def left_last(g):
        ready(1, g, 0)
        more = came(1, g, 0, 3) + came(1, g, 1, 3)
        start, count = BACK.part("Y", g)
        wire.arrived(f"mate{g}", mate_in.at[g, pl.ds(0, count)], mate)
        sum_part(1, g, 0, start, count, more + [(mate_in.at[g], start)], put_left)
        sum_part(1, g, 0, start + count, 8, more, put_left)
        rows = pl.ds(BACK.start[g] * 8, BACK.size[g] * 8)
        wire.start(f"last{g}", give.at[rows], got.at[rows], core)

    def column(which, dx):
        return dr.at[me.across(which == 1, dx)]

    def right_first(which, g):
        low, high = BACK.rows(g)
        ref = column(which, 2)
        wire.start(f"x+{which}{g}0", ref.at[low], x_in.at[0, which, 0, low], east)
        wire.start(f"x-{which}{g}0", ref.at[high], x_in.at[1, which, 0, high], west)

    def right_step(which, g):
        parts = BACK.rows(g)
        for way, sign, to, dx in ((0, "+", east, 1), (1, "-", west, 3)):
            ref = x_in.at[way, which, 0]
            wire.arrived(f"x{sign}{which}{g}0", ref.at[parts[way]], to)
            add(column(which, dx), parts[way].start, BACK.size[g], [(ref, 0)])
            for part, tag in zip(parts, "ab"):
                wire.start(
                    f"x{sign}{which}{g}1{tag}", column(which, dx).at[part],
                    x_in.at[way, which, 1, part], to,
                )

    def right_came(which, g):
        for way, sign, to in ((0, "+", east), (1, "-", west)):
            for part, tag in zip(BACK.rows(g), "ab"):
                ref = x_in.at[way, which, 1, part]
                wire.arrived(f"x{sign}{which}{g}1{tag}", ref, to)
        return [(x_in.at[0, which, 1], 0), (x_in.at[1, which, 1], 0)]

    def right_last_other(g):
        terms = right_came(0, g)
        low, high = BACK.rows(g)
        for part in (low, high):
            add(column(0, 0), part.start, BACK.size[g], terms)
        wire.start(f"ya{g}", column(0, 0).at[low], relay.at[0, g, pl.ds(0, BACK.size[g])], north)
        wire.start(f"yb{g}", column(0, 0).at[high], relay.at[1, g, pl.ds(0, BACK.size[g])], south)

    def over_y_on(g):
        low, high = BACK.rows(g)
        wire.arrived(f"ya{g}", relay.at[0, g, pl.ds(0, BACK.size[g])], north)
        wire.start(f"ya{g}2", relay.at[0, g, pl.ds(0, BACK.size[g])], pair_in.at[low], north)
        wire.arrived(f"yb{g}", relay.at[1, g, pl.ds(0, BACK.size[g])], south)
        wire.start(f"yb{g}2", relay.at[1, g, pl.ds(0, BACK.size[g])], pair_in.at[high], south)

    def put_right(t, total):
        rows = pl.ds(pl.multiple_of(t * 128, 128), 128)
        flat_right[rows, :] = total.reshape(128, 128)

    def right_last(g):
        terms = right_came(1, g)
        low, high = BACK.rows(g)
        wire.arrived(f"ya{g}2", pair_in.at[low], north)
        wire.arrived(f"yb{g}2", pair_in.at[high], south)
        for part in (low, high):
            add(column(1, 0), part.start, BACK.size[g], terms + [(pair_in, 0)], put_right)

    for made in loads[0]:
        made.wait()
    panels_back(1 - me.e, 0, 24)
    met()
    core_send(0)
    panels_back(me.e, 0, 24)
    right_first(0, 0)
    right_first(1, 0)
    left_step(0, 0, 0)
    left_step(1, 0, 0)
    for made in loads[1]:
        made.wait()
    panels_back(1 - me.e, 24, 16)
    left_step(0, 0, 1)
    right_step(0, 0)
    panels_back(1 - me.e, 40, 24)
    core_send(1)
    left_step(1, 0, 1)
    right_step(1, 0)
    panels_back(me.e, 24, 16)
    left_step(0, 0, 2)
    panels_back(me.e, 40, 24)
    right_first(0, 1)
    right_first(1, 1)
    left_step(1, 0, 2)
    left_step(0, 1, 0)
    left_step(1, 1, 0)
    fill(1)
    left_step(0, 0, 3)
    right_last_other(0)
    left_step(1, 0, 3)
    fill(2)
    right_step(0, 1)
    left_step(0, 1, 1)
    over_y_on(0)
    left_last_other(0)
    left_step(1, 1, 1)
    right_step(1, 1)
    fill(3)
    left_last(0)
    right_last(0)
    fill(1)
    left_step(0, 1, 2)
    fill(2)
    left_step(1, 1, 2)
    right_last_other(1)
    fill(3)
    left_step(0, 1, 3)
    over_y_on(1)
    left_step(1, 1, 3)
    right_last(1)

    @pl.loop(0, 16, unroll=4)
    def _(k):
        rows = flat_right[pl.ds(k, 128, stride=16), :] * right_mask(mid_ref, cols_ref, k)
        turned = rows.T
        back[pl.ds(k, 64, stride=32), :] = turned[:64, :]
        back[pl.ds(k + 16, 64, stride=32), :] = turned[64:, :]

    left_last_other(1)
    side_back(range(5), right_w, 1024)
    left_last(1)
    side_back(range(5, 8), right_w, 1024)
    for g in (0, 1):
        rows = pl.ds(BACK.start[g] * 8, BACK.size[g] * 8)
        wire.arrived(f"last{g}", got.at[rows], core)
    flat_left[pl.ds(pl.multiple_of((1 - me.e) * 512, 512), 512), :] = got[...]

    @pl.loop(0, 8, unroll=4)
    def _(k):
        rows = flat_left[pl.ds(k, 128, stride=8), :] * left_mask(mid_ref, rows_ref, k)
        back[pl.ds(k, 128, stride=8), :] = rows.T

    side_back(range(4), left_w, 0)
    wire.finish()


def scatter(*operands):
    return pl.pallas_call(
        scatter_kernel,
        out_shape=jax.ShapeDtypeStruct((3072, 128), BF),
        in_specs=[ANY, ANY, ANY] + [VMEM] * 4 + [SMEM] + [VMEM] * 5,
        out_specs=VMEM,
        scratch_shapes=[
            pltpu.VMEM((2, 8, 128, 16, 128), BF),
            pltpu.VMEM((8, 128, 16, 128), BF),
            pltpu.VMEM((8, 1024, 128), F32),
            pltpu.VMEM((2, 8, 128, 16, 128), BF),
            pltpu.VMEM((8, 128, 16, 128), BF),
            pltpu.VMEM((2, 8, 64, 16, 128), BF),
            pltpu.VMEM((2, 2, 4, 64, 16, 128), BF),
            pltpu.VMEM((2, 8, 8, 16, 128), BF),
            pltpu.VMEM((2, 32, 16, 128), BF),
            pltpu.VMEM((512, 128), F32),
            pltpu.VMEM((512, 128), F32),
            pltpu.VMEM((2, 2, 2, 128, 16, 128), BF),
            pltpu.VMEM((2, 2, 40, 16, 128), BF),
            pltpu.VMEM((128, 16, 128), BF),
            pltpu.VMEM((1024, 128), F32),
            pltpu.VMEM((2048, 128), F32),
            pltpu.VMEM((2048, 128), F32),
            pltpu.VMEM((3072, 128), F32),
            pltpu.VMEM((3072, 128), F32),
            pltpu.VMEM((3072, 128), F32),
            pltpu.VMEM((3072, 128), F32),
            pltpu.SemaphoreType.DMA((128,)),
            pltpu.SemaphoreType.DMA((128,)),
            pltpu.SemaphoreType.DMA((12,)),
        ],
        compiler_params=pltpu.CompilerParams(
            collective_id=1, has_side_effects=True, vmem_limit_bytes=LIMIT
        ),
        name="scatter_sums",
    )(*operands)


def split_kernel(both, left_out, right_out, local):
    made = []
    for step in range(6):
        src = both.at[pl.ds(step * 512, 512)]
        out, shift = (left_out, 0) if step < 2 else (right_out, 2)
        dst = out.at[pl.ds((step - shift) * 512, 512)]
        made.append(pltpu.make_async_copy(src, dst, local.at[step]))
    for one in made:
        one.start()
    for one in made:
        one.wait()


def split(both):
    return pl.pallas_call(
        split_kernel,
        out_shape=(
            jax.ShapeDtypeStruct((1024, 128), BF),
            jax.ShapeDtypeStruct((2048, 128), BF),
        ),
        in_specs=[ANY],
        out_specs=(ANY, ANY),
        scratch_shapes=[pltpu.SemaphoreType.DMA((6,))],
        name="split_sides",
    )(both)


JS = 8


def middle_kernel(
    tri_ref, tile_ref, up_ref, in_gain_ref, gate_w_ref, mid_gain_ref, proj_w_ref,
    update_ref, d_tile_ref, d_tri_ref, flat, rstds,
):
    mid_gain = jnp.broadcast_to(mid_gain_ref[...], (128, 128)).T
    in_gain = in_gain_ref[...]
    proj_w = proj_w_ref[...]
    gate_w = gate_w_ref[...]

    for j in range(JS):
        normed, rstd = norm(tri_ref[0, pl.ds(j, 128, stride=8), :], 0)
        d_tri_ref[0, pl.ds(j, 128, stride=8), :] = normed
        rstds[pl.ds(j, 1), :] = rstd
        value = tn((normed * mid_gain).astype(BF), proj_w)
        flat[pl.ds(j, 128, stride=8), :] = value

    for t in range(8):
        rows = pl.ds(t * 128, 128)
        items = pl.ds(t * 16, 16)
        tile = tile_ref[items].astype(F32).reshape(128, 128)
        upstream = up_ref[items].astype(F32).reshape(128, 128)
        normed, rstd = norm(tile, -1)
        gate = sigmoid(nn((normed * in_gain).astype(BF), gate_w))
        value = flat[rows, :]
        update_ref[items] = (gate * value).reshape(16, 8, 128).astype(BF)
        gated = upstream * gate
        flat[rows, :] = gated
        d_gate = (gated * value * (1.0 - gate)).astype(BF)
        d_norm = nt(d_gate, gate_w)
        d_tile = norm_back(normed, rstd, in_gain, d_norm, -1)
        d_tile_ref[items] = d_tile.reshape(16, 8, 128).astype(BF)

    for j in range(JS):
        here = pl.ds(j, 128, stride=8)
        normed, rstd = d_tri_ref[0, here, :], rstds[pl.ds(j, 1), :]
        d_norm = nt(proj_w, flat[here, :].astype(BF))
        d_tri_ref[0, here, :] = norm_back(normed, rstd, mid_gain, d_norm, 0)


def middle(tri, tile, upstream, in_gain, gate_w, mid_gain, proj_w):
    cell = pl.BlockSpec((128, JS, 128), lambda s: (0, s, 0))
    cube = pl.BlockSpec((1, 1024, 128), lambda s: (s, 0, 0))
    whole = pl.BlockSpec((128, 128), lambda s: (0, 0))
    line = pl.BlockSpec((1, 128), lambda s: (0, 0))
    return pl.pallas_call(
        middle_kernel,
        grid=(64 // JS,),
        out_shape=(
            jax.ShapeDtypeStruct((128, 64, 128), BF),
            jax.ShapeDtypeStruct((128, 64, 128), BF),
            jax.ShapeDtypeStruct((8, 1024, 128), F32),
        ),
        in_specs=[cube, cell, cell, line, whole, line, whole],
        out_specs=(cell, cell, cube),
        scratch_shapes=[pltpu.VMEM((1024, 128), F32), pltpu.VMEM((JS, 128), F32)],
        compiler_params=pltpu.CompilerParams(
            vmem_limit_bytes=LIMIT, dimension_semantics=("arbitrary",)
        ),
        name="middle",
    )(tri, tile, upstream, in_gain, gate_w, mid_gain, proj_w)


def body(
    pair_left,
    pair_right,
    pair_tile,
    d_update,
    mask_rows,
    mask_cols,
    mask_mid,
    ln_in_gain,
    left_gate_w,
    left_proj_w,
    right_gate_w,
    right_proj_w,
    out_gate_w,
    ln_mid_gain,
    out_proj_w,
):
    flat_left = pair_left.reshape(1024, 128)
    flat_right = pair_right.reshape(2048, 128)
    gain = ln_in_gain.reshape(1, 128)
    sides = (
        flat_left, flat_right, mask_rows.reshape(1, 128), mask_cols.reshape(1, 64),
        mask_mid, gain, left_gate_w, left_proj_w, right_gate_w, right_proj_w,
    )
    lp, rp, tri = gather(*sides)
    update, d_tile, d_tri = middle(
        tri, pair_tile, d_update, gain, out_gate_w, ln_mid_gain.reshape(1, 128), out_proj_w
    )
    d_left, d_right = split(scatter(lp, rp, d_tri, *sides))
    return (
        update,
        d_left.reshape(128, 8, 128),
        d_right.reshape(64, 32, 128),
        d_tile,
    )


def solution(mesh):
    in_specs = (
        P("row", "col", None),
        P("col", "row", None),
        P("row", "col", None),
        P("row", "col", None),
        P("row"),
        P("col"),
        P(),
        P(),
        P(),
        P(),
        P(),
        P(),
        P(),
        P(),
        P(),
    )
    out_specs = (
        P("row", "col", None),
        P("row", "col", None),
        P("col", "row", None),
        P("row", "col", None),
    )
    return jax.shard_map(body, mesh=mesh, in_specs=in_specs, out_specs=out_specs, check_vma=False)
```

```python
import functools

import jax
import jax.numpy as jnp
from jax import lax
from jax.experimental import pallas as pl
from jax.experimental.pallas import tpu as pltpu
from jax.sharding import PartitionSpec as P

MESH = pl.DeviceIdType.MESH
BF = jnp.bfloat16
F32 = jnp.float32
VMEM = pl.BlockSpec(memory_space=pltpu.VMEM)
SMEM = pl.BlockSpec(memory_space=pltpu.SMEM)
ANY = pl.BlockSpec(memory_space=pl.ANY)
LIMIT = 60 * 1024 * 1024


def nn(a, b):
    return lax.dot_general(a, b, (((1,), (0,)), ((), ())), preferred_element_type=F32)


def nt(a, b):
    return lax.dot_general(a, b, (((1,), (1,)), ((), ())), preferred_element_type=F32)


def tn(a, b):
    return lax.dot_general(a, b, (((0,), (0,)), ((), ())), preferred_element_type=F32)


def sigmoid(v):
    return 0.5 * jnp.tanh(0.5 * v) + 0.5


def norm(values, axis):
    centred = values - jnp.mean(values, axis=axis, keepdims=True)
    rstd = lax.rsqrt(jnp.mean(centred * centred, axis=axis, keepdims=True) + 1e-05)
    return centred * rstd, rstd


def norm_back(normed, rstd, gain, upstream, axis):
    scaled = upstream * gain
    inner = jnp.mean(scaled * normed, axis=axis, keepdims=True)
    return (scaled - jnp.mean(scaled, axis=axis, keepdims=True) - normed * inner) * rstd


def left_mask(mid_ref, rows_ref, k):
    keep = mid_ref[lax.axis_index("col") * 8 + k].astype(F32)
    return rows_ref[...].astype(F32) * keep


def right_mask(mid_ref, cols_ref, k):
    base = lax.axis_index("row") * 32 + k
    low = mid_ref[base].astype(F32)
    high = mid_ref[base + 16].astype(F32)
    cols = cols_ref[...].astype(F32)
    return jnp.concatenate([cols * low, cols * high], axis=1)


def project(ref, t, gain, weights):
    rows = pl.ds(t * 256, 256)
    normed, rstd = norm(ref[rows, :].astype(F32), -1)
    both = nn((normed * gain).astype(BF), weights)
    return rows, normed, rstd, sigmoid(both[:, :128]), both[:, 128:]


class Fill:
    def __init__(self):
        self.todo = []

    def __call__(self, count=1):
        for work in self.todo[:count]:
            work()
        self.todo = self.todo[count:]


class Place:
    def __init__(self):
        row, col = lax.axis_index("row"), lax.axis_index("col")
        self.row, self.col = row, col
        self.x, self.yh = row // 2, lax.rem(row, 2)
        self.yl, self.z = col // 16, lax.rem(col // 2, 8)
        self.e = lax.rem(col, 2)

    def at(self, x=None, y=None, z=None, e=None):
        here = self.yh * 2 + self.yl
        y = here if y is None else lax.rem(here + y + 4, 4)
        x = self.x if x is None else lax.rem(self.x + x + 4, 4)
        z = self.z if z is None else lax.rem(self.z + z + 8, 8)
        e = self.e if e is None else 1 - self.e
        return (x * 2 + y // 2, lax.rem(y, 2) * 16 + z * 2 + e)

    def mate(self):
        return (self.row, (1 - self.yl) * 16 + self.z * 2 + self.e)

    def slot(self, same_y, dz):
        z = lax.rem(self.z + dz + 8, 8)
        yl = self.yl if same_y else 1 - self.yl
        return lax.rem(z, 2), yl * 4 + z // 2

    def across(self, same_y, dx):
        x = lax.rem(self.x + dx + 4, 4)
        yh = self.yh if same_y else 1 - self.yh
        return x * 2 + yh


def greet(place):
    barrier = pltpu.get_barrier_semaphore()
    partners = [
        place.at(e=1), place.at(z=1), place.at(z=-1), place.at(x=1), place.at(x=-1),
        place.at(y=1), place.at(y=-1),
    ]
    for partner in partners:
        pl.semaphore_signal(barrier, inc=1, device_id=partner, device_id_type=MESH)
    return lambda: pl.semaphore_wait(barrier, len(partners))


class Wire:
    def __init__(self, send, recv):
        self.send, self.recv = send, recv
        self.number, self.open = {}, []

    def copy(self, name, src, dst, to):
        index = self.number.setdefault(name, len(self.number))
        return pltpu.make_async_remote_copy(
            src_ref=src, dst_ref=dst, send_sem=self.send.at[index],
            recv_sem=self.recv.at[index], device_id=to, device_id_type=MESH,
        )

    def start(self, name, src, dst, to):
        made = self.copy(name, src, dst, to)
        made.start()
        self.open.append(made)

    def arrived(self, name, dst, to):
        self.copy(name, dst, dst, to).wait_recv()

    def finish(self):
        for made in self.open:
            made.wait_send()


class Groups:
    def __init__(self, *sizes):
        self.size = sizes
        self.start = tuple(sum(sizes[:g]) for g in range(len(sizes)))

    def whole(self, g):
        return (self.start[g], self.size[g])

    def part(self, name, g):
        return (self.start[g], self.size[g] - (0 if name == "O" else 8))

    def late(self, g):
        return (self.start[g] + self.size[g] - 8, 8)

    def halves(self, name, g):
        start, count = self.part(name, g)
        first = count - 16 if name == "O" else count // 2
        return (start, first), (start + first, count - first)

    def rows(self, g):
        start, size = self.whole(g)
        return pl.ds(start, size), pl.ds(64 + start, size)


FORTH = Groups(40, 24)
BACK = Groups(24, 40)


def gather_kernel(
    left_ref, right_ref, rows_ref, cols_ref, mid_ref, gain_ref, lg, lpw, rg, rpw,
    lp_out, rp_out, tri_out, lp, rp, tri, flat, turned, turned_left, given, relay, send, recv, local,
):
    me = Place()
    wire = Wire(send, recv)
    met = greet(me)
    core, up, down, mate = me.at(e=1), me.at(z=1), me.at(z=-1), me.mate()
    east, west, north, south = me.at(x=1), me.at(x=-1), me.at(y=1), me.at(y=-1)
    gain = gain_ref[...]
    outs = []

    def channels(start, count, half):
        return pl.ds(pl.multiple_of(half * 64 + start, 8), count)

    def piece(same_y, dz, part, half=None):
        kh, slot = me.slot(same_y, dz)
        return lp.at[kh, slot, channels(*part, me.e if half is None else half)]

    def normed_rows(ref, t):
        rows = pl.ds(t * 256, 256)
        normed, _ = norm(ref[rows, :].astype(F32), -1)
        flat[rows, :] = normed * gain

    def gated(weights, rows, mask):
        both = nt(weights, rows.astype(BF))
        return sigmoid(both[:128]) * both[128:] * mask

    left_w = jnp.concatenate([lg[...].T, lpw[...].T], axis=0)
    for t in range(4):
        normed_rows(left_ref, t)

    @pl.loop(0, 8, unroll=4)
    def _(k):
        rows = flat[pl.ds(k, 128, stride=8), :]
        turned_left[pl.ds(k, 128, stride=8), :] = gated(
            left_w, rows, left_mask(mid_ref, rows_ref, k)
        )

    met()
    there = pl.ds(pl.multiple_of((1 - me.e) * 512, 512), 512)
    wire.start("core", turned_left.at[there], given, core)
    for t in range(4):
        normed_rows(right_ref, t)
    wire.arrived("core", given, core)
    own_kh, own_slot = me.slot(True, 0)

    @pl.loop(0, 8, unroll=2)
    def _(t):
        rows = pl.ds(pl.multiple_of(me.e * 512 + t * 64, 64), 64)
        ours = turned_left[rows, :].reshape(8, 8, 128)
        theirs = given[pl.ds(pl.multiple_of(t * 64, 64), 64), :].reshape(8, 8, 128)
        first = jnp.where(me.e == 0, ours, theirs)
        second = jnp.where(me.e == 0, theirs, ours)
        both = jnp.concatenate([first, second], axis=1)
        lp[own_kh, own_slot, channels(t * 8, 8, me.e)] = both.astype(BF)

    def copy(name, ref, to):
        wire.start(name, ref, ref, to)

    def left_send(g):
        ref = piece(True, 0, FORTH.part("O", g))
        copy(f"z+O{g}1", ref, up)
        copy(f"z-O{g}1", ref, down)
        copy(f"m{g}", ref, mate)
        copy(f"cO{g}0", ref, core)

    def share(name, g, dz):
        copy(f"c{name}{g}{dz}", piece(name == "O", dz, FORTH.whole(g)), core)

    def mate_step(g):
        wire.arrived(f"m{g}", piece(False, 0, FORTH.whole(g)), mate)
        ref = piece(False, 0, FORTH.part("Y", g))
        copy(f"z+Y{g}1", ref, up)
        copy(f"z-Y{g}1", ref, down)
        share("Y", g, 0)

    def left_step(name, g, d):
        same = name == "O"
        part, halves = FORTH.part(name, g), FORTH.halves(name, g)
        for way, sign, dz, to in ((0, "z+", -d, up), (1, "z-", d, down)):
            if d < 4:
                wire.arrived(f"{sign}{name}{g}{d}", piece(same, dz, part), to)
                on = part if d < 3 else halves[way]
                copy(f"{sign}{name}{g}{d + 1}", piece(same, dz, on), to)
            else:
                wire.arrived(f"{sign}{name}{g}{d}", piece(same, dz, halves[way]), to)
        if same:
            for dz in (-d, d)[d // 4:]:
                copy(f"y{g}{dz}", piece(True, dz, FORTH.late(g)), mate)
                share("O", g, dz)

    def late(g, d):
        for dz in (-d, d)[d // 4:]:
            wire.arrived(f"y{g}{dz}", piece(False, dz, FORTH.late(g)), mate)
            share("Y", g, dz)

    def shared(g):
        for name in ("O", "Y"):
            for dz in (0, -1, 1, -2, 2, -3, 3, 4):
                ref = piece(name == "O", dz, FORTH.whole(g), 1 - me.e)
                wire.arrived(f"c{name}{g}{dz}", ref, core)

    right_w = jnp.concatenate([rg[...].T, rpw[...].T], axis=0)

    def right_turn():
        @pl.loop(0, 16, unroll=4)
        def _(k):
            first = flat[pl.ds(k, 64, stride=32), :]
            second = flat[pl.ds(k + 16, 64, stride=32), :]
            turned[pl.ds(k, 128, stride=16), :] = gated(
                right_w, jnp.concatenate([first, second], axis=0),
                right_mask(mid_ref, cols_ref, k),
            )

        @pl.loop(0, 16, unroll=4)
        def _(t):
            rows = pl.ds(pl.multiple_of(t * 128, 128), 128)
            part = turned[rows, :].reshape(8, 16, 128).astype(BF)
            rp[me.row, pl.ds(pl.multiple_of(t * 8, 8), 8)] = part

    def right_send(own, g):
        low, high = FORTH.rows(g)
        ref = rp.at[me.across(own, 0)]
        tag = f"{own:d}{g}1"
        copy("x+a" + tag, ref.at[low], east)
        copy("x-b" + tag, ref.at[high], west)
        copy("x+b" + tag, ref.at[high], east)
        copy("x-a" + tag, ref.at[low], west)

    def right_step(own, g):
        low, high = FORTH.rows(g)
        behind, ahead = rp.at[me.across(own, -1), low], rp.at[me.across(own, 1), high]
        wire.arrived(f"x+a{own:d}{g}1", behind, east)
        copy(f"x+a{own:d}{g}2", behind, east)
        wire.arrived(f"x-b{own:d}{g}1", ahead, west)
        copy(f"x-b{own:d}{g}2", ahead, west)

    def right_rest(own, g):
        low, high = FORTH.rows(g)
        behind, ahead = rp.at[me.across(own, -1), high], rp.at[me.across(own, 1), low]
        far = rp.at[me.across(own, 2)]
        wire.arrived(f"x+b{own:d}{g}1", behind, east)
        wire.arrived(f"x-a{own:d}{g}1", ahead, west)
        wire.arrived(f"x+a{own:d}{g}2", far.at[low], east)
        wire.arrived(f"x-b{own:d}{g}2", far.at[high], west)

    def over_y(g):
        low, high = FORTH.rows(g)
        wire.start(f"ya{g}", rp.at[me.row, low], relay.at[0, g, pl.ds(0, FORTH.size[g])], north)
        wire.start(f"yb{g}", rp.at[me.row, high], relay.at[1, g, pl.ds(0, FORTH.size[g])], south)

    def over_y_on(g):
        low, high = FORTH.rows(g)
        here = me.yh * 2 + me.yl
        above, below = lax.rem(here + 3, 4), lax.rem(here + 1, 4)
        wire.arrived(f"ya{g}", relay.at[0, g, pl.ds(0, FORTH.size[g])], north)
        wire.start(f"ya{g}2", relay.at[0, g, pl.ds(0, FORTH.size[g])], rp.at[me.x * 2 + above // 2, low], north)
        wire.arrived(f"yb{g}", relay.at[1, g, pl.ds(0, FORTH.size[g])], south)
        wire.start(f"yb{g}2", relay.at[1, g, pl.ds(0, FORTH.size[g])], rp.at[me.x * 2 + below // 2, high], south)

    def pair_step(g):
        low, high = FORTH.rows(g)
        pair = rp.at[me.across(False, 0)]
        wire.arrived(f"ya{g}2", pair.at[low], north)
        wire.arrived(f"yb{g}2", pair.at[high], south)
        right_send(False, g)

    def keep(g):
        for part in FORTH.rows(g):
            for src, dst in ((lp.at[:, :, part], lp_out.at[:, :, part]),
                             (rp.at[:, part], rp_out.at[:, part])):
                made = pltpu.make_async_copy(src, dst, local.at[len(outs)])
                made.start()
                outs.append(made)

    def triangle(start, count):
        @pl.loop(0, count, unroll=8)
        def _(t):
            c = start + t
            right = rp[:, c].reshape(128, 128).T
            right = jnp.concatenate([right[:64], right[64:]], axis=1)
            left = jnp.concatenate(
                [lp[0, :, c].reshape(128, 128), lp[1, :, c].reshape(128, 128)], axis=0
            )
            rows = pl.ds(pl.multiple_of(c * 8, 8), 8)
            tri[:, rows, :] = nn(right, left).reshape(8, 8, 128)

    def keep_triangle(g):
        for rows in FORTH.rows(g):
            part = pl.ds(rows.start * 8, rows.size * 8)
            made = pltpu.make_async_copy(
                tri.at[:, part], tri_out.at[:, part], local.at[len(outs)]
            )
            made.start()
            outs.append(made)

    left_send(0)
    left_send(1)
    for t in range(4, 8):
        normed_rows(right_ref, t)
    right_turn()
    right_send(True, 0)
    over_y(0)
    mate_step(0)
    left_step("O", 0, 1)
    left_step("Y", 0, 1)
    left_step("O", 0, 2)
    late(0, 1)
    over_y_on(0)
    mate_step(1)
    left_step("O", 1, 1)
    left_step("Y", 0, 2)
    right_step(True, 0)
    right_send(True, 1)
    left_step("O", 0, 3)
    late(0, 2)
    pair_step(0)
    over_y(1)
    left_step("Y", 1, 1)
    left_step("Y", 0, 3)
    left_step("O", 1, 2)
    late(1, 1)
    left_step("O", 0, 4)
    late(0, 3)
    left_step("Y", 0, 4)
    late(0, 4)
    left_step("Y", 1, 2)
    over_y_on(1)
    right_step(True, 1)
    right_step(False, 0)
    left_step("O", 1, 3)
    late(1, 2)
    pair_step(1)
    left_step("Y", 1, 3)
    right_rest(True, 0)
    right_rest(False, 0)
    shared(0)
    keep(0)
    triangle(0, 16)
    left_step("O", 1, 4)
    late(1, 3)
    triangle(16, 24)
    right_step(False, 1)
    left_step("Y", 1, 4)
    late(1, 4)
    triangle(64, 16)
    triangle(80, 24)
    keep_triangle(0)
    right_rest(True, 1)
    right_rest(False, 1)
    shared(1)
    keep(1)
    triangle(40, 24)
    triangle(104, 24)
    keep_triangle(1)
    for made in outs:
        made.wait()
    wire.finish()


def gather(*operands):
    return pl.pallas_call(
        gather_kernel,
        out_shape=(
            jax.ShapeDtypeStruct((2, 8, 128, 16, 128), BF),
            jax.ShapeDtypeStruct((8, 128, 16, 128), BF),
            jax.ShapeDtypeStruct((8, 1024, 128), F32),
        ),
        in_specs=[VMEM] * 4 + [SMEM] + [VMEM] * 5,
        out_specs=(ANY, ANY, ANY),
        scratch_shapes=[
            pltpu.VMEM((2, 8, 128, 16, 128), BF),
            pltpu.VMEM((8, 128, 16, 128), BF),
            pltpu.VMEM((8, 1024, 128), F32),
            pltpu.VMEM((2048, 128), F32),
            pltpu.VMEM((2048, 128), F32),
            pltpu.VMEM((1024, 128), F32),
            pltpu.VMEM((512, 128), F32),
            pltpu.VMEM((2, 2, 40, 16, 128), BF),
            pltpu.SemaphoreType.DMA((128,)),
            pltpu.SemaphoreType.DMA((128,)),
            pltpu.SemaphoreType.DMA((12,)),
        ],
        compiler_params=pltpu.CompilerParams(
            collective_id=0, has_side_effects=True, vmem_limit_bytes=LIMIT
        ),
        name="gather_panels",
    )(*operands)


def scatter_kernel(
    lp_hbm, rp_hbm, tri_hbm, left_ref, right_ref, rows_ref, cols_ref, mid_ref, gain_ref,
    lg, lpw, rg, rpw, both_out,
    lp, rp, tri, dl, dr,
    core_in, z_in, late_in, mate_in, give, got, x_in, relay, pair_in,
    flat_left, flat_right, back, norms, rstds, gates, values,
    send, recv, local,
):
    me = Place()
    wire = Wire(send, recv)
    met = greet(me)
    core, up, down, mate = me.at(e=1), me.at(z=1), me.at(z=-1), me.mate()
    east, west, north, south = me.at(x=1), me.at(x=-1), me.at(y=1), me.at(y=-1)
    gain = gain_ref[...]
    loads = []

    for g in (0, 1):
        start, size = BACK.whole(g)
        for side in (1 - me.e, me.e):
            part = pl.ds(pl.multiple_of(side * 64 + start, 8), size)
            rows = pl.ds(pl.multiple_of((side * 64 + start) * 8, 64), size * 8)
            for src, dst in (
                (tri_hbm.at[:, rows], tri.at[:, rows]),
                (rp_hbm.at[:, part], rp.at[:, part]),
                (lp_hbm.at[:, :, part], lp.at[:, :, part]),
            ):
                made = pltpu.make_async_copy(src, dst, local.at[len(loads)])
                made.start()
                loads.append(made)

    def loaded(count):
        for made in loads[:count]:
            made.wait()
        del loads[:count]

    fill = Fill()
    left_w = jnp.concatenate([lg[...], lpw[...]], axis=1)
    right_w = jnp.concatenate([rg[...], rpw[...]], axis=1)

    def ahead(ref, t, weights, shift):
        def work():
            _, normed, rstd, gate, value = project(ref, t, gain, weights)
            rows = pl.ds(shift + t * 256, 256)
            norms[rows, :] = normed
            rstds[rows, :] = jnp.broadcast_to(rstd, (256, 128))
            gates[rows, :] = gate
            values[rows, :] = value * gate * (1.0 - gate)

        return work

    for t in range(8):
        fill.todo.append(ahead(right_ref, t, right_w, 1024))
    for t in range(4):
        fill.todo.append(ahead(left_ref, t, left_w, 0))

    def side_back(steps, weights, shift):
        for t in steps:
            here, rows = pl.ds(t * 256, 256), pl.ds(shift + t * 256, 256)
            masked = back[here, :]
            d_value = (masked * gates[rows, :]).astype(BF)
            d_gate = (masked * values[rows, :]).astype(BF)
            d_norm = nt(jnp.concatenate([d_gate, d_value], axis=1), weights)
            result = norm_back(norms[rows, :], rstds[rows, :], gain, d_norm, -1)
            both_out[rows, :] = result.astype(BF)

    def panels_back(half, start, count):
        @pl.loop(0, count, unroll=8)
        def _(t):
            c = half * 64 + start + t
            rows = pl.ds(pl.multiple_of(c * 8, 8), 8)
            grad = tri[:, rows, :].reshape(64, 128).astype(BF)
            none = jnp.zeros((64, 128), BF)
            grad = jnp.concatenate(
                [
                    jnp.concatenate([grad, none], axis=1),
                    jnp.concatenate([none, grad], axis=1),
                ],
                axis=0,
            )
            right = rp[:, c].reshape(128, 128)
            left = jnp.concatenate(
                [lp[0, :, c].reshape(128, 128), lp[1, :, c].reshape(128, 128)], axis=1
            )
            d_left = nn(right, grad).astype(BF)
            dl[0, :, c] = d_left[:, :128].reshape(8, 16, 128)
            dl[1, :, c] = d_left[:, 128:].reshape(8, 16, 128)
            dr[:, c] = nt(left, grad).astype(BF).reshape(8, 16, 128)

    def block(which, dz, half=None):
        kh, slot = me.slot(which == 1, dz)
        start = (me.e if half is None else half) * 64
        return dl.at[kh, slot, pl.ds(pl.multiple_of(start, 64), 64)]

    def core_send(g):
        part = pl.ds(*BACK.whole(g))
        for dz in (4, 3, 5, 2, 6, 1, 7, 0):
            for which in (0, 1):
                wire.start(
                    f"c{which}{g}{dz}", block(which, dz, 1 - me.e).at[part],
                    core_in.at[which, dz, part], core,
                )

    def add(target, start, count, terms, out=None):
        def body(t):
            part = pl.ds(pl.multiple_of(start + t * 8, 8), 8)
            total = target[part].astype(F32)
            for term, shift in terms:
                place = pl.ds(pl.multiple_of(start - shift + t * 8, 8), 8)
                total = total + term[place].astype(F32)
            if out is None:
                target[part] = total.astype(BF)
            else:
                out(start // 8 + t, total)

        steps = count // 8
        if steps < 6:
            for t in range(steps):
                body(t)
        else:
            pl.loop(0, steps, unroll=4)(body)

    def ready(which, g, dz):
        part = pl.ds(*BACK.whole(g))
        wire.arrived(f"c{which}{g}{dz}", core_in.at[which, dz, part], core)
        start, count = BACK.late(g)
        if which == 0:
            add(block(0, dz), start, count, [(core_in.at[0, dz], 0)])
            wire.start(
                f"l{g}{dz}", block(0, dz).at[pl.ds(start, count)], late_in.at[g, dz], mate
            )
        else:
            wire.arrived(f"l{g}{dz}", late_in.at[g, dz], mate)

    def sum_part(which, g, dz, start, count, more, out=None):
        terms = [(core_in.at[which, dz], 0)] + more
        first, _ = BACK.late(g)
        plain = min(count, max(0, first - start))
        if plain:
            add(block(which, dz), start, plain, terms, out)
        if which == 1 and start + count > first:
            late = [(late_in.at[g, dz], first)]
            add(block(which, dz), first, start + count - first, terms + late, out)

    def put(name, way, ref, dst, part):
        sign, to = (("+", up), ("-", down))[way]
        wire.start(f"z{sign}{name}", ref.at[pl.ds(*part)], dst.at[pl.ds(*part)], to)

    def came(which, g, way, d):
        name = "O" if which else "Y"
        sign, to = (("+", up), ("-", down))[way]
        part = BACK.halves(name, g)[way] if d == 0 else BACK.part(name, g)
        ref = z_in.at[way, which, d]
        wire.arrived(f"z{sign}{name}{g}{d}", ref.at[pl.ds(*part)], to)
        return [(ref, 0)]

    def left_step(which, g, d):
        name = "O" if which else "Y"
        halves = BACK.halves(name, g)
        if d == 0:
            ready(which, g, 4)
            for way in (0, 1):
                sum_part(which, g, 4, *halves[way], [])
                put(f"{name}{g}0", way, block(which, 4), z_in.at[way, which, 0], halves[way])
            return
        for way in (0, 1):
            dz = 4 + d if way else 4 - d
            ready(which, g, dz)
            more = came(which, g, way, d - 1)
            if d == 1:
                sum_part(which, g, dz, *halves[way], more)
                sum_part(which, g, dz, *halves[1 - way], [])
            else:
                sum_part(which, g, dz, *BACK.part(name, g), more)
            put(
                f"{name}{g}{d}", way, block(which, dz), z_in.at[way, which, d],
                BACK.part(name, g),
            )

    def left_last_other(g):
        ready(0, g, 0)
        more = came(0, g, 0, 3) + came(0, g, 1, 3)
        start, count = BACK.part("Y", g)
        sum_part(0, g, 0, start, count, more)
        wire.start(
            f"mate{g}", block(0, 0).at[pl.ds(start, count)],
            mate_in.at[g, pl.ds(0, count)], mate,
        )

    def put_left(t, total):
        first, second = total[:, :8].reshape(64, 128), total[:, 8:].reshape(64, 128)
        rows = pl.ds(pl.multiple_of(me.e * 512 + t * 64, 64), 64)
        flat_left[rows, :] = jnp.where(me.e == 0, first, second)
        give[pl.ds(pl.multiple_of(t * 64, 64), 64), :] = jnp.where(me.e == 0, second, first)

    def left_last(g):
        ready(1, g, 0)
        more = came(1, g, 0, 3) + came(1, g, 1, 3)
        start, count = BACK.part("Y", g)
        wire.arrived(f"mate{g}", mate_in.at[g, pl.ds(0, count)], mate)
        sum_part(1, g, 0, start, count, more + [(mate_in.at[g], start)], put_left)
        sum_part(1, g, 0, start + count, 8, more, put_left)
        rows = pl.ds(BACK.start[g] * 8, BACK.size[g] * 8)
        wire.start(f"last{g}", give.at[rows], got.at[rows], core)

    def column(which, dx):
        return dr.at[me.across(which == 1, dx)]

    def right_first(which, g):
        low, high = BACK.rows(g)
        ref = column(which, 2)
        wire.start(f"x+{which}{g}0", ref.at[low], x_in.at[0, which, 0, low], east)
        wire.start(f"x-{which}{g}0", ref.at[high], x_in.at[1, which, 0, high], west)

    def right_step(which, g):
        parts = BACK.rows(g)
        for way, sign, to, dx in ((0, "+", east, 1), (1, "-", west, 3)):
            ref = x_in.at[way, which, 0]
            wire.arrived(f"x{sign}{which}{g}0", ref.at[parts[way]], to)
            add(column(which, dx), parts[way].start, BACK.size[g], [(ref, 0)])
            for part, tag in zip(parts, "ab"):
                wire.start(
                    f"x{sign}{which}{g}1{tag}", column(which, dx).at[part],
                    x_in.at[way, which, 1, part], to,
                )

    def right_came(which, g):
        for way, sign, to in ((0, "+", east), (1, "-", west)):
            for part, tag in zip(BACK.rows(g), "ab"):
                ref = x_in.at[way, which, 1, part]
                wire.arrived(f"x{sign}{which}{g}1{tag}", ref, to)
        return [(x_in.at[0, which, 1], 0), (x_in.at[1, which, 1], 0)]

    def right_last_other(g):
        terms = right_came(0, g)
        low, high = BACK.rows(g)
        for part in (low, high):
            add(column(0, 0), part.start, BACK.size[g], terms)
        wire.start(f"ya{g}", column(0, 0).at[low], relay.at[0, g, pl.ds(0, BACK.size[g])], north)
        wire.start(f"yb{g}", column(0, 0).at[high], relay.at[1, g, pl.ds(0, BACK.size[g])], south)

    def over_y_on(g):
        low, high = BACK.rows(g)
        wire.arrived(f"ya{g}", relay.at[0, g, pl.ds(0, BACK.size[g])], north)
        wire.start(f"ya{g}2", relay.at[0, g, pl.ds(0, BACK.size[g])], pair_in.at[low], north)
        wire.arrived(f"yb{g}", relay.at[1, g, pl.ds(0, BACK.size[g])], south)
        wire.start(f"yb{g}2", relay.at[1, g, pl.ds(0, BACK.size[g])], pair_in.at[high], south)

    def put_right(t, total):
        rows = pl.ds(pl.multiple_of(t * 128, 128), 128)
        flat_right[rows, :] = total.reshape(128, 128)

    def right_last(g):
        terms = right_came(1, g)
        low, high = BACK.rows(g)
        wire.arrived(f"ya{g}2", pair_in.at[low], north)
        wire.arrived(f"yb{g}2", pair_in.at[high], south)
        for part in (low, high):
            add(column(1, 0), part.start, BACK.size[g], terms + [(pair_in, 0)], put_right)

    loaded(3)
    panels_back(1 - me.e, 0, 24)
    met()
    core_send(0)
    loaded(3)
    panels_back(me.e, 0, 24)
    right_first(0, 0)
    right_first(1, 0)
    left_step(0, 0, 0)
    left_step(1, 0, 0)
    loaded(6)
    panels_back(1 - me.e, 24, 16)
    left_step(0, 0, 1)
    right_step(0, 0)
    panels_back(1 - me.e, 40, 24)
    core_send(1)
    left_step(1, 0, 1)
    right_step(1, 0)
    panels_back(me.e, 24, 16)
    left_step(0, 0, 2)
    panels_back(me.e, 40, 24)
    right_first(0, 1)
    right_first(1, 1)
    left_step(1, 0, 2)
    left_step(0, 1, 0)
    left_step(1, 1, 0)
    fill(1)
    left_step(0, 0, 3)
    right_last_other(0)
    left_step(1, 0, 3)
    fill(2)
    right_step(0, 1)
    left_step(0, 1, 1)
    over_y_on(0)
    left_last_other(0)
    left_step(1, 1, 1)
    right_step(1, 1)
    fill(3)
    left_last(0)
    right_last(0)
    fill(1)
    left_step(0, 1, 2)
    fill(2)
    left_step(1, 1, 2)
    right_last_other(1)
    fill(3)
    left_step(0, 1, 3)
    over_y_on(1)
    left_step(1, 1, 3)
    right_last(1)

    @pl.loop(0, 16, unroll=4)
    def _(k):
        rows = flat_right[pl.ds(k, 128, stride=16), :] * right_mask(mid_ref, cols_ref, k)
        turned = rows.T
        back[pl.ds(k, 64, stride=32), :] = turned[:64, :]
        back[pl.ds(k + 16, 64, stride=32), :] = turned[64:, :]

    left_last_other(1)
    side_back(range(5), right_w, 1024)
    left_last(1)
    side_back(range(5, 8), right_w, 1024)
    for g in (0, 1):
        rows = pl.ds(BACK.start[g] * 8, BACK.size[g] * 8)
        wire.arrived(f"last{g}", got.at[rows], core)
    flat_left[pl.ds(pl.multiple_of((1 - me.e) * 512, 512), 512), :] = got[...]

    @pl.loop(0, 8, unroll=4)
    def _(k):
        rows = flat_left[pl.ds(k, 128, stride=8), :] * left_mask(mid_ref, rows_ref, k)
        back[pl.ds(k, 128, stride=8), :] = rows.T

    side_back(range(4), left_w, 0)
    wire.finish()


def scatter(*operands):
    return pl.pallas_call(
        scatter_kernel,
        out_shape=jax.ShapeDtypeStruct((3072, 128), BF),
        in_specs=[ANY, ANY, ANY] + [VMEM] * 4 + [SMEM] + [VMEM] * 5,
        out_specs=VMEM,
        scratch_shapes=[
            pltpu.VMEM((2, 8, 128, 16, 128), BF),
            pltpu.VMEM((8, 128, 16, 128), BF),
            pltpu.VMEM((8, 1024, 128), F32),
            pltpu.VMEM((2, 8, 128, 16, 128), BF),
            pltpu.VMEM((8, 128, 16, 128), BF),
            pltpu.VMEM((2, 8, 64, 16, 128), BF),
            pltpu.VMEM((2, 2, 4, 64, 16, 128), BF),
            pltpu.VMEM((2, 8, 8, 16, 128), BF),
            pltpu.VMEM((2, 32, 16, 128), BF),
            pltpu.VMEM((512, 128), F32),
            pltpu.VMEM((512, 128), F32),
            pltpu.VMEM((2, 2, 2, 128, 16, 128), BF),
            pltpu.VMEM((2, 2, 40, 16, 128), BF),
            pltpu.VMEM((128, 16, 128), BF),
            pltpu.VMEM((1024, 128), F32),
            pltpu.VMEM((2048, 128), F32),
            pltpu.VMEM((2048, 128), F32),
            pltpu.VMEM((3072, 128), F32),
            pltpu.VMEM((3072, 128), F32),
            pltpu.VMEM((3072, 128), F32),
            pltpu.VMEM((3072, 128), F32),
            pltpu.SemaphoreType.DMA((128,)),
            pltpu.SemaphoreType.DMA((128,)),
            pltpu.SemaphoreType.DMA((12,)),
        ],
        compiler_params=pltpu.CompilerParams(
            collective_id=1, has_side_effects=True, vmem_limit_bytes=LIMIT
        ),
        name="scatter_sums",
    )(*operands)


def split_kernel(both, left_out, right_out):
    left_out[...] = both[:1024, :]
    right_out[...] = both[1024:, :]


def split(both):
    return pl.pallas_call(
        split_kernel,
        out_shape=(
            jax.ShapeDtypeStruct((1024, 128), BF),
            jax.ShapeDtypeStruct((2048, 128), BF),
        ),
        in_specs=[VMEM],
        out_specs=(VMEM, VMEM),
        name="split_sides",
    )(both)


JS = 8


def middle_kernel(
    tri_ref, tile_ref, up_ref, in_gain_ref, gate_w_ref, mid_gain_ref, proj_w_ref,
    update_ref, d_tile_ref, d_tri_ref, flat, rstds,
):
    mid_gain = jnp.broadcast_to(mid_gain_ref[...], (128, 128)).T
    in_gain = in_gain_ref[...]
    proj_w = proj_w_ref[...]
    gate_w = gate_w_ref[...]

    for j in range(JS):
        normed, rstd = norm(tri_ref[0, pl.ds(j, 128, stride=8), :], 0)
        d_tri_ref[0, pl.ds(j, 128, stride=8), :] = normed
        rstds[pl.ds(j, 1), :] = rstd
        value = tn((normed * mid_gain).astype(BF), proj_w)
        flat[pl.ds(j, 128, stride=8), :] = value

    for t in range(8):
        rows = pl.ds(t * 128, 128)
        items = pl.ds(t * 16, 16)
        tile = tile_ref[items].astype(F32).reshape(128, 128)
        upstream = up_ref[items].astype(F32).reshape(128, 128)
        normed, rstd = norm(tile, -1)
        gate = sigmoid(nn((normed * in_gain).astype(BF), gate_w))
        value = flat[rows, :]
        update_ref[items] = (gate * value).reshape(16, 8, 128).astype(BF)
        gated = upstream * gate
        flat[rows, :] = gated
        d_gate = (gated * value * (1.0 - gate)).astype(BF)
        d_norm = nt(d_gate, gate_w)
        d_tile = norm_back(normed, rstd, in_gain, d_norm, -1)
        d_tile_ref[items] = d_tile.reshape(16, 8, 128).astype(BF)

    for j in range(JS):
        here = pl.ds(j, 128, stride=8)
        normed, rstd = d_tri_ref[0, here, :], rstds[pl.ds(j, 1), :]
        d_norm = nt(proj_w, flat[here, :].astype(BF))
        d_tri_ref[0, here, :] = norm_back(normed, rstd, mid_gain, d_norm, 0)


def middle(tri, tile, upstream, in_gain, gate_w, mid_gain, proj_w):
    cell = pl.BlockSpec((128, JS, 128), lambda s: (0, s, 0))
    cube = pl.BlockSpec((1, 1024, 128), lambda s: (s, 0, 0))
    whole = pl.BlockSpec((128, 128), lambda s: (0, 0))
    line = pl.BlockSpec((1, 128), lambda s: (0, 0))
    return pl.pallas_call(
        middle_kernel,
        grid=(64 // JS,),
        out_shape=(
            jax.ShapeDtypeStruct((128, 64, 128), BF),
            jax.ShapeDtypeStruct((128, 64, 128), BF),
            jax.ShapeDtypeStruct((8, 1024, 128), F32),
        ),
        in_specs=[cube, cell, cell, line, whole, line, whole],
        out_specs=(cell, cell, cube),
        scratch_shapes=[pltpu.VMEM((1024, 128), F32), pltpu.VMEM((JS, 128), F32)],
        compiler_params=pltpu.CompilerParams(
            vmem_limit_bytes=LIMIT, dimension_semantics=("arbitrary",)
        ),
        name="middle",
    )(tri, tile, upstream, in_gain, gate_w, mid_gain, proj_w)


def body(
    pair_left,
    pair_right,
    pair_tile,
    d_update,
    mask_rows,
    mask_cols,
    mask_mid,
    ln_in_gain,
    left_gate_w,
    left_proj_w,
    right_gate_w,
    right_proj_w,
    out_gate_w,
    ln_mid_gain,
    out_proj_w,
):
    flat_left = pair_left.reshape(1024, 128)
    flat_right = pair_right.reshape(2048, 128)
    gain = ln_in_gain.reshape(1, 128)
    sides = (
        flat_left, flat_right, mask_rows.reshape(1, 128), mask_cols.reshape(1, 64),
        mask_mid, gain, left_gate_w, left_proj_w, right_gate_w, right_proj_w,
    )
    lp, rp, tri = gather(*sides)
    update, d_tile, d_tri = middle(
        tri, pair_tile, d_update, gain, out_gate_w, ln_mid_gain.reshape(1, 128), out_proj_w
    )
    d_left, d_right = split(scatter(lp, rp, d_tri, *sides))
    return (
        update,
        d_left.reshape(128, 8, 128),
        d_right.reshape(64, 32, 128),
        d_tile,
    )


def solution(mesh):
    in_specs = (
        P("row", "col", None),
        P("col", "row", None),
        P("row", "col", None),
        P("row", "col", None),
        P("row"),
        P("col"),
        P(),
        P(),
        P(),
        P(),
        P(),
        P(),
        P(),
        P(),
        P(),
    )
    out_specs = (
        P("row", "col", None),
        P("row", "col", None),
        P("col", "row", None),
        P("row", "col", None),
    )
    return jax.shard_map(body, mesh=mesh, in_specs=in_specs, out_specs=out_specs, check_vma=False)
```

```python
import functools

import jax
import jax.numpy as jnp
from jax import lax
from jax.experimental import pallas as pl
from jax.experimental.pallas import tpu as pltpu
from jax.sharding import PartitionSpec as P

MESH = pl.DeviceIdType.MESH
BF = jnp.bfloat16
F32 = jnp.float32
VMEM = pl.BlockSpec(memory_space=pltpu.VMEM)
SMEM = pl.BlockSpec(memory_space=pltpu.SMEM)
ANY = pl.BlockSpec(memory_space=pl.ANY)
LIMIT = 60 * 1024 * 1024


def nn(a, b):
    return lax.dot_general(a, b, (((1,), (0,)), ((), ())), preferred_element_type=F32)


def nt(a, b):
    return lax.dot_general(a, b, (((1,), (1,)), ((), ())), preferred_element_type=F32)


def tn(a, b):
    return lax.dot_general(a, b, (((0,), (0,)), ((), ())), preferred_element_type=F32)


def sigmoid(v):
    return 0.5 * jnp.tanh(0.5 * v) + 0.5


def norm(values, axis):
    centred = values - jnp.mean(values, axis=axis, keepdims=True)
    rstd = lax.rsqrt(jnp.mean(centred * centred, axis=axis, keepdims=True) + 1e-05)
    return centred * rstd, rstd


def norm_back(normed, rstd, gain, upstream, axis):
    scaled = upstream * gain
    inner = jnp.mean(scaled * normed, axis=axis, keepdims=True)
    return (scaled - jnp.mean(scaled, axis=axis, keepdims=True) - normed * inner) * rstd


def left_mask(mid_ref, rows_ref, k):
    keep = mid_ref[lax.axis_index("col") * 8 + k].astype(F32)
    return rows_ref[...].astype(F32) * keep


def right_mask(mid_ref, cols_ref, k):
    base = lax.axis_index("row") * 32 + k
    low = mid_ref[base].astype(F32)
    high = mid_ref[base + 16].astype(F32)
    cols = cols_ref[...].astype(F32)
    return jnp.concatenate([cols * low, cols * high], axis=1)


def project(ref, t, gain, weights):
    rows = pl.ds(t * 256, 256)
    normed, rstd = norm(ref[rows, :].astype(F32), -1)
    both = nn((normed * gain).astype(BF), weights)
    return rows, normed, rstd, sigmoid(both[:, :128]), both[:, 128:]


class Fill:
    def __init__(self):
        self.todo = []

    def __call__(self, count=1):
        for work in self.todo[:count]:
            work()
        self.todo = self.todo[count:]


class Place:
    def __init__(self):
        row, col = lax.axis_index("row"), lax.axis_index("col")
        self.row, self.col = row, col
        self.x, self.yh = row // 2, lax.rem(row, 2)
        self.yl, self.z = col // 16, lax.rem(col // 2, 8)
        self.e = lax.rem(col, 2)

    def at(self, x=None, y=None, z=None, e=None):
        here = self.yh * 2 + self.yl
        y = here if y is None else lax.rem(here + y + 4, 4)
        x = self.x if x is None else lax.rem(self.x + x + 4, 4)
        z = self.z if z is None else lax.rem(self.z + z + 8, 8)
        e = self.e if e is None else 1 - self.e
        return (x * 2 + y // 2, lax.rem(y, 2) * 16 + z * 2 + e)

    def mate(self):
        return (self.row, (1 - self.yl) * 16 + self.z * 2 + self.e)

    def slot(self, same_y, dz):
        z = lax.rem(self.z + dz + 8, 8)
        yl = self.yl if same_y else 1 - self.yl
        return lax.rem(z, 2), yl * 4 + z // 2

    def across(self, same_y, dx):
        x = lax.rem(self.x + dx + 4, 4)
        yh = self.yh if same_y else 1 - self.yh
        return x * 2 + yh


def greet(place):
    barrier = pltpu.get_barrier_semaphore()
    partners = [
        place.at(e=1), place.at(z=1), place.at(z=-1), place.at(x=1), place.at(x=-1),
        place.at(y=1), place.at(y=-1),
    ]
    for partner in partners:
        pl.semaphore_signal(barrier, inc=1, device_id=partner, device_id_type=MESH)
    return lambda: pl.semaphore_wait(barrier, len(partners))


class Wire:
    def __init__(self, send, recv):
        self.send, self.recv = send, recv
        self.number, self.open = {}, []

    def copy(self, name, src, dst, to):
        index = self.number.setdefault(name, len(self.number))
        return pltpu.make_async_remote_copy(
            src_ref=src, dst_ref=dst, send_sem=self.send.at[index],
            recv_sem=self.recv.at[index], device_id=to, device_id_type=MESH,
        )

    def start(self, name, src, dst, to):
        made = self.copy(name, src, dst, to)
        made.start()
        self.open.append(made)

    def arrived(self, name, dst, to):
        self.copy(name, dst, dst, to).wait_recv()

    def finish(self):
        for made in self.open:
            made.wait_send()


class Groups:
    def __init__(self, *sizes):
        self.size = sizes
        self.start = tuple(sum(sizes[:g]) for g in range(len(sizes)))

    def whole(self, g):
        return (self.start[g], self.size[g])

    def part(self, name, g):
        return (self.start[g], self.size[g] - (0 if name == "O" else 8))

    def late(self, g):
        return (self.start[g] + self.size[g] - 8, 8)

    def halves(self, name, g):
        start, count = self.part(name, g)
        first = count - 16 if name == "O" else count // 2
        return (start, first), (start + first, count - first)

    def rows(self, g):
        start, size = self.whole(g)
        return pl.ds(start, size), pl.ds(64 + start, size)


FORTH = Groups(40, 24)
BACK = Groups(24, 40)


def gather_kernel(
    left_ref, right_ref, rows_ref, cols_ref, mid_ref, gain_ref, lg, lpw, rg, rpw,
    lp_out, rp_out, tri_out, lp, rp, tri, flat, turned, turned_left, given, relay, send, recv, local,
):
    me = Place()
    wire = Wire(send, recv)
    met = greet(me)
    core, up, down, mate = me.at(e=1), me.at(z=1), me.at(z=-1), me.mate()
    east, west, north, south = me.at(x=1), me.at(x=-1), me.at(y=1), me.at(y=-1)
    gain = gain_ref[...]
    outs = []

    def channels(start, count, half):
        return pl.ds(pl.multiple_of(half * 64 + start, 8), count)

    def piece(same_y, dz, part, half=None):
        kh, slot = me.slot(same_y, dz)
        return lp.at[kh, slot, channels(*part, me.e if half is None else half)]

    def normed_rows(ref, t):
        rows = pl.ds(t * 256, 256)
        normed, _ = norm(ref[rows, :].astype(F32), -1)
        flat[rows, :] = normed * gain

    def gated(weights, rows, mask):
        both = nt(weights, rows.astype(BF))
        return sigmoid(both[:128]) * both[128:] * mask

    left_w = jnp.concatenate([lg[...].T, lpw[...].T], axis=0)
    for t in range(4):
        normed_rows(left_ref, t)

    @pl.loop(0, 8, unroll=4)
    def _(k):
        rows = flat[pl.ds(k, 128, stride=8), :]
        turned_left[pl.ds(k, 128, stride=8), :] = gated(
            left_w, rows, left_mask(mid_ref, rows_ref, k)
        )

    met()
    there = pl.ds(pl.multiple_of((1 - me.e) * 512, 512), 512)
    wire.start("core", turned_left.at[there], given, core)
    for t in range(4):
        normed_rows(right_ref, t)
    wire.arrived("core", given, core)
    own_kh, own_slot = me.slot(True, 0)

    @pl.loop(0, 8, unroll=2)
    def _(t):
        rows = pl.ds(pl.multiple_of(me.e * 512 + t * 64, 64), 64)
        ours = turned_left[rows, :].reshape(8, 8, 128)
        theirs = given[pl.ds(pl.multiple_of(t * 64, 64), 64), :].reshape(8, 8, 128)
        first = jnp.where(me.e == 0, ours, theirs)
        second = jnp.where(me.e == 0, theirs, ours)
        both = jnp.concatenate([first, second], axis=1)
        lp[own_kh, own_slot, channels(t * 8, 8, me.e)] = both.astype(BF)

    def copy(name, ref, to):
        wire.start(name, ref, ref, to)

    def left_send(g):
        ref = piece(True, 0, FORTH.part("O", g))
        copy(f"z+O{g}1", ref, up)
        copy(f"z-O{g}1", ref, down)
        copy(f"m{g}", ref, mate)
        copy(f"cO{g}0", ref, core)

    def share(name, g, dz):
        copy(f"c{name}{g}{dz}", piece(name == "O", dz, FORTH.whole(g)), core)

    def mate_step(g):
        wire.arrived(f"m{g}", piece(False, 0, FORTH.whole(g)), mate)
        ref = piece(False, 0, FORTH.part("Y", g))
        copy(f"z+Y{g}1", ref, up)
        copy(f"z-Y{g}1", ref, down)
        share("Y", g, 0)

    def left_step(name, g, d):
        same = name == "O"
        part, halves = FORTH.part(name, g), FORTH.halves(name, g)
        for way, sign, dz, to in ((0, "z+", -d, up), (1, "z-", d, down)):
            if d < 4:
                wire.arrived(f"{sign}{name}{g}{d}", piece(same, dz, part), to)
                on = part if d < 3 else halves[way]
                copy(f"{sign}{name}{g}{d + 1}", piece(same, dz, on), to)
            else:
                wire.arrived(f"{sign}{name}{g}{d}", piece(same, dz, halves[way]), to)
        if same:
            for dz in (-d, d)[d // 4:]:
                copy(f"y{g}{dz}", piece(True, dz, FORTH.late(g)), mate)
                share("O", g, dz)

    def late(g, d):
        for dz in (-d, d)[d // 4:]:
            wire.arrived(f"y{g}{dz}", piece(False, dz, FORTH.late(g)), mate)
            share("Y", g, dz)

    def shared(g):
        for name in ("O", "Y"):
            for dz in (0, -1, 1, -2, 2, -3, 3, 4):
                ref = piece(name == "O", dz, FORTH.whole(g), 1 - me.e)
                wire.arrived(f"c{name}{g}{dz}", ref, core)

    right_w = jnp.concatenate([rg[...].T, rpw[...].T], axis=0)

    def right_turn():
        @pl.loop(0, 16, unroll=4)
        def _(k):
            first = flat[pl.ds(k, 64, stride=32), :]
            second = flat[pl.ds(k + 16, 64, stride=32), :]
            turned[pl.ds(k, 128, stride=16), :] = gated(
                right_w, jnp.concatenate([first, second], axis=0),
                right_mask(mid_ref, cols_ref, k),
            )

        @pl.loop(0, 16, unroll=4)
        def _(t):
            rows = pl.ds(pl.multiple_of(t * 128, 128), 128)
            part = turned[rows, :].reshape(8, 16, 128).astype(BF)
            rp[me.row, pl.ds(pl.multiple_of(t * 8, 8), 8)] = part

    def right_send(own, g):
        low, high = FORTH.rows(g)
        ref = rp.at[me.across(own, 0)]
        tag = f"{own:d}{g}1"
        copy("x+a" + tag, ref.at[low], east)
        copy("x-b" + tag, ref.at[high], west)
        copy("x+b" + tag, ref.at[high], east)
        copy("x-a" + tag, ref.at[low], west)

    def right_step(own, g):
        low, high = FORTH.rows(g)
        behind, ahead = rp.at[me.across(own, -1), low], rp.at[me.across(own, 1), high]
        wire.arrived(f"x+a{own:d}{g}1", behind, east)
        copy(f"x+a{own:d}{g}2", behind, east)
        wire.arrived(f"x-b{own:d}{g}1", ahead, west)
        copy(f"x-b{own:d}{g}2", ahead, west)

    def right_rest(own, g):
        low, high = FORTH.rows(g)
        behind, ahead = rp.at[me.across(own, -1), high], rp.at[me.across(own, 1), low]
        far = rp.at[me.across(own, 2)]
        wire.arrived(f"x+b{own:d}{g}1", behind, east)
        wire.arrived(f"x-a{own:d}{g}1", ahead, west)
        wire.arrived(f"x+a{own:d}{g}2", far.at[low], east)
        wire.arrived(f"x-b{own:d}{g}2", far.at[high], west)

    def over_y(g):
        low, high = FORTH.rows(g)
        wire.start(f"ya{g}", rp.at[me.row, low], relay.at[0, g, pl.ds(0, FORTH.size[g])], north)
        wire.start(f"yb{g}", rp.at[me.row, high], relay.at[1, g, pl.ds(0, FORTH.size[g])], south)

    def over_y_on(g):
        low, high = FORTH.rows(g)
        here = me.yh * 2 + me.yl
        above, below = lax.rem(here + 3, 4), lax.rem(here + 1, 4)
        wire.arrived(f"ya{g}", relay.at[0, g, pl.ds(0, FORTH.size[g])], north)
        wire.start(f"ya{g}2", relay.at[0, g, pl.ds(0, FORTH.size[g])], rp.at[me.x * 2 + above // 2, low], north)
        wire.arrived(f"yb{g}", relay.at[1, g, pl.ds(0, FORTH.size[g])], south)
        wire.start(f"yb{g}2", relay.at[1, g, pl.ds(0, FORTH.size[g])], rp.at[me.x * 2 + below // 2, high], south)

    def pair_step(g):
        low, high = FORTH.rows(g)
        pair = rp.at[me.across(False, 0)]
        wire.arrived(f"ya{g}2", pair.at[low], north)
        wire.arrived(f"yb{g}2", pair.at[high], south)
        right_send(False, g)

    def keep(g):
        for part in FORTH.rows(g):
            for src, dst in ((lp.at[:, :, part], lp_out.at[:, :, part]),
                             (rp.at[:, part], rp_out.at[:, part])):
                made = pltpu.make_async_copy(src, dst, local.at[len(outs)])
                made.start()
                outs.append(made)

    def triangle(start, count):
        @pl.loop(0, count, unroll=8)
        def _(t):
            c = start + t
            right = rp[:, c].reshape(128, 128).T
            right = jnp.concatenate([right[:64], right[64:]], axis=1)
            left = jnp.concatenate(
                [lp[0, :, c].reshape(128, 128), lp[1, :, c].reshape(128, 128)], axis=0
            )
            rows = pl.ds(pl.multiple_of(c * 8, 8), 8)
            tri[:, rows, :] = nn(right, left).reshape(8, 8, 128)

    def keep_triangle(g):
        for rows in FORTH.rows(g):
            part = pl.ds(rows.start * 8, rows.size * 8)
            made = pltpu.make_async_copy(
                tri.at[:, part], tri_out.at[:, part], local.at[len(outs)]
            )
            made.start()
            outs.append(made)

    left_send(0)
    left_send(1)
    for t in range(4, 8):
        normed_rows(right_ref, t)
    right_turn()
    right_send(True, 0)
    over_y(0)
    mate_step(0)
    left_step("O", 0, 1)
    left_step("Y", 0, 1)
    left_step("O", 0, 2)
    late(0, 1)
    over_y_on(0)
    mate_step(1)
    left_step("O", 1, 1)
    left_step("Y", 0, 2)
    right_step(True, 0)
    right_send(True, 1)
    left_step("O", 0, 3)
    late(0, 2)
    pair_step(0)
    over_y(1)
    left_step("Y", 1, 1)
    left_step("Y", 0, 3)
    left_step("O", 1, 2)
    late(1, 1)
    left_step("O", 0, 4)
    late(0, 3)
    left_step("Y", 0, 4)
    late(0, 4)
    left_step("Y", 1, 2)
    over_y_on(1)
    right_step(True, 1)
    right_step(False, 0)
    left_step("O", 1, 3)
    late(1, 2)
    pair_step(1)
    left_step("Y", 1, 3)
    right_rest(True, 0)
    right_rest(False, 0)
    shared(0)
    keep(0)
    triangle(0, 16)
    left_step("O", 1, 4)
    late(1, 3)
    triangle(16, 24)
    right_step(False, 1)
    left_step("Y", 1, 4)
    late(1, 4)
    triangle(64, 16)
    triangle(80, 24)
    keep_triangle(0)
    right_rest(True, 1)
    right_rest(False, 1)
    shared(1)
    keep(1)
    triangle(40, 24)
    triangle(104, 24)
    keep_triangle(1)
    for made in outs:
        made.wait()
    wire.finish()


def gather(*operands):
    return pl.pallas_call(
        gather_kernel,
        out_shape=(
            jax.ShapeDtypeStruct((2, 8, 128, 16, 128), BF),
            jax.ShapeDtypeStruct((8, 128, 16, 128), BF),
            jax.ShapeDtypeStruct((8, 1024, 128), F32),
        ),
        in_specs=[VMEM] * 4 + [SMEM] + [VMEM] * 5,
        out_specs=(ANY, ANY, ANY),
        scratch_shapes=[
            pltpu.VMEM((2, 8, 128, 16, 128), BF),
            pltpu.VMEM((8, 128, 16, 128), BF),
            pltpu.VMEM((8, 1024, 128), F32),
            pltpu.VMEM((2048, 128), F32),
            pltpu.VMEM((2048, 128), F32),
            pltpu.VMEM((1024, 128), F32),
            pltpu.VMEM((512, 128), F32),
            pltpu.VMEM((2, 2, 40, 16, 128), BF),
            pltpu.SemaphoreType.DMA((128,)),
            pltpu.SemaphoreType.DMA((128,)),
            pltpu.SemaphoreType.DMA((12,)),
        ],
        compiler_params=pltpu.CompilerParams(
            collective_id=0, has_side_effects=True, vmem_limit_bytes=LIMIT
        ),
        name="gather_panels",
    )(*operands)


def scatter_kernel(
    lp_hbm, rp_hbm, tri_hbm, left_ref, right_ref, rows_ref, cols_ref, mid_ref, gain_ref,
    lg, lpw, rg, rpw, both_out,
    lp, rp, tri, dl, dr,
    core_in, z_in, late_in, mate_in, give, got, x_in, relay, pair_in,
    flat_left, flat_right, back, norms, rstds, gates, values,
    send, recv, local,
):
    me = Place()
    wire = Wire(send, recv)
    met = greet(me)
    core, up, down, mate = me.at(e=1), me.at(z=1), me.at(z=-1), me.mate()
    east, west, north, south = me.at(x=1), me.at(x=-1), me.at(y=1), me.at(y=-1)
    gain = gain_ref[...]
    loads = []

    for g in (0, 1):
        start, size = BACK.whole(g)
        for side in (1 - me.e, me.e):
            part = pl.ds(pl.multiple_of(side * 64 + start, 8), size)
            rows = pl.ds(pl.multiple_of((side * 64 + start) * 8, 64), size * 8)
            for src, dst in (
                (tri_hbm.at[:, rows], tri.at[:, rows]),
                (rp_hbm.at[:, part], rp.at[:, part]),
                (lp_hbm.at[:, :, part], lp.at[:, :, part]),
            ):
                made = pltpu.make_async_copy(src, dst, local.at[len(loads)])
                made.start()
                loads.append(made)

    def loaded(count):
        for made in loads[:count]:
            made.wait()
        del loads[:count]

    fill = Fill()
    left_w = jnp.concatenate([lg[...], lpw[...]], axis=1)
    right_w = jnp.concatenate([rg[...], rpw[...]], axis=1)

    def ahead(ref, t, weights, shift):
        def work():
            _, normed, rstd, gate, value = project(ref, t, gain, weights)
            rows = pl.ds(shift + t * 256, 256)
            norms[rows, :] = normed
            rstds[rows, :] = jnp.broadcast_to(rstd, (256, 128))
            gates[rows, :] = gate
            values[rows, :] = value * gate * (1.0 - gate)

        return work

    for t in range(8):
        fill.todo.append(ahead(right_ref, t, right_w, 1024))
    for t in range(4):
        fill.todo.append(ahead(left_ref, t, left_w, 0))

    def side_back(steps, weights, shift):
        for t in steps:
            here, rows = pl.ds(t * 256, 256), pl.ds(shift + t * 256, 256)
            masked = back[here, :]
            d_value = (masked * gates[rows, :]).astype(BF)
            d_gate = (masked * values[rows, :]).astype(BF)
            d_norm = nt(jnp.concatenate([d_gate, d_value], axis=1), weights)
            result = norm_back(norms[rows, :], rstds[rows, :], gain, d_norm, -1)
            both_out[rows, :] = result.astype(BF)

    def panels_back(half, start, count):
        @pl.loop(0, count, unroll=8)
        def _(t):
            c = half * 64 + start + t
            rows = pl.ds(pl.multiple_of(c * 8, 8), 8)
            grad = tri[:, rows, :].reshape(64, 128).astype(BF)
            none = jnp.zeros((64, 128), BF)
            grad = jnp.concatenate(
                [
                    jnp.concatenate([grad, none], axis=1),
                    jnp.concatenate([none, grad], axis=1),
                ],
                axis=0,
            )
            right = rp[:, c].reshape(128, 128)
            left = jnp.concatenate(
                [lp[0, :, c].reshape(128, 128), lp[1, :, c].reshape(128, 128)], axis=1
            )
            d_left = nn(right, grad).astype(BF)
            dl[0, :, c] = d_left[:, :128].reshape(8, 16, 128)
            dl[1, :, c] = d_left[:, 128:].reshape(8, 16, 128)
            dr[:, c] = nt(left, grad).astype(BF).reshape(8, 16, 128)

    def block(which, dz, half=None):
        kh, slot = me.slot(which == 1, dz)
        start = (me.e if half is None else half) * 64
        return dl.at[kh, slot, pl.ds(pl.multiple_of(start, 64), 64)]

    def core_send(g):
        part = pl.ds(*BACK.whole(g))
        for dz in (4, 3, 5, 2, 6, 1, 7, 0):
            for which in (0, 1):
                wire.start(
                    f"c{which}{g}{dz}", block(which, dz, 1 - me.e).at[part],
                    core_in.at[which, dz, part], core,
                )

    def add(target, start, count, terms, out=None):
        def body(t):
            part = pl.ds(pl.multiple_of(start + t * 8, 8), 8)
            total = target[part].astype(F32)
            for term, shift in terms:
                place = pl.ds(pl.multiple_of(start - shift + t * 8, 8), 8)
                total = total + term[place].astype(F32)
            if out is None:
                target[part] = total.astype(BF)
            else:
                out(start // 8 + t, total)

        steps = count // 8
        if steps < 6:
            for t in range(steps):
                body(t)
        else:
            pl.loop(0, steps, unroll=4)(body)

    def ready(which, g, dz):
        part = pl.ds(*BACK.whole(g))
        wire.arrived(f"c{which}{g}{dz}", core_in.at[which, dz, part], core)
        start, count = BACK.late(g)
        if which == 0:
            add(block(0, dz), start, count, [(core_in.at[0, dz], 0)])
            wire.start(
                f"l{g}{dz}", block(0, dz).at[pl.ds(start, count)], late_in.at[g, dz], mate
            )
        else:
            wire.arrived(f"l{g}{dz}", late_in.at[g, dz], mate)

    def sum_part(which, g, dz, start, count, more, out=None):
        terms = [(core_in.at[which, dz], 0)] + more
        first, _ = BACK.late(g)
        plain = min(count, max(0, first - start))
        if plain:
            add(block(which, dz), start, plain, terms, out)
        if which == 1 and start + count > first:
            late = [(late_in.at[g, dz], first)]
            add(block(which, dz), first, start + count - first, terms + late, out)

    def put(name, way, ref, dst, part):
        sign, to = (("+", up), ("-", down))[way]
        wire.start(f"z{sign}{name}", ref.at[pl.ds(*part)], dst.at[pl.ds(*part)], to)

    def came(which, g, way, d):
        name = "O" if which else "Y"
        sign, to = (("+", up), ("-", down))[way]
        part = BACK.halves(name, g)[way] if d == 0 else BACK.part(name, g)
        ref = z_in.at[way, which, d]
        wire.arrived(f"z{sign}{name}{g}{d}", ref.at[pl.ds(*part)], to)
        return [(ref, 0)]

    def left_step(which, g, d):
        name = "O" if which else "Y"
        halves = BACK.halves(name, g)
        if d == 0:
            ready(which, g, 4)
            for way in (0, 1):
                sum_part(which, g, 4, *halves[way], [])
                put(f"{name}{g}0", way, block(which, 4), z_in.at[way, which, 0], halves[way])
            return
        for way in (0, 1):
            dz = 4 + d if way else 4 - d
            ready(which, g, dz)
            more = came(which, g, way, d - 1)
            if d == 1:
                sum_part(which, g, dz, *halves[way], more)
                sum_part(which, g, dz, *halves[1 - way], [])
            else:
                sum_part(which, g, dz, *BACK.part(name, g), more)
            put(
                f"{name}{g}{d}", way, block(which, dz), z_in.at[way, which, d],
                BACK.part(name, g),
            )

    def left_last_other(g):
        ready(0, g, 0)
        more = came(0, g, 0, 3) + came(0, g, 1, 3)
        start, count = BACK.part("Y", g)
        sum_part(0, g, 0, start, count, more)
        wire.start(
            f"mate{g}", block(0, 0).at[pl.ds(start, count)],
            mate_in.at[g, pl.ds(0, count)], mate,
        )

    def put_left(t, total):
        first, second = total[:, :8].reshape(64, 128), total[:, 8:].reshape(64, 128)
        rows = pl.ds(pl.multiple_of(me.e * 512 + t * 64, 64), 64)
        flat_left[rows, :] = jnp.where(me.e == 0, first, second)
        give[pl.ds(pl.multiple_of(t * 64, 64), 64), :] = jnp.where(me.e == 0, second, first)

    def left_last(g):
        ready(1, g, 0)
        more = came(1, g, 0, 3) + came(1, g, 1, 3)
        start, count = BACK.part("Y", g)
        wire.arrived(f"mate{g}", mate_in.at[g, pl.ds(0, count)], mate)
        sum_part(1, g, 0, start, count, more + [(mate_in.at[g], start)], put_left)
        sum_part(1, g, 0, start + count, 8, more, put_left)
        rows = pl.ds(BACK.start[g] * 8, BACK.size[g] * 8)
        wire.start(f"last{g}", give.at[rows], got.at[rows], core)

    def column(which, dx):
        return dr.at[me.across(which == 1, dx)]

    def right_first(which, g):
        low, high = BACK.rows(g)
        ref = column(which, 2)
        wire.start(f"x+{which}{g}0", ref.at[low], x_in.at[0, which, 0, low], east)
        wire.start(f"x-{which}{g}0", ref.at[high], x_in.at[1, which, 0, high], west)

    def right_step(which, g):
        parts = BACK.rows(g)
        for way, sign, to, dx in ((0, "+", east, 1), (1, "-", west, 3)):
            ref = x_in.at[way, which, 0]
            wire.arrived(f"x{sign}{which}{g}0", ref.at[parts[way]], to)
            add(column(which, dx), parts[way].start, BACK.size[g], [(ref, 0)])
            for part, tag in zip(parts, "ab"):
                wire.start(
                    f"x{sign}{which}{g}1{tag}", column(which, dx).at[part],
                    x_in.at[way, which, 1, part], to,
                )

    def right_came(which, g):
        for way, sign, to in ((0, "+", east), (1, "-", west)):
            for part, tag in zip(BACK.rows(g), "ab"):
                ref = x_in.at[way, which, 1, part]
                wire.arrived(f"x{sign}{which}{g}1{tag}", ref, to)
        return [(x_in.at[0, which, 1], 0), (x_in.at[1, which, 1], 0)]

    def right_last_other(g):
        terms = right_came(0, g)
        low, high = BACK.rows(g)
        for part in (low, high):
            add(column(0, 0), part.start, BACK.size[g], terms)
        wire.start(f"ya{g}", column(0, 0).at[low], relay.at[0, g, pl.ds(0, BACK.size[g])], north)
        wire.start(f"yb{g}", column(0, 0).at[high], relay.at[1, g, pl.ds(0, BACK.size[g])], south)

    def over_y_on(g):
        low, high = BACK.rows(g)
        wire.arrived(f"ya{g}", relay.at[0, g, pl.ds(0, BACK.size[g])], north)
        wire.start(f"ya{g}2", relay.at[0, g, pl.ds(0, BACK.size[g])], pair_in.at[low], north)
        wire.arrived(f"yb{g}", relay.at[1, g, pl.ds(0, BACK.size[g])], south)
        wire.start(f"yb{g}2", relay.at[1, g, pl.ds(0, BACK.size[g])], pair_in.at[high], south)

    def put_right(t, total):
        rows = pl.ds(pl.multiple_of(t * 128, 128), 128)
        flat_right[rows, :] = total.reshape(128, 128)

    def right_last(g):
        terms = right_came(1, g)
        low, high = BACK.rows(g)
        wire.arrived(f"ya{g}2", pair_in.at[low], north)
        wire.arrived(f"yb{g}2", pair_in.at[high], south)
        for part in (low, high):
            add(column(1, 0), part.start, BACK.size[g], terms + [(pair_in, 0)], put_right)

    loaded(3)
    panels_back(1 - me.e, 0, 24)
    met()
    core_send(0)
    loaded(3)
    panels_back(me.e, 0, 24)
    right_first(0, 0)
    right_first(1, 0)
    left_step(0, 0, 0)
    left_step(1, 0, 0)
    loaded(6)
    panels_back(1 - me.e, 24, 16)
    left_step(0, 0, 1)
    right_step(0, 0)
    panels_back(1 - me.e, 40, 24)
    core_send(1)
    left_step(1, 0, 1)
    right_step(1, 0)
    panels_back(me.e, 24, 16)
    left_step(0, 0, 2)
    panels_back(me.e, 40, 24)
    right_first(0, 1)
    right_first(1, 1)
    left_step(1, 0, 2)
    left_step(0, 1, 0)
    left_step(1, 1, 0)
    fill(1)
    left_step(0, 0, 3)
    right_last_other(0)
    left_step(1, 0, 3)
    fill(2)
    right_step(0, 1)
    left_step(0, 1, 1)
    over_y_on(0)
    left_last_other(0)
    left_step(1, 1, 1)
    right_step(1, 1)
    fill(3)
    left_last(0)
    right_last(0)
    fill(1)
    left_step(0, 1, 2)
    fill(2)
    left_step(1, 1, 2)
    right_last_other(1)
    fill(3)
    left_step(0, 1, 3)
    over_y_on(1)
    left_step(1, 1, 3)
    right_last(1)

    @pl.loop(0, 16, unroll=4)
    def _(k):
        rows = flat_right[pl.ds(k, 128, stride=16), :] * right_mask(mid_ref, cols_ref, k)
        turned = rows.T
        back[pl.ds(k, 64, stride=32), :] = turned[:64, :]
        back[pl.ds(k + 16, 64, stride=32), :] = turned[64:, :]

    left_last_other(1)
    side_back(range(5), right_w, 1024)
    left_last(1)
    side_back(range(5, 8), right_w, 1024)
    for g in (0, 1):
        rows = pl.ds(BACK.start[g] * 8, BACK.size[g] * 8)
        wire.arrived(f"last{g}", got.at[rows], core)
    flat_left[pl.ds(pl.multiple_of((1 - me.e) * 512, 512), 512), :] = got[...]

    @pl.loop(0, 8, unroll=4)
    def _(k):
        rows = flat_left[pl.ds(k, 128, stride=8), :] * left_mask(mid_ref, rows_ref, k)
        back[pl.ds(k, 128, stride=8), :] = rows.T

    side_back(range(4), left_w, 0)
    wire.finish()


def scatter(*operands):
    return pl.pallas_call(
        scatter_kernel,
        out_shape=jax.ShapeDtypeStruct((3072, 128), BF),
        in_specs=[ANY, ANY, ANY] + [VMEM] * 4 + [SMEM] + [VMEM] * 5,
        out_specs=VMEM,
        scratch_shapes=[
            pltpu.VMEM((2, 8, 128, 16, 128), BF),
            pltpu.VMEM((8, 128, 16, 128), BF),
            pltpu.VMEM((8, 1024, 128), F32),
            pltpu.VMEM((2, 8, 128, 16, 128), BF),
            pltpu.VMEM((8, 128, 16, 128), BF),
            pltpu.VMEM((2, 8, 64, 16, 128), BF),
            pltpu.VMEM((2, 2, 4, 64, 16, 128), BF),
            pltpu.VMEM((2, 8, 8, 16, 128), BF),
            pltpu.VMEM((2, 32, 16, 128), BF),
            pltpu.VMEM((512, 128), F32),
            pltpu.VMEM((512, 128), F32),
            pltpu.VMEM((2, 2, 2, 128, 16, 128), BF),
            pltpu.VMEM((2, 2, 40, 16, 128), BF),
            pltpu.VMEM((128, 16, 128), BF),
            pltpu.VMEM((1024, 128), F32),
            pltpu.VMEM((2048, 128), F32),
            pltpu.VMEM((2048, 128), F32),
            pltpu.VMEM((3072, 128), F32),
            pltpu.VMEM((3072, 128), F32),
            pltpu.VMEM((3072, 128), F32),
            pltpu.VMEM((3072, 128), F32),
            pltpu.SemaphoreType.DMA((128,)),
            pltpu.SemaphoreType.DMA((128,)),
            pltpu.SemaphoreType.DMA((12,)),
        ],
        compiler_params=pltpu.CompilerParams(
            collective_id=1, has_side_effects=True, vmem_limit_bytes=LIMIT
        ),
        name="scatter_sums",
    )(*operands)


def split_kernel(both, left_out, right_out):
    left_out[...] = both[:1024, :]
    right_out[...] = both[1024:, :]


def split(both):
    return pl.pallas_call(
        split_kernel,
        out_shape=(
            jax.ShapeDtypeStruct((1024, 128), BF),
            jax.ShapeDtypeStruct((2048, 128), BF),
        ),
        in_specs=[VMEM],
        out_specs=(VMEM, VMEM),
        name="split_sides",
    )(both)


JS = 8


def middle_kernel(
    tri_ref, tile_ref, up_ref, in_gain_ref, gate_w_ref, mid_gain_ref, proj_w_ref,
    update_ref, d_tile_ref, d_tri_ref, flat, rstds,
):
    mid_gain = jnp.broadcast_to(mid_gain_ref[...], (256, 128)).T
    in_gain = in_gain_ref[...]
    proj_w = proj_w_ref[...]
    gate_w = gate_w_ref[...]

    def pair(j):
        return pl.ds(j, 128, stride=8), pl.ds(j + 1, 128, stride=8)

    for j in range(0, JS, 2):
        one, two = pair(j)
        both = jnp.concatenate([tri_ref[0, one, :], tri_ref[0, two, :]], axis=1)
        normed, rstd = norm(both, 0)
        d_tri_ref[0, one, :] = normed[:, :128]
        d_tri_ref[0, two, :] = normed[:, 128:]
        rstds[pl.ds(j // 2, 1), :] = rstd
        value = tn((normed * mid_gain).astype(BF), proj_w)
        flat[one, :] = value[:128]
        flat[two, :] = value[128:]

    for t in range(4):
        rows = pl.ds(t * 256, 256)
        items = pl.ds(t * 32, 32)
        tile = tile_ref[items].astype(F32).reshape(256, 128)
        upstream = up_ref[items].astype(F32).reshape(256, 128)
        normed, rstd = norm(tile, -1)
        gate = sigmoid(nn((normed * in_gain).astype(BF), gate_w))
        value = flat[rows, :]
        update_ref[items] = (gate * value).reshape(32, 8, 128).astype(BF)
        gated = upstream * gate
        flat[rows, :] = gated
        d_gate = (gated * value * (1.0 - gate)).astype(BF)
        d_norm = nt(d_gate, gate_w)
        d_tile = norm_back(normed, rstd, in_gain, d_norm, -1)
        d_tile_ref[items] = d_tile.reshape(32, 8, 128).astype(BF)

    for j in range(0, JS, 2):
        one, two = pair(j)
        normed = jnp.concatenate([d_tri_ref[0, one, :], d_tri_ref[0, two, :]], axis=1)
        gated = jnp.concatenate([flat[one, :], flat[two, :]], axis=0)
        d_norm = nt(proj_w, gated.astype(BF))
        rstd = rstds[pl.ds(j // 2, 1), :]
        result = norm_back(normed, rstd, mid_gain, d_norm, 0)
        d_tri_ref[0, one, :] = result[:, :128]
        d_tri_ref[0, two, :] = result[:, 128:]


def middle(tri, tile, upstream, in_gain, gate_w, mid_gain, proj_w):
    cell = pl.BlockSpec((128, JS, 128), lambda s: (0, s, 0))
    cube = pl.BlockSpec((1, 1024, 128), lambda s: (s, 0, 0))
    whole = pl.BlockSpec((128, 128), lambda s: (0, 0))
    line = pl.BlockSpec((1, 128), lambda s: (0, 0))
    return pl.pallas_call(
        middle_kernel,
        grid=(64 // JS,),
        out_shape=(
            jax.ShapeDtypeStruct((128, 64, 128), BF),
            jax.ShapeDtypeStruct((128, 64, 128), BF),
            jax.ShapeDtypeStruct((8, 1024, 128), F32),
        ),
        in_specs=[cube, cell, cell, line, whole, line, whole],
        out_specs=(cell, cell, cube),
        scratch_shapes=[pltpu.VMEM((1024, 128), F32), pltpu.VMEM((JS, 256), F32)],
        compiler_params=pltpu.CompilerParams(
            vmem_limit_bytes=LIMIT, dimension_semantics=("arbitrary",)
        ),
        name="middle",
    )(tri, tile, upstream, in_gain, gate_w, mid_gain, proj_w)


def body(
    pair_left,
    pair_right,
    pair_tile,
    d_update,
    mask_rows,
    mask_cols,
    mask_mid,
    ln_in_gain,
    left_gate_w,
    left_proj_w,
    right_gate_w,
    right_proj_w,
    out_gate_w,
    ln_mid_gain,
    out_proj_w,
):
    flat_left = pair_left.reshape(1024, 128)
    flat_right = pair_right.reshape(2048, 128)
    gain = ln_in_gain.reshape(1, 128)
    sides = (
        flat_left, flat_right, mask_rows.reshape(1, 128), mask_cols.reshape(1, 64),
        mask_mid, gain, left_gate_w, left_proj_w, right_gate_w, right_proj_w,
    )
    lp, rp, tri = gather(*sides)
    update, d_tile, d_tri = middle(
        tri, pair_tile, d_update, gain, out_gate_w, ln_mid_gain.reshape(1, 128), out_proj_w
    )
    d_left, d_right = split(scatter(lp, rp, d_tri, *sides))
    return (
        update,
        d_left.reshape(128, 8, 128),
        d_right.reshape(64, 32, 128),
        d_tile,
    )


def solution(mesh):
    in_specs = (
        P("row", "col", None),
        P("col", "row", None),
        P("row", "col", None),
        P("row", "col", None),
        P("row"),
        P("col"),
        P(),
        P(),
        P(),
        P(),
        P(),
        P(),
        P(),
        P(),
        P(),
    )
    out_specs = (
        P("row", "col", None),
        P("row", "col", None),
        P("col", "row", None),
        P("row", "col", None),
    )
    return jax.shard_map(body, mesh=mesh, in_specs=in_specs, out_specs=out_specs, check_vma=False)
```
